128 devices in a mesh: lon: 32 (over z, x, y_lo), lat: 4 (over y_hi, core).
Axes of the slice: x: 4, y: 4 (y_hi: 2, y_lo: 2; y = y_hi * 2 + y_lo), z: 4, core: 2. Of those that a mesh axis runs over, the one named last changes fastest.
Arguments:
- control: float32 [100, 64, 4096], P(None, 'lat', 'lon'), may hold values from -6 to 6
- lon_coef: float32 [100, 64], P(None, 'lat'), may hold values from 0.02 to 0.2
- lat_coef: float32 [100, 64], P(None, 'lat'), may hold values from 0.02 to 0.2
- obs_base: int32 [128, 128, 128], P(('lon', 'lat')), may hold values from 0 to 1918, as said below
- obs_field: int32 [128, 128, 128], P(('lon', 'lat')), may hold values from 0 to 99
- obs_weight: float32 [4, 128, 128, 128], P(None, ('lon', 'lat')), may hold values from 0 to 1
- obs_count: int32 [128, 128], P(('lon', 'lat')), may hold values from 1 to 128, as said below
- obs_value: float32 [128, 128, 128], P(('lon', 'lat')), may hold values from -6 to 6
- obs_precision: float32 [128, 128, 128], P(('lon', 'lat')), may hold values from 0.5 to 2
Outputs:
- increment: float32 [100, 64, 4096], P(None, 'lat', 'lon')
- gradient: float32 [100, 64, 4096], P(None, 'lat', 'lon')
The draws below stay inside these ranges and needn't reach their ends.
Inputs may be any that keep to these rules, and one draw needn't show every extreme that they name: `obs_base`: every corner lies in the holder's block: row below 15, column below 127. `obs_count`: each holder sends a full 128 slots to at least one owner.
All inputs are finite; a program needn't handle non-finite values.
Results may differ from the reference program's by a relative error of at most 0.00002.
Values sent between devices are 32-bit elements; how exact they have to be, the bound alone decides.
A program may use at most 64 MiB of HBM per device.

```python
import math
import jax
import jax.numpy as jnp

F = 100
CLAT = 16
CLON = 128
SWEEPS = 4
CAP = 128
NLAT = 64
NLON = 4096
N_LAT = 4
DEVICES = 128


def draw_obs_base(key, part):
    key = jax.random.fold_in(key, 11)
    key_row, key_col = jax.random.split(key)
    shape = (DEVICES, DEVICES, CAP)
    rows = jax.random.randint(key_row, shape, 0, CLAT - 1)
    cols = jax.random.randint(key_col, shape, 0, CLON - 1)
    return (rows * CLON + cols).astype(jnp.int32)


def draw_obs_count(key, part):
    key = jax.random.fold_in(key, 23)
    key_count, key_full = jax.random.split(key)
    counts = jax.random.randint(key_count, (DEVICES, DEVICES), 1, CAP + 1)
    full_owner = jax.random.randint(key_full, (DEVICES,), 0, DEVICES)
    owners = jnp.arange(DEVICES, dtype=jnp.int32)[None, :]
    return jnp.where(owners == full_owner[:, None], CAP, counts).astype(jnp.int32)


def touch_ends(array, key, least, high):
    shape = array.shape
    index_at = [jax.random.randint(jax.random.fold_in(key, axis), (), 0, shape[axis]) for axis in range(len(shape))]
    array = array.at[tuple(index_at)].set(least)
    longest = shape.index(max(shape))
    index_at[longest] = (index_at[longest] + 1) % shape[longest]
    return array.at[tuple(index_at)].set(high)


def steps_of(rng, extent, pieces, least, largest):
    gain = 1.0
    for position, blocks in pieces:
        heights = jax.random.uniform(jax.random.fold_in(jax.random.fold_in(rng, 6), position), (blocks,), jnp.float32, least / len(pieces), largest / len(pieces))
        gain = gain * jnp.repeat(jnp.exp(heights), extent[position] // blocks).reshape((-1,) + (1,) * (len(extent) - 1 - position))
    return gain


def centred(stream_key, dims, deviation, bound, cuts=(), kind=jnp.bfloat16):
    result = deviation * jax.random.normal(stream_key, dims, jnp.float32)
    if cuts:
        result = result * steps_of(stream_key, dims, cuts, -0.22, 0.18)
    return jnp.clip(result, -bound, bound).astype(kind)


def setup_inputs(seed: int = 0) -> dict:
    streams_of = jax.random.split(jax.random.key(seed), 10)
    return {
        "control": centred(streams_of[0], (F, NLAT, NLON), 1.0, 6.0, ((1, 4), (2, 32)), jnp.float32),
        "lon_coef": jnp.clip(jnp.exp(math.log(0.2) - 2.3025851 * jax.random.uniform(streams_of[1], (F, NLAT), jnp.float32) ** steps_of(streams_of[1], (F, NLAT), ((1, 4),), -0.2, 0.2)), 0.02, 0.2),
        "lat_coef": jnp.clip(jnp.exp(math.log(0.2) - 2.3025851 * jax.random.uniform(streams_of[2], (F, NLAT), jnp.float32) ** steps_of(streams_of[2], (F, NLAT), ((1, 4),), -0.2, 0.2)), 0.02, 0.2),
        "obs_base": draw_obs_base(jax.random.fold_in(streams_of[9], 71), 0),
        "obs_field": touch_ends(jax.random.randint(streams_of[4], (DEVICES, DEVICES, CAP), 0, F), jax.random.fold_in(streams_of[4], 1), 0, F - 1).astype(jnp.int32),
        "obs_weight": jnp.clip(1.0 * jax.random.uniform(streams_of[5], (4, DEVICES, DEVICES, CAP), jnp.float32) ** steps_of(streams_of[5], (4, DEVICES, DEVICES, CAP), ((1, 128),), -0.2, 0.2), 0.0, 1.0),
        "obs_count": draw_obs_count(jax.random.fold_in(streams_of[9], 71), 0),
        "obs_value": centred(streams_of[7], (DEVICES, DEVICES, CAP), 1.0, 6.0, ((0, 128),), jnp.float32),
        "obs_precision": jnp.clip(jnp.exp(math.log(2.0) - 1.3862944 * jax.random.uniform(streams_of[8], (DEVICES, DEVICES, CAP), jnp.float32) ** steps_of(streams_of[8], (DEVICES, DEVICES, CAP), ((0, 128),), -0.2, 0.2)), 0.5, 2.0),
    }


def diffuse_step(field, lon_rate, lat_rate):
    padded = jnp.pad(field, ((0, 0), (1, 1), (0, 0)))
    padded = jnp.concatenate([padded[:, :, -1:], padded, padded[:, :, :1]], axis=2)
    zonal_rate = jnp.pad(lon_rate, ((0, 0), (1, 1)))
    merid_rate = jnp.pad(lat_rate, ((0, 0), (1, 1)))
    centre = padded[:, 1:-1, 1:-1]
    zonal = padded[:, 1:-1, 2:] + padded[:, 1:-1, :-2] - 2.0 * centre
    north = merid_rate[:, 1:-1, None] * (padded[:, 2:, 1:-1] - centre)
    south = merid_rate[:, :-2, None] * (centre - padded[:, :-2, 1:-1])
    return centre + zonal_rate[:, 1:-1, None] * zonal + north - south


def reference(control, lon_coef, lat_coef, obs_base, obs_field, obs_weight, obs_count, obs_value, obs_precision):
    lat_rows = jnp.arange(NLAT, dtype=jnp.int32)
    open_rate = lat_coef * (lat_rows < NLAT - 1).astype(jnp.float32)[None, :]
    increment = control
    for step in range(SWEEPS):
        increment = diffuse_step(increment, lon_coef, open_rate)
    holder = jnp.arange(DEVICES, dtype=jnp.int32)
    lat_start = (holder % N_LAT) * CLAT
    lon_start = (holder // N_LAT) * CLON
    row_glob = obs_base // CLON + lat_start[:, None, None]
    col_glob = obs_base % CLON + lon_start[:, None, None]
    corner = ((obs_field * NLAT + row_glob) * NLON + col_glob).astype(jnp.int32)
    offsets = (0, 1, NLON, NLON + 1)
    flat_field = increment.reshape(-1)
    modelled = obs_weight[0] * flat_field[corner + offsets[0]]
    for k in range(1, 4):
        modelled = modelled + obs_weight[k] * flat_field[corner + offsets[k]]
    misfit = obs_precision * (jnp.transpose(modelled, (1, 0, 2)) - obs_value)
    back_misfit = jnp.transpose(misfit, (1, 0, 2))
    live_slot = jnp.arange(CAP, dtype=jnp.int32)[None, None, :] < obs_count[:, :, None]
    back_misfit = jnp.where(live_slot, back_misfit, jnp.float32(0.0))
    places = jnp.concatenate([(corner + o).reshape(-1) for o in offsets])
    amounts = jnp.concatenate([(obs_weight[k] * back_misfit).reshape(-1) for k in range(4)])
    forcing = jnp.zeros((F * NLAT * NLON,), jnp.float32).at[places].add(amounts)
    adjoint = forcing.reshape(F, NLAT, NLON)
    for step in range(SWEEPS):
        adjoint = diffuse_step(adjoint, lon_coef, open_rate)
    return increment, control + adjoint
```

```python
import jax
import jax.numpy as jnp
from jax import lax
from jax.experimental import pallas as pl
from jax.experimental.pallas import tpu as pltpu
from jax.sharding import PartitionSpec as P

SWEEPS = 4
PAD = 8
NACC = 8


def passed_along(value, axis, steps):
    count = lax.axis_size(axis)
    leading, last = (max(0, -steps), min(count, count - steps))
    return lax.ppermute(value, axis, [(source, source + steps) for source in range(leading, last)])


def padded_2(block, sides, width, periodic):
    for axis, dim in sides:
        count = lax.axis_size(axis)
        forward = [(i, i + 1) for i in range(count - 1)]
        if periodic:
            forward.append((count - 1, 0))
        backward = [(target, source) for source, target in forward]
        low = lax.ppermute(
            lax.slice_in_dim(block, block.shape[dim] - width, None, axis=dim), axis, forward
        )
        high = lax.ppermute(lax.slice_in_dim(block, 0, width, axis=dim), axis, backward)
        block = jnp.concatenate([low, block, high], axis=dim)
    return block


def diffuse_step(padded, zonal_rate, merid_rate):
    centre = padded[:, 1:-1, 1:-1]
    zonal = padded[:, 1:-1, 2:] + padded[:, 1:-1, :-2] - 2.0 * centre
    north = merid_rate[:, 1:-1, None] * (padded[:, 2:, 1:-1] - centre)
    south = merid_rate[:, :-2, None] * (centre - padded[:, :-2, 1:-1])
    return centre + zonal_rate[:, 1:-1, None] * zonal + north - south


def rate_rims(rates):
    below = passed_along(rates[1][:, -1:], "lat", 1)
    blank = jnp.zeros_like(below)
    zonal_rim = jnp.pad(rates[0], ((0, 0), (1, 1)))
    merid_rim = jnp.concatenate([below, rates[1], blank], axis=1)
    return jnp.stack([zonal_rim, merid_rim])


def covariance_root(field, rate_rim):
    for step in range(SWEEPS):
        padded = padded_2(field, (("lat", 1),), 1, False)
        padded = padded_2(padded, (("lon", 2),), 1, True)
        field = diffuse_step(padded, rate_rim[0], rate_rim[1])
    return field


def obs_kernel(cnt_ref, tab_ref, base_ref, field_ref, w_ref, val_ref, prec_ref, out_ref,
               tab, stack, dense, cidx, ridx, ridx_s, sem, *accs):
    rows = tab_ref.shape[0]
    cells = 16 * 128
    lane = lax.broadcasted_iota(jnp.int32, (8, 128), 1)
    sub = lax.broadcasted_iota(jnp.int32, (8, 128), 0)
    zero = jnp.zeros((8, 128), jnp.float32)

    @pl.loop(0, rows // 80)
    def _(i):
        for k in range(10):
            at = pl.multiple_of(i * 80 + 8 * k, 8)
            tab[pl.ds(at + PAD, 8), :] = tab_ref[pl.ds(at, 8), :]

    tab[pl.ds(0, 8), :] = zero
    tab[pl.ds(rows + PAD, 8), :] = zero

    @pl.loop(0, 16)
    def _(b):
        at = pl.multiple_of(b * 8, 8)
        part = pl.ds(at, 8)
        index = field_ref[part, :] * cells + base_ref[part, :]
        arrays = [w_ref[k, part, :] for k in range(4)]
        arrays += [val_ref[part, :], prec_ref[part, :], index.astype(jnp.float32)]
        for k, array in enumerate(arrays):
            stack[pl.ds(at * 8 + k, 8, stride=8), :] = array

    def compact(o, start):
        group = stack[pl.ds(pl.multiple_of(o * 8, 8), 8), :]
        shift = lax.bitwise_and(start, 127)
        row = pl.multiple_of(lax.shift_right_logical(start, 7) * 8, 8)
        rolled = pltpu.roll(group, shift, 1)
        dense[pl.ds(row, 8), :] = jnp.where(lane >= shift, rolled, dense[pl.ds(row, 8), :])
        dense[pl.ds(row + 8, 8), :] = rolled
        return start + cnt_ref[0, o]

    total = lax.fori_loop(0, 128, compact, jnp.int32(0), unroll=8)
    chunks = lax.shift_right_logical(total + 127, 7)

    @pl.loop(0, 16)
    def _(b):
        at = pl.multiple_of(b * 8, 8)
        index = dense[pl.ds(at * 8 + 6, 8, stride=8), :].astype(jnp.int32)
        position = (at + sub) * 128 + lane
        index = jnp.where(position < total, index, 0)
        cidx[pl.ds(at, 8), :] = lax.bitwise_and(index, 127)
        ridx[pl.ds(at, 8), :] = lax.shift_right_logical(index, 7) + PAD

    copy = pltpu.make_async_copy(ridx, ridx_s, sem)
    copy.start()

    @pl.loop(0, (rows + 2 * PAD) // 8)
    def _(i):
        for acc in accs:
            acc[pl.ds(pl.multiple_of(i * 8, 8), 8), :] = zero

    copy.wait()

    even = lax.bitwise_and(lane, 1) == 0
    quad = lax.shift_right_logical(sub, 1)
    first = lax.bitwise_and(sub, 1) == 0
    keys = (
        lax.shift_right_logical(lane, 1) - 16 * quad,
        lax.shift_right_logical(lax.bitwise_and(lane - 1, 127), 1) - 16 * quad,
    )

    def spread(row):
        return jnp.broadcast_to(row, (8, 128))

    def gather(d):
        group = dense[pl.ds(pl.multiple_of(d * 8, 8), 8), :]
        cols = spread(cidx[pl.ds(d, 1), :])
        after = pltpu.roll(cols, 1, 1) + 1
        starts = (jnp.where(even, cols, after), jnp.where(even, after, cols))
        w0 = jnp.where(first, spread(group[0:1]), spread(group[2:3]))
        w1 = pltpu.roll(jnp.where(first, spread(group[1:2]), spread(group[3:4])), 1, 1)
        weights = (jnp.where(even, w0, w1), jnp.where(even, w1, w0))
        sums = []
        for par in range(2):
            found = zero
            for g in range(16):
                merged = None
                for q in range(4):
                    r = ridx_s[d, 2 * (g + 16 * q) + par]
                    value = tab[pl.ds(r - 2 * q, 8), :]
                    merged = value if q == 0 else jnp.where(sub >= 2 * q, value, merged)
                picked = jnp.take_along_axis(merged, starts[par], axis=1, mode="promise_in_bounds")
                found = jnp.where(keys[par] == g, picked, found)
            sums.append(spread(jnp.sum(found * weights[par], axis=0, keepdims=True)))
        here = jnp.where(even, sums[0], sums[1])
        there = jnp.where(even, sums[1], sums[0])
        modelled = here + pltpu.roll(there, 127, 1)
        misfit = spread(group[5:6]) * (modelled - spread(group[4:5]))
        misfit = jnp.where(d * 128 + lane < total, misfit, 0.0)
        moved = pltpu.roll(misfit, 1, 1)
        amounts = (
            weights[0] * jnp.where(even, misfit, moved),
            weights[1] * jnp.where(even, moved, misfit),
        )
        return amounts[0], amounts[1], lane - cols

    def scatter(d, amounts, shift):
        for par in range(2):
            for g in range(16):
                masked = jnp.where(keys[par] == g, amounts[par], 0.0)
                turn = jnp.take_along_axis(shift, 2 * g + par + 32 * quad, axis=1, mode="promise_in_bounds")
                source = lax.bitwise_and(lane + turn, 127)
                placed = jnp.take_along_axis(masked, source, axis=1, mode="promise_in_bounds")
                for q in range(4):
                    r = ridx_s[d, 2 * (g + 16 * q) + par]
                    acc = accs[(g % (len(accs) // 4)) * 4 + q]
                    at = pl.ds(r - 2 * q, 8)
                    acc[at, :] = acc[at, :] + jnp.where(quad == q, placed, 0.0)

    def step(d, carry):
        new = gather(jnp.minimum(d, chunks - 1))
        scatter(jnp.maximum(d - 1, 0), carry[:2], carry[2])
        return new

    lax.fori_loop(0, chunks + 1, step, (zero, zero, lane))

    @pl.loop(0, rows // 8)
    def _(i):
        at = pl.multiple_of(i * 8, 8)
        parts = [acc[pl.ds(at + PAD, 8), :] for acc in accs]
        while len(parts) > 1:
            parts = [a + b for a, b in zip(parts[::2], parts[1::2])]
        out_ref[pl.ds(at, 8), :] = parts[0]


def observe(table, count, base, field, weight, value, precision):
    rows, cols = table.shape
    vmem = pl.BlockSpec(memory_space=pltpu.VMEM)
    smem = pl.BlockSpec(memory_space=pltpu.SMEM)
    return pl.pallas_call(
        obs_kernel,
        out_shape=jax.ShapeDtypeStruct((rows, cols), jnp.float32),
        in_specs=[smem] + [vmem] * 6,
        out_specs=vmem,
        scratch_shapes=[
            pltpu.VMEM((rows + 2 * PAD, cols), jnp.float32),
            pltpu.VMEM((1024, 128), jnp.float32),
            pltpu.VMEM((129 * 8, 128), jnp.float32),
            pltpu.VMEM((128, 128), jnp.int32),
            pltpu.VMEM((128, 128), jnp.int32),
            pltpu.SMEM((128, 128), jnp.int32),
            pltpu.SemaphoreType.DMA,
        ] + [pltpu.VMEM((rows + 2 * PAD, cols), jnp.float32)] * NACC,
        compiler_params=pltpu.CompilerParams(vmem_limit_bytes=40 * 2**20),
        name="observe",
    )(count, table, base, field, weight, value, precision)


def per_device(
    control,
    lon_coef,
    lat_coef,
    obs_base,
    obs_field,
    obs_weight,
    obs_count,
    obs_value,
    obs_precision,
):
    fields, band_rows, block_cols = control.shape
    lat_devices = lax.axis_size("lat")
    lat_rows = lax.axis_index("lat") * band_rows + jnp.arange(band_rows, dtype=jnp.int32)
    open_face = (lat_rows < band_rows * lat_devices - 1).astype(jnp.float32)
    rates = jnp.stack([lon_coef, lat_coef * open_face[None, :]])
    rate_rim = rate_rims(rates)
    increment = covariance_root(control, rate_rim)
    sent = jnp.stack([obs_value[0], obs_precision[0]], axis=1)
    held = lax.all_to_all(sent, ("lon", "lat"), split_axis=0, concat_axis=0, tiled=True)
    forcing = observe(
        increment.reshape(fields * band_rows, block_cols),
        obs_count,
        obs_base[0],
        obs_field[0],
        obs_weight[:, 0],
        held[:, 0],
        held[:, 1],
    )
    adjoint = covariance_root(forcing.reshape(fields, band_rows, block_cols), rate_rim)
    return (increment, control + adjoint)


def solution(mesh):
    in_specs = (
        P(None, "lat", "lon"),
        P(None, "lat"),
        P(None, "lat"),
        P(("lon", "lat"), None, None),
        P(("lon", "lat"), None, None),
        P(None, ("lon", "lat"), None, None),
        P(("lon", "lat"), None),
        P(("lon", "lat"), None, None),
        P(("lon", "lat"), None, None),
    )
    out_specs = (P(None, "lat", "lon"), P(None, "lat", "lon"))
    return jax.shard_map(
        per_device, mesh=mesh, in_specs=in_specs, out_specs=out_specs, check_vma=False
    )
```

```python
import functools

import jax
import jax.numpy as jnp
from jax import lax
from jax.experimental import pallas as pl
from jax.experimental.pallas import tpu as pltpu
from jax.sharding import PartitionSpec as P

MESH = pl.DeviceIdType.MESH
DEEP = 4
STRIP = 10

def root_kernel(first, unroll, *refs):
    if first:
        (x_ref, lon_ref, lat_ref, out_ref, coef_out, *scratch) = refs
    else:
        (x_ref, coef_ref, out_ref, *scratch) = refs
    (main, main2, side, side2, zonal, merid, centre, packed, left, right, *scratch) = scratch
    if first:
        (coef, square, *scratch) = scratch
    send_sems, recv_sems = scratch
    fields, rows, cols = x_ref.shape
    ext = rows + 2 * DEEP
    n_lon, n_lat = lax.axis_size("lon"), lax.axis_size("lat")
    lon, lat = lax.axis_index("lon"), lax.axis_index("lat")
    west, east = lax.rem(lon + n_lon - 1, n_lon), lax.rem(lon + 1, n_lon)
    has_up, has_down = lat > 0, lat < n_lat - 1
    lane = lax.broadcasted_iota(jnp.int32, (8, cols), 1)

    barrier = pltpu.get_barrier_semaphore()

    def greet(there_lon, there_lat):
        pl.semaphore_signal(barrier, inc=1, device_id={"lon": there_lon, "lat": there_lat}, device_id_type=MESH)

    greet(west, lat)
    greet(east, lat)
    for present, there_lat in ((has_up, lat - 1), (has_down, lat + 1)):
        @pl.when(present)
        def _():
            for there_lon in (lon, west, east):
                greet(there_lon, there_lat)

    kinds = iter(range(16))

    def sending(source, target, there_lon, there_lat):
        kind = next(kinds)
        return pltpu.make_async_remote_copy(
            src_ref=source, dst_ref=target, send_sem=send_sems.at[kind], recv_sem=recv_sems.at[kind],
            device_id={"lon": there_lon, "lat": there_lat}, device_id_type=MESH,
        )

    low, high, own = pl.ds(0, DEEP), pl.ds(rows + DEEP, DEEP), pl.ds(DEEP, rows)
    top, bottom = pl.ds(0, DEEP), pl.ds(rows - DEEP, DEEP)
    up_main = sending(x_ref.at[:, top], main.at[:, high], lon, lat - 1)
    down_main = sending(x_ref.at[:, bottom], main.at[:, low], lon, lat + 1)
    to_west = sending(packed, right.at[:, own], west, lat)
    to_east = sending(packed, left.at[:, own], east, lat)
    up_west = sending(packed.at[:, top], right.at[:, high], west, lat - 1)
    up_east = sending(packed.at[:, top], left.at[:, high], east, lat - 1)
    down_west = sending(packed.at[:, bottom], right.at[:, low], west, lat + 1)
    down_east = sending(packed.at[:, bottom], left.at[:, low], east, lat + 1)
    ups, downs, flats = [up_main, up_west, up_east], [down_main, down_west, down_east], [to_west, to_east]
    if first:
        pair = pl.ds(0, 2)
        up_coef = sending(coef.at[pair, pl.ds(DEEP, DEEP)], coef.at[pair, high], lon, lat - 1)
        down_coef = sending(coef.at[pair, pl.ds(rows, DEEP)], coef.at[pair, low], lon, lat + 1)
        ups.append(up_coef)
        downs.append(down_coef)
        square[...] = jnp.zeros_like(square)
        square[pl.ds(0, fields), pl.ds(0, rows)] = lon_ref[...]
        square[pl.ds(0, fields), pl.ds(64, rows)] = lat_ref[...]
        turned = square[...].T
        coef[0, own] = turned[0:rows]
        row = lax.broadcasted_iota(jnp.int32, (rows, cols), 0)
        closed = jnp.logical_and(row == rows - 1, lat == n_lat - 1)
        coef[1, own] = jnp.where(closed, 0.0, turned[64:64 + rows])

    @pl.loop(0, fields // STRIP)
    def _(g):
        for part in range(rows // 8):
            strips = None
            for k in range(STRIP):
                value = x_ref[g * STRIP + k, pl.ds(8 * part, 8), :]
                if k == 0:
                    strips = value
                else:
                    key = lax.shift_right_logical(lax.bitwise_and(lane + 4, 127), 3)
                    strips = jnp.where(key == k, pltpu.roll(value, 8 * k, 1), strips)
            packed[g, pl.ds(8 * part, 8), :] = strips

    pl.semaphore_wait(barrier, 2 + 3 * has_up.astype(jnp.int32) + 3 * has_down.astype(jnp.int32))

    for present, group, at in ((has_up, ups, low), (has_down, downs, high)):
        @pl.when(present)
        def _():
            for copy in (group if not first else group[-1:] + group[:-1]):
                copy.start()

        @pl.when(jnp.logical_not(present))
        def _():
            main[:, at] = jnp.zeros((fields, DEEP, cols), jnp.float32)
            for halo in (left, right):
                halo[:, at] = jnp.zeros((fields // STRIP, DEEP, cols), jnp.float32)
            if first:
                coef[pl.ds(0, 2), at] = jnp.zeros((2, DEEP, cols), jnp.float32)

    for copy in flats:
        copy.start()

    @pl.loop(0, fields // 10)
    def _(g):
        for k in range(10):
            for part in range(rows // 8):
                main[g * 10 + k, pl.ds(DEEP + 8 * part, 8), :] = x_ref[g * 10 + k, pl.ds(8 * part, 8), :]

    if first:
        @pl.when(has_up)
        def _():
            down_coef.wait_recv()

        @pl.when(has_down)
        def _():
            up_coef.wait_recv()

        coef[2] = jnp.zeros((ext, cols), jnp.float32)
        for start in (1, 9, ext - 9):
            at = pl.ds(start, 8)
            coef[2, at] = 1.0 - 2.0 * coef[0, at] - coef[1, at] - coef[1, pl.ds(start - 1, 8)]
        coef_ref = coef
        coef_out[...] = coef[...]

    @pl.loop(0, fields // 5)
    def _(g):
        tables = [[coef_ref[k, pl.ds(8 * part, 8), :] for part in range(ext // 8)] for k in range(3)]
        for k in range(5):
            f = g * 5 + k
            which = jnp.full((8, cols), f, jnp.int32)
            for table, target in zip(tables, (zonal, merid, centre)):
                for part in range(ext // 8):
                    target[f, pl.ds(8 * part, 8), :] = jnp.take_along_axis(
                        table[part], which, axis=1, mode="promise_in_bounds")

    for copy in flats:
        copy.wait_recv()

    @pl.when(has_up)
    def _():
        for copy in downs[:3]:
            copy.wait_recv()

    @pl.when(has_down)
    def _():
        for copy in ups[:3]:
            copy.wait_recv()

    @pl.loop(0, fields // STRIP)
    def _(g):
        for part in range(ext // 8):
            at = pl.ds(8 * part, 8)
            both = jnp.where(lax.bitwise_and(lane, 7) >= 4, left[g, at, :], right[g, at, :])
            for k in range(STRIP):
                side[g * STRIP + k, at, :] = pltpu.roll(both, (-8 * k) % 128, 1) if k else both

    def sweep(source, source_side, target, target_side, starts, shift):
        @pl.loop(0, fields // unroll)
        def _(g):
            for k in range(unroll):
                f = g * unroll + k
                for start in starts:
                    at, before, after = pl.ds(start, 8), pl.ds(start - 1, 8), pl.ds(start + 1, 8)
                    m, e = source[f, at, :], source_side[f, at, :]
                    m_w, e_w, m_e, e_e = (pltpu.roll(m, 1, 1), pltpu.roll(e, 1, 1), pltpu.roll(m, 127, 1), pltpu.roll(e, 127, 1))
                    c, z, n, s = centre[f, at, :], zonal[f, at, :], merid[f, at, :], merid[f, before, :]
                    out = c * m + z * (jnp.where(lane == 0, e_w, m_w) + jnp.where(lane == 127, e_e, m_e))
                    out = out + n * source[f, after, :] + s * source[f, before, :]
                    target[f, pl.ds(start - shift, 8), :] = out
                    if target_side is not None:
                        out = c * e + z * (jnp.where(lane == 0, m_w, e_w) + jnp.where(lane == 127, m_e, e_e))
                        out = out + n * source_side[f, after, :] + s * source_side[f, before, :]
                        target_side[f, at, :] = out

    sweep(main, side, main2, side2, (1, 9, 15), 0)
    sweep(main2, side2, main, side, (2, 10, 14), 0)
    sweep(main, side, main2, side2, (3, 11, 13), 0)
    sweep(main2, side2, out_ref, None, (4, 12), 4)

    for copy in flats:
        copy.wait_send()

    @pl.when(has_up)
    def _():
        for copy in ups:
            copy.wait_send()

    @pl.when(has_down)
    def _():
        for copy in downs:
            copy.wait_send()


def root(field, coefs, first, unroll=5):
    fields, rows, cols = field.shape
    ext = rows + 2 * DEEP
    vmem = pl.BlockSpec(memory_space=pltpu.VMEM)
    f32 = lambda *shape: jax.ShapeDtypeStruct(shape, jnp.float32)
    big = pltpu.VMEM((fields, ext, cols), jnp.float32)
    strips = fields // STRIP
    scratch = [big] * 7 + [pltpu.VMEM((strips, rows, cols), jnp.float32)] + [pltpu.VMEM((strips, ext, cols), jnp.float32)] * 2
    outs = [f32(fields, rows, cols)]
    if first:
        scratch += [pltpu.VMEM((3, ext, cols), jnp.float32), pltpu.VMEM((128, 128), jnp.float32)]
        outs.append(f32(3, ext, cols))
    count = 10 if first else 8
    scratch += [pltpu.SemaphoreType.DMA((count,))] * 2
    return pl.pallas_call(
        functools.partial(root_kernel, first, unroll),
        out_shape=outs,
        in_specs=[vmem] * (1 + len(coefs)),
        out_specs=[vmem] * len(outs),
        scratch_shapes=scratch,
        compiler_params=pltpu.CompilerParams(
            collective_id=0 if first else 1, has_side_effects=True, vmem_limit_bytes=48 * 2**20),
        name="root_first" if first else "root_second",
    )(field, *coefs)


PAD = 8
NACC = 8

def obs_kernel(cnt_ref, tab_ref, base_ref, field_ref, w_ref, val_ref, prec_ref, inc_ref, out_ref,
               tab, stack, dense, cidx, ridx, ridx_s, sem, *accs):
    rows = tab_ref.shape[0]
    cells = 16 * 128
    lane = lax.broadcasted_iota(jnp.int32, (8, 128), 1)
    sub = lax.broadcasted_iota(jnp.int32, (8, 128), 0)
    zero = jnp.zeros((8, 128), jnp.float32)

    @pl.loop(0, rows // 80)
    def _(i):
        for k in range(10):
            at = pl.multiple_of(i * 80 + 8 * k, 8)
            value = tab_ref[pl.ds(at, 8), :]
            tab[pl.ds(at + PAD, 8), :] = value
            inc_ref[pl.ds(at, 8), :] = value

    tab[pl.ds(0, 8), :] = zero
    tab[pl.ds(rows + PAD, 8), :] = zero

    @pl.loop(0, 16)
    def _(b):
        at = pl.multiple_of(b * 8, 8)
        part = pl.ds(at, 8)
        index = field_ref[part, :] * cells + base_ref[part, :]
        arrays = [w_ref[k, part, :] for k in range(4)]
        arrays += [val_ref[part, :], prec_ref[part, :], index.astype(jnp.float32)]
        for k, array in enumerate(arrays):
            stack[pl.ds(at * 8 + k, 8, stride=8), :] = array

    def compact(o, start):
        group = stack[pl.ds(pl.multiple_of(o * 8, 8), 8), :]
        shift = lax.bitwise_and(start, 127)
        row = pl.multiple_of(lax.shift_right_logical(start, 7) * 8, 8)
        rolled = pltpu.roll(group, shift, 1)
        dense[pl.ds(row, 8), :] = jnp.where(lane >= shift, rolled, dense[pl.ds(row, 8), :])
        dense[pl.ds(row + 8, 8), :] = rolled
        return start + cnt_ref[0, o]

    total = lax.fori_loop(0, 128, compact, jnp.int32(0), unroll=8)
    chunks = lax.shift_right_logical(total + 127, 7)

    @pl.loop(0, 16)
    def _(b):
        at = pl.multiple_of(b * 8, 8)
        index = dense[pl.ds(at * 8 + 6, 8, stride=8), :].astype(jnp.int32)
        position = (at + sub) * 128 + lane
        index = jnp.where(position < total, index, 0)
        cidx[pl.ds(at, 8), :] = lax.bitwise_and(index, 127)
        ridx[pl.ds(at, 8), :] = lax.shift_right_logical(index, 7) + PAD

    copy = pltpu.make_async_copy(ridx, ridx_s, sem)
    copy.start()

    @pl.loop(0, (rows + 2 * PAD) // 8)
    def _(i):
        for acc in accs:
            acc[pl.ds(pl.multiple_of(i * 8, 8), 8), :] = zero

    copy.wait()

    even = lax.bitwise_and(lane, 1) == 0
    quad = lax.shift_right_logical(sub, 1)
    first = lax.bitwise_and(sub, 1) == 0
    keys = (
        lax.shift_right_logical(lane, 1) - 16 * quad,
        lax.shift_right_logical(lax.bitwise_and(lane - 1, 127), 1) - 16 * quad,
    )

    def spread(row):
        return jnp.broadcast_to(row, (8, 128))

    def gather(d):
        group = dense[pl.ds(pl.multiple_of(d * 8, 8), 8), :]
        cols = spread(cidx[pl.ds(d, 1), :])
        after = pltpu.roll(cols, 1, 1) + 1
        starts = (jnp.where(even, cols, after), jnp.where(even, after, cols))
        w0 = jnp.where(first, spread(group[0:1]), spread(group[2:3]))
        w1 = pltpu.roll(jnp.where(first, spread(group[1:2]), spread(group[3:4])), 1, 1)
        weights = (jnp.where(even, w0, w1), jnp.where(even, w1, w0))
        sums = []
        for par in range(2):
            found = zero
            for g in range(16):
                merged = None
                for q in range(4):
                    r = ridx_s[d, 2 * (g + 16 * q) + par]
                    value = tab[pl.ds(r - 2 * q, 8), :]
                    merged = value if q == 0 else jnp.where(sub >= 2 * q, value, merged)
                picked = jnp.take_along_axis(merged, starts[par], axis=1, mode="promise_in_bounds")
                found = jnp.where(keys[par] == g, picked, found)
            sums.append(spread(jnp.sum(found * weights[par], axis=0, keepdims=True)))
        here = jnp.where(even, sums[0], sums[1])
        there = jnp.where(even, sums[1], sums[0])
        modelled = here + pltpu.roll(there, 127, 1)
        misfit = spread(group[5:6]) * (modelled - spread(group[4:5]))
        misfit = jnp.where(d * 128 + lane < total, misfit, 0.0)
        moved = pltpu.roll(misfit, 1, 1)
        amounts = (
            weights[0] * jnp.where(even, misfit, moved),
            weights[1] * jnp.where(even, moved, misfit),
        )
        return amounts[0], amounts[1], lane - cols

    def scatter(d, amounts, shift):
        for par in range(2):
            for g in range(16):
                masked = jnp.where(keys[par] == g, amounts[par], 0.0)
                turn = jnp.take_along_axis(shift, 2 * g + par + 32 * quad, axis=1, mode="promise_in_bounds")
                source = lax.bitwise_and(lane + turn, 127)
                placed = jnp.take_along_axis(masked, source, axis=1, mode="promise_in_bounds")
                for q in range(4):
                    r = ridx_s[d, 2 * (g + 16 * q) + par]
                    acc = accs[(g % (len(accs) // 4)) * 4 + q]
                    at = pl.ds(r - 2 * q, 8)
                    acc[at, :] = acc[at, :] + jnp.where(quad == q, placed, 0.0)

    def step(d, carry):
        new = gather(jnp.minimum(d, chunks - 1))
        scatter(jnp.maximum(d - 1, 0), carry[:2], carry[2])
        return new

    lax.fori_loop(0, chunks + 1, step, (zero, zero, lane))

    @pl.loop(0, rows // 8)
    def _(i):
        at = pl.multiple_of(i * 8, 8)
        parts = [acc[pl.ds(at + PAD, 8), :] for acc in accs]
        while len(parts) > 1:
            parts = [a + b for a, b in zip(parts[::2], parts[1::2])]
        out_ref[pl.ds(at, 8), :] = parts[0]


def observe(table, count, base, field, weight, value, precision):
    rows, cols = table.shape
    vmem = pl.BlockSpec(memory_space=pltpu.VMEM)
    smem = pl.BlockSpec(memory_space=pltpu.SMEM)
    return pl.pallas_call(
        obs_kernel,
        out_shape=[jax.ShapeDtypeStruct((rows, cols), jnp.float32)] * 2,
        in_specs=[smem] + [vmem] * 6,
        out_specs=[vmem] * 2,
        scratch_shapes=[
            pltpu.VMEM((rows + 2 * PAD, cols), jnp.float32),
            pltpu.VMEM((1024, 128), jnp.float32),
            pltpu.VMEM((129 * 8, 128), jnp.float32),
            pltpu.VMEM((128, 128), jnp.int32),
            pltpu.VMEM((128, 128), jnp.int32),
            pltpu.SMEM((128, 128), jnp.int32),
            pltpu.SemaphoreType.DMA,
        ] + [pltpu.VMEM((rows + 2 * PAD, cols), jnp.float32)] * NACC,
        compiler_params=pltpu.CompilerParams(vmem_limit_bytes=40 * 2**20),
        name="observe",
    )(count, table, base, field, weight, value, precision)


def per_device(
    control,
    lon_coef,
    lat_coef,
    obs_base,
    obs_field,
    obs_weight,
    obs_count,
    obs_value,
    obs_precision,
):
    fields, band_rows, block_cols = control.shape
    sent = jnp.stack([obs_value[0], obs_precision[0]], axis=1)
    held = lax.all_to_all(sent, ("lon", "lat"), split_axis=0, concat_axis=0, tiled=True)
    increment, coefs = root(control, (lon_coef, lat_coef), True)
    increment, forcing = observe(
        increment.reshape(fields * band_rows, block_cols),
        obs_count,
        obs_base[0],
        obs_field[0],
        obs_weight[:, 0],
        held[:, 0],
        held[:, 1],
    )
    (adjoint,) = root(forcing.reshape(control.shape), (coefs,), False)
    return (increment.reshape(control.shape), control + adjoint)


def solution(mesh):
    in_specs = (
        P(None, "lat", "lon"),
        P(None, "lat"),
        P(None, "lat"),
        P(("lon", "lat"), None, None),
        P(("lon", "lat"), None, None),
        P(None, ("lon", "lat"), None, None),
        P(("lon", "lat"), None),
        P(("lon", "lat"), None, None),
        P(("lon", "lat"), None, None),
    )
    out_specs = (P(None, "lat", "lon"), P(None, "lat", "lon"))
    return jax.shard_map(
        per_device, mesh=mesh, in_specs=in_specs, out_specs=out_specs, check_vma=False
    )
```

```python
import functools

import jax
import jax.numpy as jnp
from jax import lax
from jax.experimental import pallas as pl
from jax.experimental.pallas import tpu as pltpu
from jax.sharding import PartitionSpec as P

MESH = pl.DeviceIdType.MESH
DEEP = 4
STRIP = 10
GROUP = 20
UNROLL = 20


LANES = lax.GatherDimensionNumbers(
    offset_dims=(), collapsed_slice_dims=(1,), start_index_map=(1,),
    operand_batching_dims=(0,), start_indices_batching_dims=(0,))


def pick_lanes(value, index):
    return lax.gather(value, index[:, :, None], LANES, slice_sizes=(1, 1), mode="promise_in_bounds")


def root_kernel(first, *refs):
    if first:
        (x_ref, zonal_ref, merid_ref, value_ref, precision_ref, out_ref, coef_out, value_out, precision_out, *scratch) = refs
        (coef, value_mid, precision_mid, near_sems, far_sems, own_sems, *scratch) = scratch
    else:
        (x_ref, coef, out_ref, *scratch) = refs
    (main, main2, side, side2, zonal, merid, centre, packed, left, right, send_sems, recv_sems) = scratch
    fields, rows, cols = x_ref.shape
    ext = rows + 2 * DEEP
    groups, strips = fields // GROUP, GROUP // STRIP
    n_lon, n_lat = lax.axis_size("lon"), lax.axis_size("lat")
    lon, lat = lax.axis_index("lon"), lax.axis_index("lat")
    west, east = lax.rem(lon + n_lon - 1, n_lon), lax.rem(lon + 1, n_lon)
    has_up, has_down = lat > 0, lat < n_lat - 1
    lane = lax.broadcasted_iota(jnp.int32, (8, cols), 1)
    low, high, own = pl.ds(0, DEEP), pl.ds(rows + DEEP, DEEP), pl.ds(DEEP, rows)
    top, bottom = pl.ds(0, DEEP), pl.ds(rows - DEEP, DEEP)

    barrier = pltpu.get_barrier_semaphore()

    def greet(there_lon, there_lat):
        pl.semaphore_signal(barrier, inc=1, device_id={"lon": there_lon, "lat": there_lat}, device_id_type=MESH)

    sides = has_up.astype(jnp.int32) + has_down.astype(jnp.int32)
    for present, there_lat in ((has_up, lat - 1), (has_down, lat + 1)):
        @pl.when(present)
        def _():
            for there_lon in (west, east) if first else (lon, west, east):
                greet(there_lon, there_lat)

    if first:
        for k in range(1, n_lat):
            greet(lon, lax.rem(lat + k, n_lat))

        @pl.loop(1, n_lon)
        def _(k):
            greet(lax.rem(lon + k, n_lon), lat)

        greetings = 2 * sides + (n_lat - 1) + (n_lon - 1)
    else:
        greet(west, lat)
        greet(east, lat)
        greetings = 3 * sides + 2

    def remote(source, target, send, recv, there_lon, there_lat):
        return pltpu.make_async_remote_copy(
            src_ref=source, dst_ref=target, send_sem=send, recv_sem=recv,
            device_id={"lon": there_lon, "lat": there_lat}, device_id_type=MESH,
        )

    def exchange(kind, g):
        fs, ss = pl.ds(g * GROUP, GROUP), pl.ds(g * strips, strips)
        source, target, there_lon, there_lat = {
            "up_main": (x_ref.at[fs, top], main.at[fs, high], lon, lat - 1),
            "up_west": (packed.at[ss, top], right.at[ss, high], west, lat - 1),
            "up_east": (packed.at[ss, top], left.at[ss, high], east, lat - 1),
            "down_main": (x_ref.at[fs, bottom], main.at[fs, low], lon, lat + 1),
            "down_west": (packed.at[ss, bottom], right.at[ss, low], west, lat + 1),
            "down_east": (packed.at[ss, bottom], left.at[ss, low], east, lat + 1),
            "west": (packed.at[ss], right.at[ss, own], west, lat),
            "east": (packed.at[ss], left.at[ss, own], east, lat),
        }[kind]
        slot = KINDS.index(kind)
        return remote(source, target, send_sems.at[slot, g], recv_sems.at[slot, g], there_lon, there_lat)

    def exchange_coef(kind):
        pair, slot = pl.ds(0, 2), KINDS.index(kind)
        source, target, there_lat = {
            "up_coef": (coef.at[pair, pl.ds(DEEP, DEEP)], coef.at[pair, high], lat - 1),
            "down_coef": (coef.at[pair, pl.ds(rows, DEEP)], coef.at[pair, low], lat + 1),
        }[kind]
        return remote(source, target, send_sems.at[slot, 0], recv_sems.at[slot, 0], lon, there_lat)

    if first:
        row = lax.broadcasted_iota(jnp.int32, (rows, fields), 0)
        closed = jnp.logical_and(row == rows - 1, lat == n_lat - 1)
        blank = jnp.zeros((rows, cols), jnp.float32)
        for k, rates in enumerate((zonal_ref[...], jnp.where(closed, 0.0, merid_ref[...]))):
            coef[k, own] = blank
            coef[k, own, pl.ds(0, fields)] = rates

    pl.semaphore_wait(barrier, greetings)

    for present, way, at in ((has_up, "up", low), (has_down, "down", high)):
        @pl.when(present)
        def _():
            if first:
                exchange_coef(way + "_coef").start()

            @pl.loop(0, groups)
            def _(g):
                exchange(way + "_main", g).start()

        @pl.when(jnp.logical_not(present))
        def _():
            main[:, at] = jnp.zeros((fields, DEEP, cols), jnp.float32)
            for halo in (left, right):
                halo[:, at] = jnp.zeros((fields // STRIP, DEEP, cols), jnp.float32)
            if first:
                coef[pl.ds(0, 2), at] = jnp.zeros((2, DEEP, cols), jnp.float32)

    key = lax.shift_right_logical(lax.bitwise_and(lane + 4, 127), 3)

    @pl.loop(0, groups)
    def _(g):
        for s in range(strips):
            for part in range(rows // 8):
                at = pl.ds(8 * part, 8)
                strip = x_ref[g * GROUP + s * STRIP, at, :]
                for k in range(1, STRIP):
                    value = x_ref[g * GROUP + s * STRIP + k, at, :]
                    strip = jnp.where(key == k, pltpu.roll(value, 8 * k, 1), strip)
                packed[g * strips + s, at, :] = strip
        exchange("west", g).start()
        exchange("east", g).start()
        for present, way in ((has_up, "up"), (has_down, "down")):
            @pl.when(present)
            def _():
                exchange(way + "_west", g).start()
                exchange(way + "_east", g).start()

    if first:
        pairs = ((value_ref, value_mid, value_out), (precision_ref, precision_mid, precision_out))

        def near(n, k):
            source, target, _ = pairs[n]
            there = lax.rem(lat + k, n_lat)
            return remote(source.at[:, there], target.at[lat], near_sems.at[0, n, k], near_sems.at[1, n, k], lon, there)

        def far(n, k):
            _, source, target = pairs[n]
            there = lax.rem(lon + k, n_lon)
            return remote(source.at[:, there], target.at[lon], far_sems.at[0, n, k], far_sems.at[1, n, k], there, lat)

        def stays(n, stage):
            source, middle, target = pairs[n]
            if stage == 0:
                return pltpu.make_async_copy(source.at[:, lat], middle.at[lat], own_sems.at[0, n])
            return pltpu.make_async_copy(middle.at[:, lon], target.at[lon], own_sems.at[1, n])

        for n in range(2):
            for k in range(1, n_lat):
                near(n, k).start()
            stays(n, 0).start()

    @pl.loop(0, fields // 10)
    def _(g):
        for k in range(10):
            for part in range(rows // 8):
                main[g * 10 + k, pl.ds(DEEP + 8 * part, 8), :] = x_ref[g * 10 + k, pl.ds(8 * part, 8), :]

    def spread_tables(tables, targets):
        @pl.loop(0, fields // 10)
        def _(g):
            for k in range(10):
                f = g * 10 + k
                which = jnp.full((8, cols), f, jnp.int32)
                for table, (target, places) in zip(tables, targets):
                    value = pick_lanes(table, which)
                    for start, size, at in places:
                        target[f, pl.ds(at, size), :] = value[start:start + size]

    whole = lambda at: ((0, 8, at),)
    if first:
        spread_tables(
            [coef[k, pl.ds(at, 8), :] for k in range(2) for at in (DEEP, DEEP + 8)],
            [(target, whole(at)) for target in (zonal, merid) for at in (DEEP, DEEP + 8)],
        )
        for n in range(2):
            for k in range(1, n_lat):
                near(n, k).wait_recv()
            stays(n, 0).wait()

        @pl.loop(1, n_lon)
        def _(k):
            for n in range(2):
                far(n, k).start()

        for n in range(2):
            stays(n, 1).start()

        for present, way in ((has_up, "down_coef"), (has_down, "up_coef")):
            @pl.when(present)
            def _():
                exchange_coef(way).wait_recv()

        coef[2] = jnp.zeros((ext, cols), jnp.float32)
        for start in (1, 9, ext - 9):
            at = pl.ds(start, 8)
            coef[2, at] = 1.0 - 2.0 * coef[0, at] - coef[1, at] - coef[1, pl.ds(start - 1, 8)]
        coef_out[...] = coef[...]
        rims = [jnp.concatenate([coef[k, low], coef[k, high]], axis=0) for k in range(2)]
        parts = ((0, DEEP, 0), (DEEP, DEEP, rows + DEEP))
        spread_tables(
            rims + [coef[2, pl.ds(8 * part, 8), :] for part in range(ext // 8)],
            [(zonal, parts), (merid, parts)] + [(centre, whole(8 * part)) for part in range(ext // 8)],
        )
    else:
        spread_tables(
            [coef[k, pl.ds(8 * part, 8), :] for k in range(3) for part in range(ext // 8)],
            [(target, whole(8 * part)) for target in (zonal, merid, centre) for part in range(ext // 8)],
        )

    def sweep(g, source, source_side, target, target_side, starts, shift):
        def fields_from(base):
            for k in range(UNROLL):
                f = base + k
                for start in starts:
                    at, before, after = pl.ds(start, 8), pl.ds(start - 1, 8), pl.ds(start + 1, 8)
                    m, e = source[f, at, :], source_side[f, at, :]
                    m_w, e_w = pltpu.roll(m, 1, 1), pltpu.roll(e, 1, 1)
                    m_e, e_e = pltpu.roll(m, 127, 1), pltpu.roll(e, 127, 1)
                    c, z, n, s = centre[f, at, :], zonal[f, at, :], merid[f, at, :], merid[f, before, :]
                    out = c * m + z * (jnp.where(lane == 0, e_w, m_w) + jnp.where(lane == 127, e_e, m_e))
                    out = out + n * source[f, after, :] + s * source[f, before, :]
                    target[f, pl.ds(start - shift, 8), :] = out
                    if target_side is not None:
                        out = c * e + z * (jnp.where(lane == 0, m_w, e_w) + jnp.where(lane == 127, m_e, e_e))
                        out = out + n * source_side[f, after, :] + s * source_side[f, before, :]
                        target_side[f, at, :] = out

        if UNROLL == GROUP:
            fields_from(g * GROUP)
        else:
            @pl.loop(0, GROUP // UNROLL)
            def _(u):
                fields_from(g * GROUP + u * UNROLL)

    @pl.loop(0, groups)
    def _(g):
        for kind in ("west", "east"):
            exchange(kind, g).wait_recv()
        for present, way in ((has_up, "down"), (has_down, "up")):
            @pl.when(present)
            def _():
                for kind in ("_main", "_west", "_east"):
                    exchange(way + kind, g).wait_recv()

        for s in range(strips):
            for part in range(ext // 8):
                at = pl.ds(8 * part, 8)
                both = jnp.where(lax.bitwise_and(lane, 7) >= 4, left[g * strips + s, at, :], right[g * strips + s, at, :])
                for k in range(STRIP):
                    side[g * GROUP + s * STRIP + k, at, :] = pltpu.roll(both, (-8 * k) % 128, 1) if k else both

        sweep(g, main, side, main2, side2, (1, 9, 15), 0)
        sweep(g, main2, side2, main, side, (2, 10, 14), 0)
        sweep(g, main, side, main2, side2, (3, 11, 13), 0)
        sweep(g, main2, side2, out_ref, None, (4, 12), 4)

    @pl.loop(0, groups)
    def _(g):
        for kind in ("west", "east"):
            exchange(kind, g).wait_send()
        for present, way in ((has_up, "up"), (has_down, "down")):
            @pl.when(present)
            def _():
                for kind in ("_main", "_west", "_east"):
                    exchange(way + kind, g).wait_send()

    if first:
        for present, way in ((has_up, "up_coef"), (has_down, "down_coef")):
            @pl.when(present)
            def _():
                exchange_coef(way).wait_send()

        for n in range(2):
            for k in range(1, n_lat):
                near(n, k).wait_send()

        @pl.loop(1, n_lon)
        def _(k):
            for n in range(2):
                far(n, k).wait_recv()
                far(n, k).wait_send()

        for n in range(2):
            stays(n, 1).wait()


KINDS = (
    "up_main", "up_west", "up_east", "down_main", "down_west", "down_east", "west", "east", "up_coef", "down_coef",
)


def root(field, operands, first):
    fields, rows, cols = field.shape
    ext = rows + 2 * DEEP
    vmem = pl.BlockSpec(memory_space=pltpu.VMEM)
    f32 = lambda *shape: jax.ShapeDtypeStruct(shape, jnp.float32)
    scratch = [pltpu.VMEM((fields, ext, cols), jnp.float32)] * 7
    scratch += [pltpu.VMEM((fields // STRIP, rows, cols), jnp.float32)]
    scratch += [pltpu.VMEM((fields // STRIP, ext, cols), jnp.float32)] * 2
    scratch += [pltpu.SemaphoreType.DMA((len(KINDS), fields // GROUP))] * 2
    outs = [f32(fields, rows, cols)]
    in_specs, out_specs = [vmem] * (1 + len(operands)), [vmem]
    if first:
        anywhere = [pl.BlockSpec(memory_space=pl.ANY)] * 2
        in_specs[3:] = anywhere
        out_specs += [vmem] + anywhere
        n_lon, n_lat = lax.axis_size("lon"), lax.axis_size("lat")
        outs += [f32(3, ext, cols)] + [f32(n_lon, n_lat, 1, cols)] * 2
        scratch = (
            [pltpu.VMEM((3, ext, cols), jnp.float32)]
            + [pltpu.VMEM((n_lat, n_lon, 1, cols), jnp.float32)] * 2
            + [pltpu.SemaphoreType.DMA((2, 2, n_lat)), pltpu.SemaphoreType.DMA((2, 2, n_lon)), pltpu.SemaphoreType.DMA((2, 2))]
            + scratch
        )
    return pl.pallas_call(
        functools.partial(root_kernel, first),
        out_shape=outs,
        in_specs=in_specs,
        out_specs=out_specs,
        scratch_shapes=scratch,
        compiler_params=pltpu.CompilerParams(
            collective_id=0 if first else 1, has_side_effects=True, vmem_limit_bytes=60 * 2**20),
        name="root_first" if first else "root_second",
    )(field, *operands)


PAD = 8
NACC = 8


def obs_kernel(cnt_ref, tab_ref, base_ref, field_ref, w_ref, val_ref, prec_ref, inc_ref, out_ref,
               tab, stack, dense, cidx, ridx, ridx_s, sem, *accs):
    rows = tab_ref.shape[0]
    cells = 16 * 128
    lane = lax.broadcasted_iota(jnp.int32, (8, 128), 1)
    sub = lax.broadcasted_iota(jnp.int32, (8, 128), 0)
    zero = jnp.zeros((8, 128), jnp.float32)

    @pl.loop(0, rows // 80)
    def _(i):
        for k in range(10):
            at = pl.multiple_of(i * 80 + 8 * k, 8)
            value = tab_ref[pl.ds(at, 8), :]
            tab[pl.ds(at + PAD, 8), :] = value
            inc_ref[pl.ds(at, 8), :] = value

    tab[pl.ds(0, 8), :] = zero
    tab[pl.ds(rows + PAD, 8), :] = zero

    @pl.loop(0, 16)
    def _(b):
        at = pl.multiple_of(b * 8, 8)
        part = pl.ds(at, 8)
        index = field_ref[part, :] * cells + base_ref[part, :]
        arrays = [w_ref[k, part, :] for k in range(4)]
        arrays += [val_ref[part, :], prec_ref[part, :], index.astype(jnp.float32)]
        for k, array in enumerate(arrays):
            stack[pl.ds(at * 8 + k, 8, stride=8), :] = array

    def compact(o, start):
        group = stack[pl.ds(pl.multiple_of(o * 8, 8), 8), :]
        shift = lax.bitwise_and(start, 127)
        row = pl.multiple_of(lax.shift_right_logical(start, 7) * 8, 8)
        rolled = pltpu.roll(group, shift, 1)
        dense[pl.ds(row, 8), :] = jnp.where(lane >= shift, rolled, dense[pl.ds(row, 8), :])
        dense[pl.ds(row + 8, 8), :] = rolled
        return start + cnt_ref[0, o]

    total = lax.fori_loop(0, 128, compact, jnp.int32(0), unroll=8)
    chunks = lax.shift_right_logical(total + 127, 7)

    @pl.loop(0, 16)
    def _(b):
        at = pl.multiple_of(b * 8, 8)
        index = dense[pl.ds(at * 8 + 6, 8, stride=8), :].astype(jnp.int32)
        position = (at + sub) * 128 + lane
        index = jnp.where(position < total, index, 0)
        cidx[pl.ds(at, 8), :] = lax.bitwise_and(index, 127)
        ridx[pl.ds(at, 8), :] = lax.shift_right_logical(index, 7) + PAD

    copy = pltpu.make_async_copy(ridx, ridx_s, sem)
    copy.start()

    @pl.loop(0, (rows + 2 * PAD) // 8)
    def _(i):
        for acc in accs:
            acc[pl.ds(pl.multiple_of(i * 8, 8), 8), :] = zero

    copy.wait()

    even = lax.bitwise_and(lane, 1) == 0
    quad = lax.shift_right_logical(sub, 1)
    first = lax.bitwise_and(sub, 1) == 0
    keys = (
        lax.shift_right_logical(lane, 1) - 16 * quad,
        lax.shift_right_logical(lax.bitwise_and(lane - 1, 127), 1) - 16 * quad,
    )

    def spread(row):
        return jnp.broadcast_to(row, (8, 128))

    def gather(d):
        group = dense[pl.ds(pl.multiple_of(d * 8, 8), 8), :]
        cols = spread(cidx[pl.ds(d, 1), :])
        after = pltpu.roll(cols, 1, 1) + 1
        starts = (jnp.where(even, cols, after), jnp.where(even, after, cols))
        w0 = jnp.where(first, spread(group[0:1]), spread(group[2:3]))
        w1 = pltpu.roll(jnp.where(first, spread(group[1:2]), spread(group[3:4])), 1, 1)
        weights = (jnp.where(even, w0, w1), jnp.where(even, w1, w0))
        row_at = ridx_s.at[d]
        sums = []
        for par in range(2):
            found = zero
            for g in range(16):
                merged = None
                for q in range(4):
                    r = row_at[2 * (g + 16 * q) + par]
                    value = tab[pl.ds(r - 2 * q, 8), :]
                    merged = value if q == 0 else jnp.where(sub >= 2 * q, value, merged)
                picked = pick_lanes(merged, starts[par])
                found = jnp.where(keys[par] == g, picked, found)
            sums.append(spread(jnp.sum(found * weights[par], axis=0, keepdims=True)))
        here = jnp.where(even, sums[0], sums[1])
        there = jnp.where(even, sums[1], sums[0])
        modelled = here + pltpu.roll(there, 127, 1)
        misfit = spread(group[5:6]) * (modelled - spread(group[4:5]))
        misfit = jnp.where(d * 128 + lane < total, misfit, 0.0)
        moved = pltpu.roll(misfit, 1, 1)
        amounts = (
            weights[0] * jnp.where(even, misfit, moved),
            weights[1] * jnp.where(even, moved, misfit),
        )
        return amounts[0], amounts[1], lane - cols

    lane_par = lax.bitwise_and(lane, 1)
    ones = jnp.ones((128, 128), jnp.bfloat16)

    def scatter(d, amounts, shift):
        row_at = ridx_s.at[d]
        turn = shift.astype(jnp.float32)
        picked = [jnp.where(jnp.logical_and(keys[par] == g, lane_par == par), turn, 0.0) for par in range(2) for g in range(16)]
        picked = jnp.concatenate(picked, axis=0).astype(jnp.bfloat16)
        turns = jnp.dot(picked, ones, preferred_element_type=jnp.float32).astype(jnp.int32)
        for par in range(2):
            for g in range(16):
                masked = jnp.where(keys[par] == g, amounts[par], 0.0)
                at = 8 * (16 * par + g)
                source = lax.bitwise_and(lane + turns[at:at + 8], 127)
                placed = pick_lanes(masked, source)
                for q in range(4):
                    r = row_at[2 * (g + 16 * q) + par]
                    acc = accs[(g % (len(accs) // 4)) * 4 + q]
                    at = pl.ds(r - 2 * q, 8)
                    acc[at, :] = acc[at, :] + jnp.where(quad == q, placed, 0.0)

    def step(d, carry):
        new = gather(jnp.minimum(d, chunks - 1))
        scatter(jnp.maximum(d - 1, 0), carry[:2], carry[2])
        return new

    lax.fori_loop(0, chunks + 1, step, (zero, zero, lane))

    @pl.loop(0, rows // 8)
    def _(i):
        at = pl.multiple_of(i * 8, 8)
        parts = [acc[pl.ds(at + PAD, 8), :] for acc in accs]
        while len(parts) > 1:
            parts = [a + b for a, b in zip(parts[::2], parts[1::2])]
        out_ref[pl.ds(at, 8), :] = parts[0]


def observe(table, count, base, field, weight, value, precision):
    rows, cols = table.shape
    vmem = pl.BlockSpec(memory_space=pltpu.VMEM)
    smem = pl.BlockSpec(memory_space=pltpu.SMEM)
    return pl.pallas_call(
        obs_kernel,
        out_shape=[jax.ShapeDtypeStruct((rows, cols), jnp.float32)] * 2,
        in_specs=[smem] + [vmem] * 6,
        out_specs=[vmem] * 2,
        scratch_shapes=[
            pltpu.VMEM((rows + 2 * PAD, cols), jnp.float32),
            pltpu.VMEM((1024, 128), jnp.float32),
            pltpu.VMEM((129 * 8, 128), jnp.float32),
            pltpu.VMEM((128, 128), jnp.int32),
            pltpu.VMEM((128, 128), jnp.int32),
            pltpu.SMEM((128, 128), jnp.int32),
            pltpu.SemaphoreType.DMA,
        ] + [pltpu.VMEM((rows + 2 * PAD, cols), jnp.float32)] * NACC,
        compiler_params=pltpu.CompilerParams(vmem_limit_bytes=60 * 2**20),
        name="observe",
    )(count, table, base, field, weight, value, precision)


def per_device(
    control,
    lon_coef,
    lat_coef,
    obs_base,
    obs_field,
    obs_weight,
    obs_count,
    obs_value,
    obs_precision,
):
    fields, band_rows, block_cols = control.shape
    owners, slots = obs_base.shape[1:]
    by_device = (lax.axis_size("lon"), lax.axis_size("lat"), 1, slots)
    increment, coefs, value, precision = root(
        control,
        (lon_coef.T, lat_coef.T, obs_value.reshape(by_device), obs_precision.reshape(by_device)),
        True,
    )
    increment, forcing = observe(
        increment.reshape(fields * band_rows, block_cols),
        obs_count,
        obs_base[0],
        obs_field[0],
        obs_weight[:, 0],
        value.reshape(owners, slots),
        precision.reshape(owners, slots),
    )
    (adjoint,) = root(forcing.reshape(control.shape), (coefs,), False)
    return (increment.reshape(control.shape), control + adjoint)


def solution(mesh):
    in_specs = (
        P(None, "lat", "lon"),
        P(None, "lat"),
        P(None, "lat"),
        P(("lon", "lat"), None, None),
        P(("lon", "lat"), None, None),
        P(None, ("lon", "lat"), None, None),
        P(("lon", "lat"), None),
        P(("lon", "lat"), None, None),
        P(("lon", "lat"), None, None),
    )
    out_specs = (P(None, "lat", "lon"), P(None, "lat", "lon"))
    return jax.shard_map(
        per_device, mesh=mesh, in_specs=in_specs, out_specs=out_specs, check_vma=False
    )
```

```python
import functools

import jax
import jax.numpy as jnp
from jax import lax
from jax.experimental import pallas as pl
from jax.experimental.pallas import tpu as pltpu
from jax.sharding import PartitionSpec as P

MESH = pl.DeviceIdType.MESH
DEEP = 4
STRIP = 10
GROUP = 20
UNROLL = 20


LANES = lax.GatherDimensionNumbers(
    offset_dims=(), collapsed_slice_dims=(1,), start_index_map=(1,),
    operand_batching_dims=(0,), start_indices_batching_dims=(0,))


def pick_lanes(value, index):
    return lax.gather(value, index[:, :, None], LANES, slice_sizes=(1, 1), mode="promise_in_bounds")


def root_kernel(first, *refs):
    if first:
        (x_ref, zonal_ref, merid_ref, value_ref, precision_ref, out_ref, coef_out, value_out, precision_out, *scratch) = refs
        (coef, value_mid, precision_mid, near_sems, far_sems, own_sems, *scratch) = scratch
    else:
        (x_ref, coef, add_hbm, out_ref, add_ref, add_sem, *scratch) = refs
        addend = pltpu.make_async_copy(add_hbm, add_ref, add_sem)
        addend.start()
    (main, main2, side, side2, zonal, merid, centre, packed, left, right, send_sems, recv_sems) = scratch
    fields, rows, cols = x_ref.shape
    ext = rows + 2 * DEEP
    groups, strips = fields // GROUP, GROUP // STRIP
    n_lon, n_lat = lax.axis_size("lon"), lax.axis_size("lat")
    lon, lat = lax.axis_index("lon"), lax.axis_index("lat")
    west, east = lax.rem(lon + n_lon - 1, n_lon), lax.rem(lon + 1, n_lon)
    has_up, has_down = lat > 0, lat < n_lat - 1
    lane = lax.broadcasted_iota(jnp.int32, (8, cols), 1)
    low, high, own = pl.ds(0, DEEP), pl.ds(rows + DEEP, DEEP), pl.ds(DEEP, rows)
    top, bottom = pl.ds(0, DEEP), pl.ds(rows - DEEP, DEEP)

    barrier = pltpu.get_barrier_semaphore()

    def greet(there_lon, there_lat):
        pl.semaphore_signal(barrier, inc=1, device_id={"lon": there_lon, "lat": there_lat}, device_id_type=MESH)

    sides = has_up.astype(jnp.int32) + has_down.astype(jnp.int32)
    for present, there_lat in ((has_up, lat - 1), (has_down, lat + 1)):
        @pl.when(present)
        def _():
            for there_lon in (west, east) if first else (lon, west, east):
                greet(there_lon, there_lat)

    if first:
        for k in range(1, n_lat):
            greet(lon, lax.rem(lat + k, n_lat))

        @pl.loop(1, n_lon)
        def _(k):
            greet(lax.rem(lon + k, n_lon), lat)

        greetings = 2 * sides + (n_lat - 1) + (n_lon - 1)
    else:
        greet(west, lat)
        greet(east, lat)
        greetings = 3 * sides + 2

    def remote(source, target, send, recv, there_lon, there_lat):
        return pltpu.make_async_remote_copy(
            src_ref=source, dst_ref=target, send_sem=send, recv_sem=recv,
            device_id={"lon": there_lon, "lat": there_lat}, device_id_type=MESH,
        )

    def exchange(kind, g):
        fs, ss = pl.ds(g * GROUP, GROUP), pl.ds(g * strips, strips)
        source, target, there_lon, there_lat = {
            "up_main": (x_ref.at[fs, top], main.at[fs, high], lon, lat - 1),
            "up_west": (packed.at[ss, top], right.at[ss, high], west, lat - 1),
            "up_east": (packed.at[ss, top], left.at[ss, high], east, lat - 1),
            "down_main": (x_ref.at[fs, bottom], main.at[fs, low], lon, lat + 1),
            "down_west": (packed.at[ss, bottom], right.at[ss, low], west, lat + 1),
            "down_east": (packed.at[ss, bottom], left.at[ss, low], east, lat + 1),
            "west": (packed.at[ss], right.at[ss, own], west, lat),
            "east": (packed.at[ss], left.at[ss, own], east, lat),
        }[kind]
        slot = KINDS.index(kind)
        return remote(source, target, send_sems.at[slot, g], recv_sems.at[slot, g], there_lon, there_lat)

    def exchange_coef(kind):
        pair, slot = pl.ds(0, 2), KINDS.index(kind)
        source, target, there_lat = {
            "up_coef": (coef.at[pair, pl.ds(DEEP, DEEP)], coef.at[pair, high], lat - 1),
            "down_coef": (coef.at[pair, pl.ds(rows, DEEP)], coef.at[pair, low], lat + 1),
        }[kind]
        return remote(source, target, send_sems.at[slot, 0], recv_sems.at[slot, 0], lon, there_lat)

    if first:
        row = lax.broadcasted_iota(jnp.int32, (rows, fields), 0)
        closed = jnp.logical_and(row == rows - 1, lat == n_lat - 1)
        blank = jnp.zeros((rows, cols), jnp.float32)
        for k, rates in enumerate((zonal_ref[...], jnp.where(closed, 0.0, merid_ref[...]))):
            coef[k, own] = blank
            coef[k, own, pl.ds(0, fields)] = rates

    pl.semaphore_wait(barrier, greetings)

    for present, way, at in ((has_up, "up", low), (has_down, "down", high)):
        @pl.when(present)
        def _():
            if first:
                exchange_coef(way + "_coef").start()

            @pl.loop(0, groups)
            def _(g):
                exchange(way + "_main", g).start()

        @pl.when(jnp.logical_not(present))
        def _():
            main[:, at] = jnp.zeros((fields, DEEP, cols), jnp.float32)
            for halo in (left, right):
                halo[:, at] = jnp.zeros((fields // STRIP, DEEP, cols), jnp.float32)
            if first:
                coef[pl.ds(0, 2), at] = jnp.zeros((2, DEEP, cols), jnp.float32)

    key = lax.shift_right_logical(lax.bitwise_and(lane + 4, 127), 3)

    @pl.loop(0, groups)
    def _(g):
        for s in range(strips):
            for part in range(rows // 8):
                at = pl.ds(8 * part, 8)
                strip = x_ref[g * GROUP + s * STRIP, at, :]
                for k in range(1, STRIP):
                    value = x_ref[g * GROUP + s * STRIP + k, at, :]
                    strip = jnp.where(key == k, pltpu.roll(value, 8 * k, 1), strip)
                packed[g * strips + s, at, :] = strip
        exchange("west", g).start()
        exchange("east", g).start()
        for present, way in ((has_up, "up"), (has_down, "down")):
            @pl.when(present)
            def _():
                exchange(way + "_west", g).start()
                exchange(way + "_east", g).start()

    if first:
        pairs = ((value_ref, value_mid, value_out), (precision_ref, precision_mid, precision_out))

        def near(n, k):
            source, target, _ = pairs[n]
            there = lax.rem(lat + k, n_lat)
            return remote(source.at[:, there], target.at[lat], near_sems.at[0, n, k], near_sems.at[1, n, k], lon, there)

        def far(n, k):
            _, source, target = pairs[n]
            there = lax.rem(lon + k, n_lon)
            return remote(source.at[:, there], target.at[lon], far_sems.at[0, n, k], far_sems.at[1, n, k], there, lat)

        def stays(n, stage):
            source, middle, target = pairs[n]
            if stage == 0:
                return pltpu.make_async_copy(source.at[:, lat], middle.at[lat], own_sems.at[0, n])
            return pltpu.make_async_copy(middle.at[:, lon], target.at[lon], own_sems.at[1, n])

        for n in range(2):
            for k in range(1, n_lat):
                near(n, k).start()
            stays(n, 0).start()

    @pl.loop(0, fields // 10)
    def _(g):
        for k in range(10):
            for part in range(rows // 8):
                main[g * 10 + k, pl.ds(DEEP + 8 * part, 8), :] = x_ref[g * 10 + k, pl.ds(8 * part, 8), :]

    def spread_tables(tables, targets):
        @pl.loop(0, fields // 10)
        def _(g):
            for k in range(10):
                f = g * 10 + k
                which = jnp.full((8, cols), f, jnp.int32)
                for table, (target, places) in zip(tables, targets):
                    value = pick_lanes(table, which)
                    for start, size, at in places:
                        target[f, pl.ds(at, size), :] = value[start:start + size]

    whole = lambda at: ((0, 8, at),)
    if first:
        spread_tables(
            [coef[k, pl.ds(at, 8), :] for k in range(2) for at in (DEEP, DEEP + 8)],
            [(target, whole(at)) for target in (zonal, merid) for at in (DEEP, DEEP + 8)],
        )
        for n in range(2):
            for k in range(1, n_lat):
                near(n, k).wait_recv()
            stays(n, 0).wait()

        @pl.loop(1, n_lon)
        def _(k):
            for n in range(2):
                far(n, k).start()

        for n in range(2):
            stays(n, 1).start()

        for present, way in ((has_up, "down_coef"), (has_down, "up_coef")):
            @pl.when(present)
            def _():
                exchange_coef(way).wait_recv()

        coef[2] = jnp.zeros((ext, cols), jnp.float32)
        for start in (1, 9, ext - 9):
            at = pl.ds(start, 8)
            coef[2, at] = 1.0 - 2.0 * coef[0, at] - coef[1, at] - coef[1, pl.ds(start - 1, 8)]
        coef_out[...] = coef[...]
        rims = [jnp.concatenate([coef[k, low], coef[k, high]], axis=0) for k in range(2)]
        parts = ((0, DEEP, 0), (DEEP, DEEP, rows + DEEP))
        spread_tables(
            rims + [coef[2, pl.ds(8 * part, 8), :] for part in range(ext // 8)],
            [(zonal, parts), (merid, parts)] + [(centre, whole(8 * part)) for part in range(ext // 8)],
        )
    else:
        spread_tables(
            [coef[k, pl.ds(8 * part, 8), :] for k in range(3) for part in range(ext // 8)],
            [(target, whole(8 * part)) for target in (zonal, merid, centre) for part in range(ext // 8)],
        )

    def sweep(g, source, source_side, target, target_side, starts, shift):
        last = target_side is None and not first

        def fields_from(base):
            for k in range(UNROLL):
                f = base + k
                for start in starts:
                    at, before, after = pl.ds(start, 8), pl.ds(start - 1, 8), pl.ds(start + 1, 8)
                    m, e = source[f, at, :], source_side[f, at, :]
                    m_w, e_w = pltpu.roll(m, 1, 1), pltpu.roll(e, 1, 1)
                    m_e, e_e = pltpu.roll(m, 127, 1), pltpu.roll(e, 127, 1)
                    c, z, n, s = centre[f, at, :], zonal[f, at, :], merid[f, at, :], merid[f, before, :]
                    out = c * m + z * (jnp.where(lane == 0, e_w, m_w) + jnp.where(lane == 127, e_e, m_e))
                    out = out + n * source[f, after, :] + s * source[f, before, :]
                    if last:
                        out = out + add_ref[f, pl.ds(start - shift, 8), :]
                    target[f, pl.ds(start - shift, 8), :] = out
                    if target_side is not None:
                        out = c * e + z * (jnp.where(lane == 0, m_w, e_w) + jnp.where(lane == 127, m_e, e_e))
                        out = out + n * source_side[f, after, :] + s * source_side[f, before, :]
                        target_side[f, at, :] = out

        if UNROLL == GROUP:
            fields_from(g * GROUP)
        else:
            @pl.loop(0, GROUP // UNROLL)
            def _(u):
                fields_from(g * GROUP + u * UNROLL)

    if not first:
        addend.wait()

    @pl.loop(0, groups)
    def _(g):
        for kind in ("west", "east"):
            exchange(kind, g).wait_recv()
        for present, way in ((has_up, "down"), (has_down, "up")):
            @pl.when(present)
            def _():
                for kind in ("_main", "_west", "_east"):
                    exchange(way + kind, g).wait_recv()

        for s in range(strips):
            for part in range(ext // 8):
                at = pl.ds(8 * part, 8)
                both = jnp.where(lax.bitwise_and(lane, 7) >= 4, left[g * strips + s, at, :], right[g * strips + s, at, :])
                for k in range(STRIP):
                    side[g * GROUP + s * STRIP + k, at, :] = pltpu.roll(both, (-8 * k) % 128, 1) if k else both

        sweep(g, main, side, main2, side2, (1, 9, 15), 0)
        sweep(g, main2, side2, main, side, (2, 10, 14), 0)
        sweep(g, main, side, main2, side2, (3, 11, 13), 0)
        sweep(g, main2, side2, out_ref, None, (4, 12), 4)

    @pl.loop(0, groups)
    def _(g):
        for kind in ("west", "east"):
            exchange(kind, g).wait_send()
        for present, way in ((has_up, "up"), (has_down, "down")):
            @pl.when(present)
            def _():
                for kind in ("_main", "_west", "_east"):
                    exchange(way + kind, g).wait_send()

    if first:
        for present, way in ((has_up, "up_coef"), (has_down, "down_coef")):
            @pl.when(present)
            def _():
                exchange_coef(way).wait_send()

        for n in range(2):
            for k in range(1, n_lat):
                near(n, k).wait_send()

        @pl.loop(1, n_lon)
        def _(k):
            for n in range(2):
                far(n, k).wait_recv()
                far(n, k).wait_send()

        for n in range(2):
            stays(n, 1).wait()


KINDS = (
    "up_main", "up_west", "up_east", "down_main", "down_west", "down_east", "west", "east", "up_coef", "down_coef",
)


def root(field, operands, first):
    fields, rows, cols = field.shape
    ext = rows + 2 * DEEP
    vmem = pl.BlockSpec(memory_space=pltpu.VMEM)
    f32 = lambda *shape: jax.ShapeDtypeStruct(shape, jnp.float32)
    scratch = [pltpu.VMEM((fields, ext, cols), jnp.float32)] * 7
    scratch += [pltpu.VMEM((fields // STRIP, rows, cols), jnp.float32)]
    scratch += [pltpu.VMEM((fields // STRIP, ext, cols), jnp.float32)] * 2
    scratch += [pltpu.SemaphoreType.DMA((len(KINDS), fields // GROUP))] * 2
    outs = [f32(fields, rows, cols)]
    in_specs, out_specs = [vmem] * (1 + len(operands)), [vmem]
    if first:
        anywhere = [pl.BlockSpec(memory_space=pl.ANY)] * 2
        in_specs[3:] = anywhere
        out_specs += [vmem] + anywhere
        n_lon, n_lat = lax.axis_size("lon"), lax.axis_size("lat")
        outs += [f32(3, ext, cols)] + [f32(n_lon, n_lat, 1, cols)] * 2
        scratch = (
            [pltpu.VMEM((3, ext, cols), jnp.float32)]
            + [pltpu.VMEM((n_lat, n_lon, 1, cols), jnp.float32)] * 2
            + [pltpu.SemaphoreType.DMA((2, 2, n_lat)), pltpu.SemaphoreType.DMA((2, 2, n_lon)), pltpu.SemaphoreType.DMA((2, 2))]
            + scratch
        )
    else:
        in_specs[2] = pl.BlockSpec(memory_space=pl.ANY)
        scratch = [pltpu.VMEM((fields, rows, cols), jnp.float32), pltpu.SemaphoreType.DMA] + scratch
    return pl.pallas_call(
        functools.partial(root_kernel, first),
        out_shape=outs,
        in_specs=in_specs,
        out_specs=out_specs,
        scratch_shapes=scratch,
        compiler_params=pltpu.CompilerParams(
            collective_id=0 if first else 1, has_side_effects=True, vmem_limit_bytes=60 * 2**20),
        name="root_first" if first else "root_second",
    )(field, *operands)


PAD = 8
NACC = 8


def obs_kernel(cnt_ref, tab_hbm, base_hbm, field_hbm, w_hbm, val_hbm, prec_hbm, inc_hbm, out_ref,
               base_ref, field_ref, w_ref, val_ref, prec_ref, in_sems,
               tab, stack, dense, plan, cidx, ridx, ridx_s, sem, windows, places, sources, *accs):
    rows = tab_hbm.shape[0]
    cells = 16 * 128
    lane = lax.broadcasted_iota(jnp.int32, (8, 128), 1)
    sub = lax.broadcasted_iota(jnp.int32, (8, 128), 0)
    zero = jnp.zeros((8, 128), jnp.float32)
    body = pl.ds(PAD, rows)
    loads = [
        pltpu.make_async_copy(source, target, in_sems.at[k])
        for k, (source, target) in enumerate((
            (base_hbm, base_ref), (field_hbm, field_ref), (w_hbm, w_ref), (val_hbm, val_ref), (prec_hbm, prec_ref),
            (tab_hbm, tab.at[body]),
        ))
    ]
    keep = pltpu.make_async_copy(tab.at[body], inc_hbm, in_sems.at[6])
    for load in loads:
        load.start()
    tab[pl.ds(0, 8), :] = zero
    tab[pl.ds(rows + PAD, 8), :] = zero
    for load in loads[:-1]:
        load.wait()

    @pl.loop(0, 16)
    def _(b):
        at = pl.multiple_of(b * 8, 8)
        part = pl.ds(at, 8)
        index = field_ref[part, :] * cells + base_ref[part, :]
        arrays = [w_ref[k, part, :] for k in range(4)]
        arrays += [val_ref[part, :], prec_ref[part, :], index.astype(jnp.float32)]
        for k, array in enumerate(arrays):
            stack[pl.ds(at * 8 + k, 8, stride=8), :] = array

    def compact(o, carry):
        start, kept = carry
        group = stack[pl.ds(pl.multiple_of(o * 8, 8), 8), :]
        shift = lax.bitwise_and(start, 127)
        row = lax.shift_right_logical(start, 7)
        rolled = pltpu.roll(group, shift, 1)
        merged = jnp.where(lane >= shift, rolled, kept)
        at = pl.multiple_of(row * 8, 8)
        dense[pl.ds(at, 8), :] = merged
        dense[pl.ds(at + 8, 8), :] = rolled
        after = start + cnt_ref[0, o]
        moved = lax.shift_right_logical(after, 7) > row
        return after, jnp.where(moved, rolled, merged)

    total, _ = lax.fori_loop(0, 128, compact, (jnp.int32(0), zero), unroll=32)
    chunks = lax.shift_right_logical(total + 127, 7)

    even = lax.bitwise_and(lane, 1) == 0

    def paired(low, high, add=0):
        after = pltpu.roll(high, 1, 1) + add
        return jnp.where(even, low, after), jnp.where(even, after, low)

    @pl.loop(0, 16)
    def _(b):
        at = pl.multiple_of(b * 8, 8)
        part = pl.ds(at, 8)
        arrays = [dense[pl.ds(at * 8 + k, 8, stride=8), :] for k in range(7)]
        live = (at + sub) * 128 + lane < total
        index = jnp.where(live, arrays[6].astype(jnp.int32), 0)
        ridx[part, :] = lax.shift_right_logical(index, 7) + PAD
        cols = lax.bitwise_and(index, 127)
        cidx[0, part, :], cidx[1, part, :] = paired(cols, cols, 1)
        cidx[2, part, :] = lane - cols
        for a in range(2):
            first_row, second_row = paired(arrays[2 * a], arrays[2 * a + 1])
            plan[a, part, :], plan[2 + a, part, :] = first_row, second_row
        precision = jnp.where(live, arrays[5], 0.0)
        value = jnp.where(live, arrays[4], 0.0)
        plan[4, part, :], plan[5, part, :] = value, precision
        plan[6, part, :], plan[7, part, :] = pltpu.roll(value, 1, 1), pltpu.roll(precision, 1, 1)

    copy = pltpu.make_async_copy(ridx, ridx_s, sem)
    copy.start()

    @pl.loop(0, (rows + 2 * PAD) // 16)
    def _(i):
        for acc in accs:
            for k in range(2):
                acc[pl.ds(pl.multiple_of(i * 16 + 8 * k, 8), 8), :] = zero

    copy.wait()
    loads[-1].wait()
    keep.start()

    quad = lax.shift_right_logical(sub, 1)
    first = lax.bitwise_and(sub, 1) == 0
    keys = (
        lax.shift_right_logical(lane, 1) - 16 * quad,
        lax.shift_right_logical(lax.bitwise_and(lane - 1, 127), 1) - 16 * quad,
    )

    def spread(row):
        return jnp.broadcast_to(row, (8, 128))

    def weights(d):
        line = pl.ds(d, 1)
        return [jnp.where(first, spread(plan[2 * par, line, :]), spread(plan[2 * par + 1, line, :])) for par in range(2)]

    def load_windows(d):
        row_at = ridx_s.at[d]
        for par in range(2):
            for g in range(16):
                merged = None
                for q in range(4):
                    r = row_at[2 * (g + 16 * q) + par]
                    value = tab[pl.ds(r - 2 * q, 8), :]
                    merged = value if q == 0 else jnp.where(sub >= 2 * q, value, merged)
                windows[16 * par + g] = merged

    def gather(d):
        sums = []
        for par in range(2):
            start = spread(cidx[par, pl.ds(d, 1), :])
            found = zero
            for g in range(16):
                found = jnp.where(keys[par] == g, pick_lanes(windows[16 * par + g], start), found)
            sums.append(found)
        return sums

    def compare(d, found):
        line = pl.ds(d, 1)
        weight = weights(d)
        sums = [spread(jnp.sum(found[par] * weight[par], axis=0, keepdims=True)) for par in range(2)]
        here = jnp.where(even, sums[0], sums[1])
        there = jnp.where(even, sums[1], sums[0])
        value, precision, value_w, precision_w = [spread(plan[k, line, :]) for k in range(4, 8)]
        misfit = precision * (here + pltpu.roll(there, 127, 1) - value)
        moved = precision_w * (pltpu.roll(here, 1, 1) + there - value_w)
        return (
            weight[0] * jnp.where(even, misfit, moved),
            weight[1] * jnp.where(even, moved, misfit),
        )

    lane_par = lax.bitwise_and(lane, 1)
    ones = jnp.ones((128, 128), jnp.bfloat16)

    def turn_lanes(d):
        turn = spread(cidx[2, pl.ds(d, 1), :]).astype(jnp.float32)
        picked = [
            jnp.where(jnp.logical_and(keys[par] == g, lane_par == par), turn, 0.0)
            for par in range(2) for g in range(16)
        ]
        picked = jnp.concatenate(picked, axis=0).astype(jnp.bfloat16)
        turns = jnp.dot(picked, ones, preferred_element_type=jnp.float32).astype(jnp.int32)
        for k in range(32):
            sources[k] = lax.bitwise_and(lane + turns[8 * k:8 * k + 8], 127)

    def place(amounts):
        for par in range(2):
            for g in range(16):
                masked = jnp.where(keys[par] == g, amounts[par], 0.0)
                places[16 * par + g] = pick_lanes(masked, sources[16 * par + g])

    def add_rows(d):
        row_at = ridx_s.at[d]
        for par in range(2):
            for g in range(16):
                placed = places[16 * par + g]
                for q in range(4):
                    r = row_at[2 * (g + 16 * q) + par]
                    acc = accs[(g % (len(accs) // 4)) * 4 + q]
                    at = pl.ds(r - 2 * q, 8)
                    acc[at, :] = acc[at, :] + jnp.where(quad == q, placed, 0.0)

    for k in range(32):
        windows[k] = zero
        places[k] = zero
        sources[k] = lane

    def step(d, carry):
        found_e, found_o, amounts_e, amounts_o = carry
        last = chunks - 1
        add_rows(jnp.clip(d - 4, 0, last))
        place((amounts_e, amounts_o))
        turn_lanes(jnp.clip(d - 2, 0, last))
        amounts = compare(jnp.clip(d - 2, 0, last), (found_e, found_o))
        found = gather(jnp.clip(d - 1, 0, last))
        load_windows(jnp.minimum(d, last))
        ready = d > 1
        return (*found, jnp.where(ready, amounts[0], 0.0), jnp.where(ready, amounts[1], 0.0))

    lax.fori_loop(0, chunks + 4, step, (zero,) * 4)

    @pl.loop(0, rows // 80)
    def _(i):
        for k in range(10):
            at = pl.multiple_of(i * 80 + 8 * k, 8)
            parts = [acc[pl.ds(at + PAD, 8), :] for acc in accs]
            while len(parts) > 1:
                parts = [a + b for a, b in zip(parts[::2], parts[1::2])]
            out_ref[pl.ds(at, 8), :] = parts[0]

    keep.wait()


def observe(table, count, base, field, weight, value, precision):
    rows, cols = table.shape
    vmem = pl.BlockSpec(memory_space=pltpu.VMEM)
    anywhere = pl.BlockSpec(memory_space=pl.ANY)
    smem = pl.BlockSpec(memory_space=pltpu.SMEM)
    return pl.pallas_call(
        obs_kernel,
        out_shape=[jax.ShapeDtypeStruct((rows, cols), jnp.float32)] * 2,
        in_specs=[smem] + [anywhere] * 6,
        out_specs=[anywhere, vmem],
        scratch_shapes=[
            pltpu.VMEM((128, 128), jnp.int32),
            pltpu.VMEM((128, 128), jnp.int32),
            pltpu.VMEM((4, 128, 128), jnp.float32),
            pltpu.VMEM((128, 128), jnp.float32),
            pltpu.VMEM((128, 128), jnp.float32),
            pltpu.SemaphoreType.DMA((7,)),
            pltpu.VMEM((rows + 2 * PAD, cols), jnp.float32),
            pltpu.VMEM((1024, 128), jnp.float32),
            pltpu.VMEM((129 * 8, 128), jnp.float32),
            pltpu.VMEM((8, 128, 128), jnp.float32),
            pltpu.VMEM((3, 128, 128), jnp.int32),
            pltpu.VMEM((128, 128), jnp.int32),
            pltpu.SMEM((128, 128), jnp.int32),
            pltpu.SemaphoreType.DMA,
            pltpu.VMEM((32, 8, 128), jnp.float32),
            pltpu.VMEM((32, 8, 128), jnp.float32),
            pltpu.VMEM((32, 8, 128), jnp.int32),
        ] + [pltpu.VMEM((rows + 2 * PAD, cols), jnp.float32)] * NACC,
        compiler_params=pltpu.CompilerParams(vmem_limit_bytes=60 * 2**20),
        name="observe",
    )(count, table, base, field, weight, value, precision)


def per_device(
    control,
    lon_coef,
    lat_coef,
    obs_base,
    obs_field,
    obs_weight,
    obs_count,
    obs_value,
    obs_precision,
):
    fields, band_rows, block_cols = control.shape
    owners, slots = obs_base.shape[1:]
    by_device = (lax.axis_size("lon"), lax.axis_size("lat"), 1, slots)
    increment, coefs, value, precision = root(
        control,
        (lon_coef.T, lat_coef.T, obs_value.reshape(by_device), obs_precision.reshape(by_device)),
        True,
    )
    increment, forcing = observe(
        increment.reshape(fields * band_rows, block_cols),
        obs_count,
        obs_base[0],
        obs_field[0],
        obs_weight[:, 0],
        value.reshape(owners, slots),
        precision.reshape(owners, slots),
    )
    (gradient,) = root(forcing.reshape(control.shape), (coefs, control), False)
    return (increment.reshape(control.shape), gradient)


def solution(mesh):
    in_specs = (
        P(None, "lat", "lon"),
        P(None, "lat"),
        P(None, "lat"),
        P(("lon", "lat"), None, None),
        P(("lon", "lat"), None, None),
        P(None, ("lon", "lat"), None, None),
        P(("lon", "lat"), None),
        P(("lon", "lat"), None, None),
        P(("lon", "lat"), None, None),
    )
    out_specs = (P(None, "lat", "lon"), P(None, "lat", "lon"))
    return jax.shard_map(
        per_device, mesh=mesh, in_specs=in_specs, out_specs=out_specs, check_vma=False
    )
```

```python
import functools

import jax
import jax.numpy as jnp
from jax import lax
from jax.experimental import pallas as pl
from jax.experimental.pallas import tpu as pltpu
from jax.sharding import PartitionSpec as P

MESH = pl.DeviceIdType.MESH
DEEP = 4
EDGE = 8
KINDS = (
    "up_main", "up_west", "up_east", "down_main", "down_west", "down_east", "west", "east", "up_coef", "down_coef",
)


def root_kernel(first, rows, *refs):
    if first:
        (x_ref, zonal_ref, merid_ref, value_ref, precision_ref, out_ref, coef_out, value_out, precision_out, *scratch) = refs
        (coef, value_mid, precision_mid, near_sems, far_sems, own_sems, *scratch) = scratch
    else:
        (x_ref, coef, add_hbm, out_ref, add_ref, add_sem, *scratch) = refs
        addend = pltpu.make_async_copy(add_hbm, add_ref, add_sem)
        addend.start()
    (main, main2, send_sems, recv_sems) = scratch
    cols = x_ref.shape[1]
    fields = x_ref.shape[0] // rows
    ext = rows + 2 * DEEP
    n_lon, n_lat = lax.axis_size("lon"), lax.axis_size("lat")
    lon, lat = lax.axis_index("lon"), lax.axis_index("lat")
    west, east = lax.rem(lon + n_lon - 1, n_lon), lax.rem(lon + 1, n_lon)
    has_up, has_down = lat > 0, lat < n_lat - 1
    barrier = pltpu.get_barrier_semaphore()

    def greet(there_lon, there_lat):
        pl.semaphore_signal(barrier, inc=1, device_id={"lon": there_lon, "lat": there_lat}, device_id_type=MESH)

    sides = has_up.astype(jnp.int32) + has_down.astype(jnp.int32)
    for present, there_lat in ((has_up, lat - 1), (has_down, lat + 1)):
        @pl.when(present)
        def _():
            for there_lon in (west, east) if first else (lon, west, east):
                greet(there_lon, there_lat)

    if first:
        for k in range(1, n_lat):
            greet(lon, lax.rem(lat + k, n_lat))

        @pl.loop(1, n_lon)
        def _(k):
            greet(lax.rem(lon + k, n_lon), lat)

        greetings = 2 * sides + (n_lat - 1) + (n_lon - 1)
    else:
        greet(west, lat)
        greet(east, lat)
        greetings = 3 * sides + 2

    def remote(source, target, send, recv, there_lon, there_lat):
        return pltpu.make_async_remote_copy(
            src_ref=source, dst_ref=target, send_sem=send, recv_sem=recv,
            device_id={"lon": there_lon, "lat": there_lat}, device_id_type=MESH,
        )

    above, below = pl.ds(0, DEEP), pl.ds(rows + DEEP, DEEP)
    top, bottom, band = pl.ds(DEEP, DEEP), pl.ds(rows, DEEP), pl.ds(DEEP, rows)
    block = pl.ds(EDGE, cols)
    west_edge, east_edge = pl.ds(EDGE, DEEP), pl.ds(EDGE + cols - DEEP, DEEP)
    west_halo, east_halo = pl.ds(EDGE - DEEP, DEEP), pl.ds(EDGE + cols, DEEP)

    def exchange(kind):
        source_rows, target_rows, source_cols, target_cols, there_lon, there_lat = {
            "up_main": (top, below, block, block, lon, lat - 1),
            "up_west": (top, below, west_edge, east_halo, west, lat - 1),
            "up_east": (top, below, east_edge, west_halo, east, lat - 1),
            "down_main": (bottom, above, block, block, lon, lat + 1),
            "down_west": (bottom, above, west_edge, east_halo, west, lat + 1),
            "down_east": (bottom, above, east_edge, west_halo, east, lat + 1),
            "west": (band, band, west_edge, east_halo, west, lat),
            "east": (band, band, east_edge, west_halo, east, lat),
        }[kind]
        slot = KINDS.index(kind)
        return remote(
            main.at[source_rows, source_cols], main.at[target_rows, target_cols],
            send_sems.at[slot], recv_sems.at[slot], there_lon, there_lat,
        )

    def exchange_coef(kind):
        pair, slot = pl.ds(0, 2), KINDS.index(kind)
        source, target, there_lat = (top, below, lat - 1) if kind == "up_coef" else (bottom, above, lat + 1)
        return remote(coef.at[pair, source], coef.at[pair, target], send_sems.at[slot], recv_sems.at[slot], lon, there_lat)

    whole = fields // 8
    rest = fields - 8 * whole

    def turn_in(j):
        parts = [x_ref[pl.ds(j + rows * 8 * k, 8, stride=rows), :] for k in range(whole)]
        if rest:
            tail = x_ref[pl.ds(j + rows * 8 * whole, rest, stride=rows), :]
            parts.append(jnp.concatenate([tail, jnp.zeros((8 - rest, cols), jnp.float32)], axis=0))
        parts.append(jnp.zeros((cols - 8 * len(parts), cols), jnp.float32))
        main[j + DEEP, block] = jnp.concatenate(parts, axis=0).T

    def turn_out(j, plane):
        turned = plane.T
        for k in range(whole + (rest > 0)):
            size = 8 if k < whole else rest
            at = pl.ds(j + rows * 8 * k, size, stride=rows)
            value = turned[8 * k:8 * k + size]
            if not first:
                value = value + add_ref[at, :]
            out_ref[at, :] = value

    if first:
        row = lax.broadcasted_iota(jnp.int32, (rows, fields), 0)
        closed = jnp.logical_and(row == rows - 1, lat == n_lat - 1)
        blank = jnp.zeros((rows, cols), jnp.float32)
        for k, rates in enumerate((zonal_ref[...], jnp.where(closed, 0.0, merid_ref[...]))):
            coef[k, band] = blank
            coef[k, band, pl.ds(0, fields)] = rates

    for start in (0, rows - DEEP):
        @pl.loop(start, start + DEEP)
        def _(j):
            turn_in(j)

    pl.semaphore_wait(barrier, greetings)

    for present, way, at in ((has_up, "up", above), (has_down, "down", below)):
        @pl.when(present)
        def _():
            if first:
                exchange_coef(way + "_coef").start()
            exchange(way + "_main").start()
            exchange(way + "_west").start()
            exchange(way + "_east").start()

        @pl.when(jnp.logical_not(present))
        def _():
            main[at] = jnp.zeros((DEEP,) + main.shape[1:], jnp.float32)
            if first:
                coef[pl.ds(0, 2), at] = jnp.zeros((2, DEEP, cols), jnp.float32)

    @pl.loop(DEEP, rows - DEEP)
    def _(j):
        turn_in(j)

    for kind in ("west", "east"):
        exchange(kind).start()

    if first:
        pairs = ((value_ref, value_mid, value_out), (precision_ref, precision_mid, precision_out))

        def near(n, k):
            source, target, _ = pairs[n]
            there = lax.rem(lat + k, n_lat)
            return remote(source.at[:, there], target.at[lat], near_sems.at[0, n, k], near_sems.at[1, n, k], lon, there)

        def far(n, k):
            _, source, target = pairs[n]
            there = lax.rem(lon + k, n_lon)
            return remote(source.at[:, there], target.at[lon], far_sems.at[0, n, k], far_sems.at[1, n, k], there, lat)

        def stays(n, stage):
            source, middle, target = pairs[n]
            if stage == 0:
                return pltpu.make_async_copy(source.at[:, lat], middle.at[lat], own_sems.at[0, n])
            return pltpu.make_async_copy(middle.at[:, lon], target.at[lon], own_sems.at[1, n])

        for n in range(2):
            for k in range(1, n_lat):
                near(n, k).start()
            stays(n, 0).start()

        for present, way in ((has_up, "down_coef"), (has_down, "up_coef")):
            @pl.when(present)
            def _():
                exchange_coef(way).wait_recv()

        coef[2] = jnp.zeros((ext, cols), jnp.float32)
        for start in (1, 9, ext - 9):
            at = pl.ds(start, 8)
            coef[2, at] = 1.0 - 2.0 * coef[0, at] - coef[1, at] - coef[1, pl.ds(start - 1, 8)]
        coef_out[...] = coef[...]

    for kind in ("west", "east"):
        exchange(kind).wait_recv()
    for present, way in ((has_up, "down"), (has_down, "up")):
        @pl.when(present)
        def _():
            for kind in ("_main", "_west", "_east"):
                exchange(way + kind).wait_recv()

    def swept(source, p, starts):
        rate = lambda k, q: jnp.broadcast_to(coef[k, pl.ds(q, 1), :], (8, cols))
        c, z, n, s = rate(2, p), rate(0, p), rate(1, p), rate(1, p - 1)
        out = []
        for start in starts:
            at = pl.ds(start, 8)
            value = c * source[p, at, :] + z * (source[p, pl.ds(start - 1, 8), :] + source[p, pl.ds(start + 1, 8), :])
            out.append(value + n * source[p + 1, at, :] + s * source[p - 1, at, :])
        return out

    def sweep(source, target, t):
        starts = range(EDGE - DEEP + t, EDGE + cols + DEEP - t, 8)

        @pl.loop(t, ext - t)
        def _(p):
            for start, value in zip(starts, swept(source, p, starts)):
                target[p, pl.ds(start, 8), :] = value

    sweep(main, main2, 1)

    if first:
        for n in range(2):
            for k in range(1, n_lat):
                near(n, k).wait_recv()
            stays(n, 0).wait()

        @pl.loop(1, n_lon)
        def _(k):
            for n in range(2):
                far(n, k).start()

        for n in range(2):
            stays(n, 1).start()

    for kind in ("west", "east"):
        exchange(kind).wait_send()
    for present, way in ((has_up, "up"), (has_down, "down")):
        @pl.when(present)
        def _():
            for kind in ("_main", "_west", "_east"):
                exchange(way + kind).wait_send()

    sweep(main2, main, 2)
    sweep(main, main2, 3)
    if not first:
        addend.wait()

    @pl.loop(0, rows // 2)
    def _(i):
        for k in range(2):
            j = i * 2 + k
            turn_out(j, jnp.concatenate(swept(main2, j + DEEP, range(EDGE, EDGE + cols, 8)), axis=0))

    if first:
        for present, way in ((has_up, "up_coef"), (has_down, "down_coef")):
            @pl.when(present)
            def _():
                exchange_coef(way).wait_send()

        for n in range(2):
            for k in range(1, n_lat):
                near(n, k).wait_send()

        @pl.loop(1, n_lon)
        def _(k):
            for n in range(2):
                far(n, k).wait_recv()
                far(n, k).wait_send()

        for n in range(2):
            stays(n, 1).wait()


def root(field, operands, rows, first):
    cols = field.shape[1]
    ext = rows + 2 * DEEP
    vmem = pl.BlockSpec(memory_space=pltpu.VMEM)
    f32 = lambda *shape: jax.ShapeDtypeStruct(shape, jnp.float32)
    scratch = [pltpu.VMEM((ext, cols + 2 * EDGE, cols), jnp.float32)] * 2
    scratch += [pltpu.SemaphoreType.DMA((len(KINDS),))] * 2
    outs = [f32(*field.shape)]
    in_specs, out_specs = [vmem] * (1 + len(operands)), [vmem]
    if first:
        anywhere = [pl.BlockSpec(memory_space=pl.ANY)] * 2
        in_specs[3:] = anywhere
        out_specs += [vmem] + anywhere
        n_lon, n_lat = lax.axis_size("lon"), lax.axis_size("lat")
        outs += [f32(3, ext, cols)] + [f32(n_lon, n_lat, 1, cols)] * 2
        scratch = (
            [pltpu.VMEM((3, ext, cols), jnp.float32)]
            + [pltpu.VMEM((n_lat, n_lon, 1, cols), jnp.float32)] * 2
            + [pltpu.SemaphoreType.DMA((2, 2, n_lat)), pltpu.SemaphoreType.DMA((2, 2, n_lon)), pltpu.SemaphoreType.DMA((2, 2))]
            + scratch
        )
    else:
        in_specs[2] = pl.BlockSpec(memory_space=pl.ANY)
        scratch = [pltpu.VMEM(field.shape, jnp.float32), pltpu.SemaphoreType.DMA] + scratch
    return pl.pallas_call(
        functools.partial(root_kernel, first, rows),
        out_shape=outs,
        in_specs=in_specs,
        out_specs=out_specs,
        scratch_shapes=scratch,
        compiler_params=pltpu.CompilerParams(
            collective_id=0 if first else 1, has_side_effects=True, vmem_limit_bytes=60 * 2**20),
        name="root_first" if first else "root_second",
    )(field, *operands)


PAD = 8
NACC = 8
LANES = lax.GatherDimensionNumbers(
    offset_dims=(), collapsed_slice_dims=(1,), start_index_map=(1,),
    operand_batching_dims=(0,), start_indices_batching_dims=(0,))


def pick_lanes(value, index):
    return lax.gather(value, index[:, :, None], LANES, slice_sizes=(1, 1), mode="promise_in_bounds")


def obs_kernel(cnt_ref, tab_hbm, base_hbm, field_hbm, w_hbm, val_hbm, prec_hbm, inc_hbm, out_ref,
               base_ref, field_ref, w_ref, val_ref, prec_ref, in_sems,
               tab, stack, dense, plan, cidx, ridx, ridx_s, sem, windows, places, sources, *accs):
    rows = tab_hbm.shape[0]
    cells = 16 * 128
    lane = lax.broadcasted_iota(jnp.int32, (8, 128), 1)
    sub = lax.broadcasted_iota(jnp.int32, (8, 128), 0)
    zero = jnp.zeros((8, 128), jnp.float32)
    body = pl.ds(PAD, rows)
    loads = [
        pltpu.make_async_copy(source, target, in_sems.at[k])
        for k, (source, target) in enumerate((
            (base_hbm, base_ref), (field_hbm, field_ref), (w_hbm, w_ref), (val_hbm, val_ref), (prec_hbm, prec_ref),
            (tab_hbm, tab.at[body]),
        ))
    ]
    keep = pltpu.make_async_copy(tab.at[body], inc_hbm, in_sems.at[6])
    for load in loads:
        load.start()
    tab[pl.ds(0, 8), :] = zero
    tab[pl.ds(rows + PAD, 8), :] = zero
    for load in loads[:-1]:
        load.wait()

    @pl.loop(0, 16)
    def _(b):
        at = pl.multiple_of(b * 8, 8)
        part = pl.ds(at, 8)
        index = field_ref[part, :] * cells + base_ref[part, :]
        arrays = [w_ref[k, part, :] for k in range(4)]
        arrays += [val_ref[part, :], prec_ref[part, :], index.astype(jnp.float32)]
        for k, array in enumerate(arrays):
            stack[pl.ds(at * 8 + k, 8, stride=8), :] = array

    def compact(o, carry):
        start, kept = carry
        group = stack[pl.ds(pl.multiple_of(o * 8, 8), 8), :]
        shift = lax.bitwise_and(start, 127)
        row = lax.shift_right_logical(start, 7)
        rolled = pltpu.roll(group, shift, 1)
        merged = jnp.where(lane >= shift, rolled, kept)
        at = pl.multiple_of(row * 8, 8)
        dense[pl.ds(at, 8), :] = merged
        dense[pl.ds(at + 8, 8), :] = rolled
        after = start + cnt_ref[0, o]
        moved = lax.shift_right_logical(after, 7) > row
        return after, jnp.where(moved, rolled, merged)

    total, _ = lax.fori_loop(0, 128, compact, (jnp.int32(0), zero), unroll=32)
    chunks = lax.shift_right_logical(total + 127, 7)

    even = lax.bitwise_and(lane, 1) == 0

    def paired(low, high, add=0):
        after = pltpu.roll(high, 1, 1) + add
        return jnp.where(even, low, after), jnp.where(even, after, low)

    @pl.loop(0, 16)
    def _(b):
        at = pl.multiple_of(b * 8, 8)
        part = pl.ds(at, 8)
        arrays = [dense[pl.ds(at * 8 + k, 8, stride=8), :] for k in range(7)]
        live = (at + sub) * 128 + lane < total
        index = jnp.where(live, arrays[6].astype(jnp.int32), 0)
        ridx[part, :] = lax.shift_right_logical(index, 7) + PAD
        cols = lax.bitwise_and(index, 127)
        cidx[0, part, :], cidx[1, part, :] = paired(cols, cols, 1)
        cidx[2, part, :] = lane - cols
        for a in range(2):
            first_row, second_row = paired(arrays[2 * a], arrays[2 * a + 1])
            plan[a, part, :], plan[2 + a, part, :] = first_row, second_row
        precision = jnp.where(live, arrays[5], 0.0)
        value = jnp.where(live, arrays[4], 0.0)
        plan[4, part, :], plan[5, part, :] = value, precision
        plan[6, part, :], plan[7, part, :] = pltpu.roll(value, 1, 1), pltpu.roll(precision, 1, 1)

    copy = pltpu.make_async_copy(ridx, ridx_s, sem)
    copy.start()

    @pl.loop(0, (rows + 2 * PAD) // 16)
    def _(i):
        for acc in accs:
            for k in range(2):
                acc[pl.ds(pl.multiple_of(i * 16 + 8 * k, 8), 8), :] = zero

    copy.wait()
    loads[-1].wait()
    keep.start()

    quad = lax.shift_right_logical(sub, 1)
    first = lax.bitwise_and(sub, 1) == 0
    keys = (
        lax.shift_right_logical(lane, 1) - 16 * quad,
        lax.shift_right_logical(lax.bitwise_and(lane - 1, 127), 1) - 16 * quad,
    )

    def spread(row):
        return jnp.broadcast_to(row, (8, 128))

    def weights(d):
        line = pl.ds(d, 1)
        return [jnp.where(first, spread(plan[2 * par, line, :]), spread(plan[2 * par + 1, line, :])) for par in range(2)]

    def load_windows(d):
        row_at = ridx_s.at[d]
        for par in range(2):
            for g in range(16):
                merged = None
                for q in range(4):
                    r = row_at[2 * (g + 16 * q) + par]
                    value = tab[pl.ds(r - 2 * q, 8), :]
                    merged = value if q == 0 else jnp.where(sub >= 2 * q, value, merged)
                windows[16 * par + g] = merged

    def gather(d):
        sums = []
        for par in range(2):
            start = spread(cidx[par, pl.ds(d, 1), :])
            found = zero
            for g in range(16):
                found = jnp.where(keys[par] == g, pick_lanes(windows[16 * par + g], start), found)
            sums.append(found)
        return sums

    def compare(d, found):
        line = pl.ds(d, 1)
        weight = weights(d)
        sums = [spread(jnp.sum(found[par] * weight[par], axis=0, keepdims=True)) for par in range(2)]
        here = jnp.where(even, sums[0], sums[1])
        there = jnp.where(even, sums[1], sums[0])
        value, precision, value_w, precision_w = [spread(plan[k, line, :]) for k in range(4, 8)]
        misfit = precision * (here + pltpu.roll(there, 127, 1) - value)
        moved = precision_w * (pltpu.roll(here, 1, 1) + there - value_w)
        return (
            weight[0] * jnp.where(even, misfit, moved),
            weight[1] * jnp.where(even, moved, misfit),
        )

    lane_par = lax.bitwise_and(lane, 1)
    ones = jnp.ones((128, 128), jnp.bfloat16)

    def turn_lanes(d):
        turn = spread(cidx[2, pl.ds(d, 1), :]).astype(jnp.float32)
        picked = [
            jnp.where(jnp.logical_and(keys[par] == g, lane_par == par), turn, 0.0)
            for par in range(2) for g in range(16)
        ]
        picked = jnp.concatenate(picked, axis=0).astype(jnp.bfloat16)
        turns = jnp.dot(picked, ones, preferred_element_type=jnp.float32).astype(jnp.int32)
        for k in range(32):
            sources[k] = lax.bitwise_and(lane + turns[8 * k:8 * k + 8], 127)

    def place(amounts):
        for par in range(2):
            for g in range(16):
                masked = jnp.where(keys[par] == g, amounts[par], 0.0)
                places[16 * par + g] = pick_lanes(masked, sources[16 * par + g])

    def add_rows(d):
        row_at = ridx_s.at[d]
        for par in range(2):
            for g in range(16):
                placed = places[16 * par + g]
                for q in range(4):
                    r = row_at[2 * (g + 16 * q) + par]
                    acc = accs[(g % (len(accs) // 4)) * 4 + q]
                    at = pl.ds(r - 2 * q, 8)
                    acc[at, :] = acc[at, :] + jnp.where(quad == q, placed, 0.0)

    for k in range(32):
        windows[k] = zero
        places[k] = zero
        sources[k] = lane

    def step(d, carry):
        found_e, found_o, amounts_e, amounts_o = carry
        last = chunks - 1
        add_rows(jnp.clip(d - 4, 0, last))
        place((amounts_e, amounts_o))
        turn_lanes(jnp.clip(d - 2, 0, last))
        amounts = compare(jnp.clip(d - 2, 0, last), (found_e, found_o))
        found = gather(jnp.clip(d - 1, 0, last))
        load_windows(jnp.minimum(d, last))
        ready = d > 1
        return (*found, jnp.where(ready, amounts[0], 0.0), jnp.where(ready, amounts[1], 0.0))

    lax.fori_loop(0, chunks + 4, step, (zero,) * 4)

    @pl.loop(0, rows // 80)
    def _(i):
        for k in range(10):
            at = pl.multiple_of(i * 80 + 8 * k, 8)
            parts = [acc[pl.ds(at + PAD, 8), :] for acc in accs]
            while len(parts) > 1:
                parts = [a + b for a, b in zip(parts[::2], parts[1::2])]
            out_ref[pl.ds(at, 8), :] = parts[0]

    keep.wait()


def observe(table, count, base, field, weight, value, precision):
    rows, cols = table.shape
    vmem = pl.BlockSpec(memory_space=pltpu.VMEM)
    anywhere = pl.BlockSpec(memory_space=pl.ANY)
    smem = pl.BlockSpec(memory_space=pltpu.SMEM)
    return pl.pallas_call(
        obs_kernel,
        out_shape=[jax.ShapeDtypeStruct((rows, cols), jnp.float32)] * 2,
        in_specs=[smem] + [anywhere] * 6,
        out_specs=[anywhere, vmem],
        scratch_shapes=[
            pltpu.VMEM((128, 128), jnp.int32),
            pltpu.VMEM((128, 128), jnp.int32),
            pltpu.VMEM((4, 128, 128), jnp.float32),
            pltpu.VMEM((128, 128), jnp.float32),
            pltpu.VMEM((128, 128), jnp.float32),
            pltpu.SemaphoreType.DMA((7,)),
            pltpu.VMEM((rows + 2 * PAD, cols), jnp.float32),
            pltpu.VMEM((1024, 128), jnp.float32),
            pltpu.VMEM((129 * 8, 128), jnp.float32),
            pltpu.VMEM((8, 128, 128), jnp.float32),
            pltpu.VMEM((3, 128, 128), jnp.int32),
            pltpu.VMEM((128, 128), jnp.int32),
            pltpu.SMEM((128, 128), jnp.int32),
            pltpu.SemaphoreType.DMA,
            pltpu.VMEM((32, 8, 128), jnp.float32),
            pltpu.VMEM((32, 8, 128), jnp.float32),
            pltpu.VMEM((32, 8, 128), jnp.int32),
        ] + [pltpu.VMEM((rows + 2 * PAD, cols), jnp.float32)] * NACC,
        compiler_params=pltpu.CompilerParams(vmem_limit_bytes=60 * 2**20),
        name="observe",
    )(count, table, base, field, weight, value, precision)


def per_device(
    control,
    lon_coef,
    lat_coef,
    obs_base,
    obs_field,
    obs_weight,
    obs_count,
    obs_value,
    obs_precision,
):
    fields, band_rows, block_cols = control.shape
    owners, slots = obs_base.shape[1:]
    by_device = (lax.axis_size("lon"), lax.axis_size("lat"), 1, slots)
    lines = control.reshape(fields * band_rows, block_cols)
    increment, coefs, value, precision = root(
        lines,
        (lon_coef.T, lat_coef.T, obs_value.reshape(by_device), obs_precision.reshape(by_device)),
        band_rows,
        True,
    )
    increment, forcing = observe(
        increment,
        obs_count,
        obs_base[0],
        obs_field[0],
        obs_weight[:, 0],
        value.reshape(owners, slots),
        precision.reshape(owners, slots),
    )
    (gradient,) = root(forcing, (coefs, lines), band_rows, False)
    return (increment.reshape(control.shape), gradient.reshape(control.shape))


def solution(mesh):
    in_specs = (
        P(None, "lat", "lon"),
        P(None, "lat"),
        P(None, "lat"),
        P(("lon", "lat"), None, None),
        P(("lon", "lat"), None, None),
        P(None, ("lon", "lat"), None, None),
        P(("lon", "lat"), None),
        P(("lon", "lat"), None, None),
        P(("lon", "lat"), None, None),
    )
    out_specs = (P(None, "lat", "lon"), P(None, "lat", "lon"))
    return jax.shard_map(
        per_device, mesh=mesh, in_specs=in_specs, out_specs=out_specs, check_vma=False
    )
```

```python
import functools

import jax
import jax.numpy as jnp
from jax import lax
from jax.experimental import pallas as pl
from jax.experimental.pallas import tpu as pltpu
from jax.sharding import PartitionSpec as P

MESH = pl.DeviceIdType.MESH
DEEP = 4
EDGE = 8
KINDS = (
    "up_main", "up_west", "up_east", "down_main", "down_west", "down_east", "west", "east", "up_coef", "down_coef",
)


def root_kernel(first, rows, *refs):
    if first:
        (x_hbm, zonal_hbm, merid_hbm, value_ref, precision_ref, out_ref, coef_out, held_out, *scratch) = refs
        (x_ref, zonal_ref, merid_ref, in_sems, coef, held_mid, near_sems, far_sems, own_sems, *scratch) = scratch
        loads = [
            pltpu.make_async_copy(source, target, in_sems.at[k])
            for k, (source, target) in enumerate(((zonal_hbm, zonal_ref), (merid_hbm, merid_ref), (x_hbm, x_ref)))
        ]
        for load in loads:
            load.start()
    else:
        (x_ref, coef, add_hbm, out_ref, add_ref, add_sem, *scratch) = refs
        addend = pltpu.make_async_copy(add_hbm, add_ref, add_sem)
        addend.start()
    (main, main2, send_sems, recv_sems) = scratch
    cols = x_ref.shape[1]
    fields = x_ref.shape[0] // rows
    ext = rows + 2 * DEEP
    n_lon, n_lat = lax.axis_size("lon"), lax.axis_size("lat")
    lon, lat = lax.axis_index("lon"), lax.axis_index("lat")
    west, east = lax.rem(lon + n_lon - 1, n_lon), lax.rem(lon + 1, n_lon)
    has_up, has_down = lat > 0, lat < n_lat - 1
    barrier = pltpu.get_barrier_semaphore()

    def greet(there_lon, there_lat):
        pl.semaphore_signal(barrier, inc=1, device_id={"lon": there_lon, "lat": there_lat}, device_id_type=MESH)

    sides = has_up.astype(jnp.int32) + has_down.astype(jnp.int32)
    for present, there_lat in ((has_up, lat - 1), (has_down, lat + 1)):
        @pl.when(present)
        def _():
            for there_lon in (west, east) if first else (lon, west, east):
                greet(there_lon, there_lat)

    if first:
        for k in range(1, n_lat):
            greet(lon, lax.rem(lat + k, n_lat))

        @pl.loop(1, n_lon)
        def _(k):
            greet(lax.rem(lon + k, n_lon), lat)

        greetings = 2 * sides + (n_lat - 1) + (n_lon - 1)
    else:
        greet(west, lat)
        greet(east, lat)
        greetings = 3 * sides + 2

    def remote(source, target, send, recv, there_lon, there_lat):
        return pltpu.make_async_remote_copy(
            src_ref=source, dst_ref=target, send_sem=send, recv_sem=recv,
            device_id={"lon": there_lon, "lat": there_lat}, device_id_type=MESH,
        )

    above, below = pl.ds(0, DEEP), pl.ds(rows + DEEP, DEEP)
    top, bottom, band = pl.ds(DEEP, DEEP), pl.ds(rows, DEEP), pl.ds(DEEP, rows)
    block = pl.ds(EDGE, cols)
    west_edge, east_edge = pl.ds(EDGE, DEEP), pl.ds(EDGE + cols - DEEP, DEEP)
    west_halo, east_halo = pl.ds(EDGE - DEEP, DEEP), pl.ds(EDGE + cols, DEEP)

    def exchange(kind):
        source_rows, target_rows, source_cols, target_cols, there_lon, there_lat = {
            "up_main": (top, below, block, block, lon, lat - 1),
            "up_west": (top, below, west_edge, east_halo, west, lat - 1),
            "up_east": (top, below, east_edge, west_halo, east, lat - 1),
            "down_main": (bottom, above, block, block, lon, lat + 1),
            "down_west": (bottom, above, west_edge, east_halo, west, lat + 1),
            "down_east": (bottom, above, east_edge, west_halo, east, lat + 1),
            "west": (band, band, west_edge, east_halo, west, lat),
            "east": (band, band, east_edge, west_halo, east, lat),
        }[kind]
        slot = KINDS.index(kind)
        return remote(
            main.at[source_rows, source_cols], main.at[target_rows, target_cols],
            send_sems.at[slot], recv_sems.at[slot], there_lon, there_lat,
        )

    def exchange_coef(kind):
        pair, slot = pl.ds(0, 2), KINDS.index(kind)
        source, target, there_lat = (top, below, lat - 1) if kind == "up_coef" else (bottom, above, lat + 1)
        return remote(coef.at[pair, source], coef.at[pair, target], send_sems.at[slot], recv_sems.at[slot], lon, there_lat)

    whole = fields // 8
    rest = fields - 8 * whole

    def turn_in(j):
        parts = [x_ref[pl.ds(j + rows * 8 * k, 8, stride=rows), :] for k in range(whole)]
        if rest:
            tail = x_ref[pl.ds(j + rows * 8 * whole, rest, stride=rows), :]
            parts.append(jnp.concatenate([tail, jnp.zeros((8 - rest, cols), jnp.float32)], axis=0))
        parts.append(jnp.zeros((cols - 8 * len(parts), cols), jnp.float32))
        main[j + DEEP, block] = jnp.concatenate(parts, axis=0).T

    def turn_out(j, plane):
        turned = plane.T
        for k in range(whole + (rest > 0)):
            size = 8 if k < whole else rest
            at = pl.ds(j + rows * 8 * k, size, stride=rows)
            value = turned[8 * k:8 * k + size]
            if not first:
                value = value + add_ref[at, :]
            out_ref[at, :] = value

    if first:
        for load in loads:
            load.wait()
        row = lax.broadcasted_iota(jnp.int32, (rows, fields), 0)
        closed = jnp.logical_and(row == rows - 1, lat == n_lat - 1)
        blank = jnp.zeros((rows, cols), jnp.float32)
        for k, rates in enumerate((zonal_ref[...], jnp.where(closed, 0.0, merid_ref[...]))):
            coef[k, band] = blank
            coef[k, band, pl.ds(0, fields)] = rates

    for start in (0, rows - DEEP):
        @pl.loop(start, start + DEEP)
        def _(j):
            turn_in(j)

    if first:
        sent = (value_ref, precision_ref)

        def near(n, k):
            there = lax.rem(lat + k, n_lat)
            return remote(
                sent[n].at[:, there], held_mid.at[lat, :, pl.ds(n, 1)],
                near_sems.at[0, n, k], near_sems.at[1, n, k], lon, there,
            )

        def near_own(n):
            return pltpu.make_async_copy(sent[n].at[:, lat], held_mid.at[lat, :, pl.ds(n, 1)], own_sems.at[n])

        def far(k):
            there = lax.rem(lon + k, n_lon)
            return remote(held_mid.at[:, there], held_out.at[lon], far_sems.at[0, k], far_sems.at[1, k], there, lat)

        def far_own():
            return pltpu.make_async_copy(held_mid.at[:, lon], held_out.at[lon], own_sems.at[2])

    pl.semaphore_wait(barrier, greetings)

    if first:
        for n in range(2):
            for k in range(1, n_lat):
                near(n, k).start()
            near_own(n).start()

    for present, way, at in ((has_up, "up", above), (has_down, "down", below)):
        @pl.when(present)
        def _():
            if first:
                exchange_coef(way + "_coef").start()
            exchange(way + "_main").start()
            exchange(way + "_west").start()
            exchange(way + "_east").start()

        @pl.when(jnp.logical_not(present))
        def _():
            main[at] = jnp.zeros((DEEP,) + main.shape[1:], jnp.float32)
            if first:
                coef[pl.ds(0, 2), at] = jnp.zeros((2, DEEP, cols), jnp.float32)

    @pl.loop(DEEP, rows - DEEP)
    def _(j):
        turn_in(j)

    for kind in ("west", "east"):
        exchange(kind).start()

    if first:
        for n in range(2):
            for k in range(1, n_lat):
                near(n, k).wait_recv()
            near_own(n).wait()

        @pl.loop(1, n_lon)
        def _(k):
            far(k).start()

        far_own().start()

        for present, way in ((has_up, "down_coef"), (has_down, "up_coef")):
            @pl.when(present)
            def _():
                exchange_coef(way).wait_recv()

        coef[2] = jnp.zeros((ext, cols), jnp.float32)
        for start in (1, 9, ext - 9):
            at = pl.ds(start, 8)
            coef[2, at] = 1.0 - 2.0 * coef[0, at] - coef[1, at] - coef[1, pl.ds(start - 1, 8)]
        coef_out[...] = coef[...]

    for kind in ("west", "east"):
        exchange(kind).wait_recv()
    for present, way in ((has_up, "down"), (has_down, "up")):
        @pl.when(present)
        def _():
            for kind in ("_main", "_west", "_east"):
                exchange(way + kind).wait_recv()

    def swept(source, p, starts):
        rate = lambda k, q: jnp.broadcast_to(coef[k, pl.ds(q, 1), :], (8, cols))
        c, z, n, s = rate(2, p), rate(0, p), rate(1, p), rate(1, p - 1)
        out = []
        for start in starts:
            at = pl.ds(start, 8)
            value = c * source[p, at, :] + z * (source[p, pl.ds(start - 1, 8), :] + source[p, pl.ds(start + 1, 8), :])
            out.append(value + n * source[p + 1, at, :] + s * source[p - 1, at, :])
        return out

    def sweep(source, target, t):
        starts = range(EDGE - DEEP + t, EDGE + cols + DEEP - t, 8)

        @pl.loop(t, ext - t)
        def _(p):
            for start, value in zip(starts, swept(source, p, starts)):
                target[p, pl.ds(start, 8), :] = value

    sweep(main, main2, 1)

    for kind in ("west", "east"):
        exchange(kind).wait_send()
    for present, way in ((has_up, "up"), (has_down, "down")):
        @pl.when(present)
        def _():
            for kind in ("_main", "_west", "_east"):
                exchange(way + kind).wait_send()

    sweep(main2, main, 2)
    sweep(main, main2, 3)
    if not first:
        addend.wait()

    @pl.loop(0, rows // 2)
    def _(i):
        for k in range(2):
            j = i * 2 + k
            turn_out(j, jnp.concatenate(swept(main2, j + DEEP, range(EDGE, EDGE + cols, 8)), axis=0))

    if first:
        for present, way in ((has_up, "up_coef"), (has_down, "down_coef")):
            @pl.when(present)
            def _():
                exchange_coef(way).wait_send()

        for n in range(2):
            for k in range(1, n_lat):
                near(n, k).wait_send()

        @pl.loop(1, n_lon)
        def _(k):
            far(k).wait_recv()
            far(k).wait_send()

        far_own().wait()


def root(field, operands, rows, first):
    cols = field.shape[1]
    ext = rows + 2 * DEEP
    vmem = pl.BlockSpec(memory_space=pltpu.VMEM)
    f32 = lambda *shape: jax.ShapeDtypeStruct(shape, jnp.float32)
    scratch = [pltpu.VMEM((ext, cols + 2 * EDGE, cols), jnp.float32)] * 2
    scratch += [pltpu.SemaphoreType.DMA((len(KINDS),))] * 2
    outs = [f32(*field.shape)]
    far_memory = pl.BlockSpec(memory_space=pltpu.HBM)
    in_specs, out_specs = [vmem] * (1 + len(operands)), [vmem]
    if first:
        in_specs = [far_memory] * 5
        out_specs += [vmem, far_memory]
        n_lon, n_lat = lax.axis_size("lon"), lax.axis_size("lat")
        outs += [f32(3, ext, cols)] + [f32(n_lon, n_lat, 2, cols)]
        scratch = (
            [pltpu.VMEM(field.shape, jnp.float32)]
            + [pltpu.VMEM(operands[0].shape, jnp.float32)] * 2
            + [pltpu.SemaphoreType.DMA((3,))]
            + [pltpu.VMEM((3, ext, cols), jnp.float32)]
            + [pltpu.VMEM((n_lat, n_lon, 2, cols), jnp.float32)]
            + [pltpu.SemaphoreType.DMA((2, 2, n_lat)), pltpu.SemaphoreType.DMA((2, n_lon)), pltpu.SemaphoreType.DMA((3,))]
            + scratch
        )
    else:
        in_specs[2] = far_memory
        scratch = [pltpu.VMEM(field.shape, jnp.float32), pltpu.SemaphoreType.DMA] + scratch
    return pl.pallas_call(
        functools.partial(root_kernel, first, rows),
        out_shape=outs,
        in_specs=in_specs,
        out_specs=out_specs,
        scratch_shapes=scratch,
        compiler_params=pltpu.CompilerParams(
            collective_id=0 if first else 1, has_side_effects=True, vmem_limit_bytes=(60 if first else 16) * 2**20),
        name="root_first" if first else "root_second",
    )(field, *operands)


PAD = 8
NACC = 16
LANES = lax.GatherDimensionNumbers(
    offset_dims=(), collapsed_slice_dims=(1,), start_index_map=(1,),
    operand_batching_dims=(0,), start_indices_batching_dims=(0,))


def pick_lanes(value, index):
    return lax.gather(value, index[:, :, None], LANES, slice_sizes=(1, 1), mode="promise_in_bounds")


def obs_kernel(cnt_ref, tab_hbm, base_hbm, field_hbm, w_hbm, held_hbm, inc_hbm, out_ref,
               base_ref, field_ref, in_sems,
               tab, stack, dense, plan, cidx, ridx, ridx_s, sem, windows, places, sources, *accs):
    rows = tab_hbm.shape[0]
    cells = 16 * 128
    lane = lax.broadcasted_iota(jnp.int32, (8, 128), 1)
    sub = lax.broadcasted_iota(jnp.int32, (8, 128), 0)
    zero = jnp.zeros((8, 128), jnp.float32)
    body = pl.ds(PAD, rows)
    loads = [
        pltpu.make_async_copy(source, target, in_sems.at[k])
        for k, (source, target) in enumerate((
            (base_hbm, base_ref), (field_hbm, field_ref), (held_hbm, stack.at[:, pl.ds(4, 2)]),
            *((w_hbm.at[k], stack.at[:, pl.ds(k, 1)]) for k in range(4)), (tab_hbm, tab.at[body]),
        ))
    ]
    keep = pltpu.make_async_copy(tab.at[body], inc_hbm, in_sems.at[8])
    for load in loads:
        load.start()
    tab[pl.ds(0, 8), :] = zero
    tab[pl.ds(rows + PAD, 8), :] = zero
    for load in loads[:2]:
        load.wait()

    @pl.loop(0, 4)
    def _(b):
        for k in range(4):
            at = pl.multiple_of(b * 32 + 8 * k, 8)
            index = field_ref[pl.ds(at, 8), :] * cells + base_ref[pl.ds(at, 8), :]
            stack[pl.ds(at, 8), 6, :] = index.astype(jnp.float32)

    for load in loads[2:-1]:
        load.wait()

    def compact(o, carry):
        start, kept = carry
        group = stack[o]
        shift = lax.bitwise_and(start, 127)
        row = lax.shift_right_logical(start, 7)
        rolled = pltpu.roll(group, shift, 1)
        merged = jnp.where(lane >= shift, rolled, kept)
        at = pl.multiple_of(row * 8, 8)
        dense[pl.ds(at, 8), :] = merged
        dense[pl.ds(at + 8, 8), :] = rolled
        after = start + cnt_ref[0, o]
        moved = lax.shift_right_logical(after, 7) > row
        return after, jnp.where(moved, rolled, merged)

    total, _ = lax.fori_loop(0, 128, compact, (jnp.int32(0), zero), unroll=32)
    chunks = lax.shift_right_logical(total + 127, 7)

    even = lax.bitwise_and(lane, 1) == 0

    def paired(low, high, add=0):
        after = pltpu.roll(high, 1, 1) + add
        return jnp.where(even, low, after), jnp.where(even, after, low)

    def plan_chunks(at):
        at = pl.multiple_of(at, 8)
        part = pl.ds(at, 8)
        arrays = [dense[pl.ds(at * 8 + k, 8, stride=8), :] for k in range(7)]
        live = (at + sub) * 128 + lane < total
        index = jnp.where(live, arrays[6].astype(jnp.int32), 0)
        ridx[part, :] = lax.shift_right_logical(index, 7) + PAD
        cols = lax.bitwise_and(index, 127)
        cidx[0, part, :], cidx[1, part, :] = paired(cols, cols, 1)
        cidx[2, part, :] = lane - cols
        for a in range(2):
            first_row, second_row = paired(arrays[2 * a], arrays[2 * a + 1])
            plan[a, part, :], plan[2 + a, part, :] = first_row, second_row
        precision = jnp.where(live, arrays[5], 0.0)
        value = jnp.where(live, arrays[4], 0.0)
        plan[4, part, :], plan[5, part, :] = value, precision
        plan[6, part, :], plan[7, part, :] = pltpu.roll(value, 1, 1), pltpu.roll(precision, 1, 1)

    @pl.loop(0, 4)
    def _(b):
        for k in range(4):
            plan_chunks(b * 32 + 8 * k)

    copy = pltpu.make_async_copy(ridx, ridx_s, sem)
    copy.start()

    @pl.loop(0, (rows + 2 * PAD) // 16)
    def _(i):
        for acc in accs:
            for k in range(2):
                acc[pl.ds(pl.multiple_of(i * 16 + 8 * k, 8), 8), :] = zero

    copy.wait()
    loads[-1].wait()
    keep.start()

    quad = lax.shift_right_logical(sub, 1)
    first = lax.bitwise_and(sub, 1) == 0
    keys = (
        lax.shift_right_logical(lane, 1) - 16 * quad,
        lax.shift_right_logical(lax.bitwise_and(lane - 1, 127), 1) - 16 * quad,
    )

    def spread(row):
        return jnp.broadcast_to(row, (8, 128))

    def weights(d):
        line = pl.ds(d, 1)
        return [jnp.where(first, spread(plan[2 * par, line, :]), spread(plan[2 * par + 1, line, :])) for par in range(2)]

    def load_windows(d):
        row_at = ridx_s.at[d]
        for par in range(2):
            for g in range(16):
                merged = None
                for q in range(4):
                    r = row_at[2 * (g + 16 * q) + par]
                    value = tab[pl.ds(r - 2 * q, 8), :]
                    merged = value if q == 0 else jnp.where(sub >= 2 * q, value, merged)
                windows[16 * par + g] = merged

    def gather(d):
        sums = []
        for par in range(2):
            start = spread(cidx[par, pl.ds(d, 1), :])
            found = zero
            for g in range(16):
                found = jnp.where(keys[par] == g, pick_lanes(windows[16 * par + g], start), found)
            sums.append(found)
        return sums

    def compare(d, found):
        line = pl.ds(d, 1)
        weight = weights(d)
        sums = [spread(jnp.sum(found[par] * weight[par], axis=0, keepdims=True)) for par in range(2)]
        here = jnp.where(even, sums[0], sums[1])
        there = jnp.where(even, sums[1], sums[0])
        value, precision, value_w, precision_w = [spread(plan[k, line, :]) for k in range(4, 8)]
        misfit = precision * (here + pltpu.roll(there, 127, 1) - value)
        moved = precision_w * (pltpu.roll(here, 1, 1) + there - value_w)
        return (
            weight[0] * jnp.where(even, misfit, moved),
            weight[1] * jnp.where(even, moved, misfit),
        )

    lane_par = lax.bitwise_and(lane, 1)
    ones = jnp.ones((128, 128), jnp.bfloat16)

    def turn_lanes(d):
        turn = spread(cidx[2, pl.ds(d, 1), :]).astype(jnp.float32)
        picked = [
            jnp.where(jnp.logical_and(keys[par] == g, lane_par == par), turn, 0.0)
            for par in range(2) for g in range(16)
        ]
        picked = jnp.concatenate(picked, axis=0).astype(jnp.bfloat16)
        turns = jnp.dot(picked, ones, preferred_element_type=jnp.float32).astype(jnp.int32)
        for k in range(32):
            sources[k] = lax.bitwise_and(lane + turns[8 * k:8 * k + 8], 127)

    def place(amounts):
        for par in range(2):
            for g in range(16):
                masked = jnp.where(keys[par] == g, amounts[par], 0.0)
                places[16 * par + g] = pick_lanes(masked, sources[16 * par + g])

    def add_rows(d):
        row_at = ridx_s.at[d]
        for par in range(2):
            for g in range(16):
                placed = places[16 * par + g]
                for q in range(4):
                    r = row_at[2 * (g + 16 * q) + par]
                    acc = accs[(g % (len(accs) // 4)) * 4 + q]
                    at = pl.ds(r - 2 * q, 8)
                    acc[at, :] = acc[at, :] + jnp.where(quad == q, placed, 0.0)

    for k in range(32):
        windows[k] = zero
        places[k] = zero
        sources[k] = lane

    def step(d, carry):
        found_e, found_o, amounts_e, amounts_o = carry
        last = jnp.maximum(chunks - 1, 0)
        add_rows(jnp.clip(d - 4, 0, last))
        place((amounts_e, amounts_o))
        turn_lanes(jnp.clip(d - 2, 0, last))
        amounts = compare(jnp.clip(d - 2, 0, last), (found_e, found_o))
        found = gather(jnp.clip(d - 1, 0, last))
        load_windows(jnp.minimum(d, last))
        ready = d > 1
        return (*found, jnp.where(ready, amounts[0], 0.0), jnp.where(ready, amounts[1], 0.0))

    lax.fori_loop(0, chunks + 4, step, (zero,) * 4)

    @pl.loop(0, rows // 80)
    def _(i):
        for k in range(10):
            at = pl.multiple_of(i * 80 + 8 * k, 8)
            parts = [acc[pl.ds(at + PAD, 8), :] for acc in accs]
            while len(parts) > 1:
                parts = [a + b for a, b in zip(parts[::2], parts[1::2])]
            out_ref[pl.ds(at, 8), :] = parts[0]

    keep.wait()


def observe(table, count, base, field, weight, held):
    rows, cols = table.shape
    vmem = pl.BlockSpec(memory_space=pltpu.VMEM)
    anywhere = pl.BlockSpec(memory_space=pl.ANY)
    far_memory = pl.BlockSpec(memory_space=pltpu.HBM)
    smem = pl.BlockSpec(memory_space=pltpu.SMEM)
    return pl.pallas_call(
        obs_kernel,
        out_shape=[jax.ShapeDtypeStruct((rows, cols), jnp.float32)] * 2,
        in_specs=[smem, anywhere] + [far_memory] * 4,
        out_specs=[far_memory, vmem],
        scratch_shapes=[
            pltpu.VMEM((128, 128), jnp.int32),
            pltpu.VMEM((128, 128), jnp.int32),
            pltpu.SemaphoreType.DMA((9,)),
            pltpu.VMEM((rows + 2 * PAD, cols), jnp.float32),
            pltpu.VMEM((128, 8, 128), jnp.float32),
            pltpu.VMEM((129 * 8, 128), jnp.float32),
            pltpu.VMEM((8, 128, 128), jnp.float32),
            pltpu.VMEM((3, 128, 128), jnp.int32),
            pltpu.VMEM((128, 128), jnp.int32),
            pltpu.SMEM((128, 128), jnp.int32),
            pltpu.SemaphoreType.DMA,
            pltpu.VMEM((32, 8, 128), jnp.float32),
            pltpu.VMEM((32, 8, 128), jnp.float32),
            pltpu.VMEM((32, 8, 128), jnp.int32),
        ] + [pltpu.VMEM((rows + 2 * PAD, cols), jnp.float32)] * NACC,
        compiler_params=pltpu.CompilerParams(vmem_limit_bytes=30 * 2**20),
        name="observe",
    )(count, table, base, field, weight, held)


def per_device(
    control,
    lon_coef,
    lat_coef,
    obs_base,
    obs_field,
    obs_weight,
    obs_count,
    obs_value,
    obs_precision,
):
    fields, band_rows, block_cols = control.shape
    owners, slots = obs_base.shape[1:]
    by_device = (lax.axis_size("lon"), lax.axis_size("lat"), 1, slots)
    lines = control.reshape(fields * band_rows, block_cols)
    increment, coefs, held = root(
        lines,
        (lon_coef.T, lat_coef.T, obs_value.reshape(by_device), obs_precision.reshape(by_device)),
        band_rows,
        True,
    )
    increment, forcing = observe(
        increment,
        obs_count,
        obs_base[0],
        obs_field[0],
        obs_weight.reshape(obs_weight.shape[0], owners, 1, slots),
        held.reshape(owners, 2, slots),
    )
    (gradient,) = root(forcing, (coefs, lines), band_rows, False)
    return (increment.reshape(control.shape), gradient.reshape(control.shape))


def solution(mesh):
    in_specs = (
        P(None, "lat", "lon"),
        P(None, "lat"),
        P(None, "lat"),
        P(("lon", "lat"), None, None),
        P(("lon", "lat"), None, None),
        P(None, ("lon", "lat"), None, None),
        P(("lon", "lat"), None),
        P(("lon", "lat"), None, None),
        P(("lon", "lat"), None, None),
    )
    out_specs = (P(None, "lat", "lon"), P(None, "lat", "lon"))
    return jax.shard_map(
        per_device, mesh=mesh, in_specs=in_specs, out_specs=out_specs, check_vma=False
    )
```

```python
import functools

import jax
import jax.numpy as jnp
from jax import lax
from jax.experimental import pallas as pl
from jax.experimental.pallas import tpu as pltpu
from jax.sharding import PartitionSpec as P

MESH = pl.DeviceIdType.MESH
DEEP = 4
EDGE = 8
KINDS = (
    "up_main", "up_west", "up_east", "down_main", "down_west", "down_east", "west", "east", "up_coef", "down_coef",
)


def root_kernel(first, rows, *refs):
    if first:
        (x_hbm, zonal_hbm, merid_hbm, value_ref, precision_ref, out_ref, coef_out, held_out, *scratch) = refs
        (x_ref, zonal_ref, merid_ref, in_sems, coef, held_mid, near_sems, far_sems, own_sems, *scratch) = scratch
        loads = [
            pltpu.make_async_copy(source, target, in_sems.at[k])
            for k, (source, target) in enumerate(((zonal_hbm, zonal_ref), (merid_hbm, merid_ref), (x_hbm, x_ref)))
        ]
        for load in loads:
            load.start()
    else:
        (x_ref, coef, add_hbm, out_ref, add_ref, add_sem, *scratch) = refs
        addend = pltpu.make_async_copy(add_hbm, add_ref, add_sem)
        addend.start()
    (main, main2, send_sems, recv_sems) = scratch
    cols = x_ref.shape[1]
    fields = x_ref.shape[0] // rows
    ext = rows + 2 * DEEP
    n_lon, n_lat = lax.axis_size("lon"), lax.axis_size("lat")
    lon, lat = lax.axis_index("lon"), lax.axis_index("lat")
    west, east = lax.rem(lon + n_lon - 1, n_lon), lax.rem(lon + 1, n_lon)
    has_up, has_down = lat > 0, lat < n_lat - 1
    barrier = pltpu.get_barrier_semaphore()

    def greet(there_lon, there_lat):
        pl.semaphore_signal(barrier, inc=1, device_id={"lon": there_lon, "lat": there_lat}, device_id_type=MESH)

    sides = has_up.astype(jnp.int32) + has_down.astype(jnp.int32)
    for present, there_lat in ((has_up, lat - 1), (has_down, lat + 1)):
        @pl.when(present)
        def _():
            for there_lon in (west, east) if first else (lon, west, east):
                greet(there_lon, there_lat)

    if first:
        for k in range(1, n_lat):
            greet(lon, lax.rem(lat + k, n_lat))

        @pl.loop(1, n_lon)
        def _(k):
            greet(lax.rem(lon + k, n_lon), lat)

        greetings = 2 * sides + (n_lat - 1) + (n_lon - 1)
    else:
        greet(west, lat)
        greet(east, lat)
        greetings = 3 * sides + 2

    def remote(source, target, send, recv, there_lon, there_lat):
        return pltpu.make_async_remote_copy(
            src_ref=source, dst_ref=target, send_sem=send, recv_sem=recv,
            device_id={"lon": there_lon, "lat": there_lat}, device_id_type=MESH,
        )

    above, below = pl.ds(0, DEEP), pl.ds(rows + DEEP, DEEP)
    top, bottom, band = pl.ds(DEEP, DEEP), pl.ds(rows, DEEP), pl.ds(DEEP, rows)
    block = pl.ds(EDGE, cols)
    west_edge, east_edge = pl.ds(EDGE, DEEP), pl.ds(EDGE + cols - DEEP, DEEP)
    west_halo, east_halo = pl.ds(EDGE - DEEP, DEEP), pl.ds(EDGE + cols, DEEP)

    def exchange(kind):
        source_rows, target_rows, source_cols, target_cols, there_lon, there_lat = {
            "up_main": (top, below, block, block, lon, lat - 1),
            "up_west": (top, below, west_edge, east_halo, west, lat - 1),
            "up_east": (top, below, east_edge, west_halo, east, lat - 1),
            "down_main": (bottom, above, block, block, lon, lat + 1),
            "down_west": (bottom, above, west_edge, east_halo, west, lat + 1),
            "down_east": (bottom, above, east_edge, west_halo, east, lat + 1),
            "west": (band, band, west_edge, east_halo, west, lat),
            "east": (band, band, east_edge, west_halo, east, lat),
        }[kind]
        slot = KINDS.index(kind)
        return remote(
            main.at[source_rows, source_cols], main.at[target_rows, target_cols],
            send_sems.at[slot], recv_sems.at[slot], there_lon, there_lat,
        )

    def exchange_coef(kind):
        pair, slot = pl.ds(0, 2), KINDS.index(kind)
        source, target, there_lat = (top, below, lat - 1) if kind == "up_coef" else (bottom, above, lat + 1)
        return remote(coef.at[pair, source], coef.at[pair, target], send_sems.at[slot], recv_sems.at[slot], lon, there_lat)

    whole = fields // 8
    rest = fields - 8 * whole

    def turn_in(j):
        parts = [x_ref[pl.ds(j + rows * 8 * k, 8, stride=rows), :] for k in range(whole)]
        if rest:
            tail = x_ref[pl.ds(j + rows * 8 * whole, rest, stride=rows), :]
            parts.append(jnp.concatenate([tail, jnp.zeros((8 - rest, cols), jnp.float32)], axis=0))
        parts.append(jnp.zeros((cols - 8 * len(parts), cols), jnp.float32))
        main[j + DEEP, block] = jnp.concatenate(parts, axis=0).T

    def turn_out(j, plane):
        turned = plane.T
        for k in range(whole + (rest > 0)):
            size = 8 if k < whole else rest
            at = pl.ds(j + rows * 8 * k, size, stride=rows)
            value = turned[8 * k:8 * k + size]
            if not first:
                value = value + add_ref[at, :]
            out_ref[at, :] = value

    if first:
        for load in loads:
            load.wait()
        row = lax.broadcasted_iota(jnp.int32, (rows, fields), 0)
        closed = jnp.logical_and(row == rows - 1, lat == n_lat - 1)
        blank = jnp.zeros((rows, cols), jnp.float32)
        for k, rates in enumerate((zonal_ref[...], jnp.where(closed, 0.0, merid_ref[...]))):
            coef[k, band] = blank
            coef[k, band, pl.ds(0, fields)] = rates

    for start in (0, rows - DEEP):
        @pl.loop(start, start + DEEP)
        def _(j):
            turn_in(j)

    if first:
        sent = (value_ref, precision_ref)

        def near(n, k):
            there = lax.rem(lat + k, n_lat)
            return remote(
                sent[n].at[:, there], held_mid.at[lat, :, pl.ds(n, 1)],
                near_sems.at[0, n, k], near_sems.at[1, n, k], lon, there,
            )

        def near_own(n):
            return pltpu.make_async_copy(sent[n].at[:, lat], held_mid.at[lat, :, pl.ds(n, 1)], own_sems.at[n])

        def far(k):
            there = lax.rem(lon + k, n_lon)
            return remote(held_mid.at[:, there], held_out.at[lon], far_sems.at[0, k], far_sems.at[1, k], there, lat)

        def far_own():
            return pltpu.make_async_copy(held_mid.at[:, lon], held_out.at[lon], own_sems.at[2])

    pl.semaphore_wait(barrier, greetings)

    if first:
        for n in range(2):
            for k in range(1, n_lat):
                near(n, k).start()
            near_own(n).start()

    for present, way, at in ((has_up, "up", above), (has_down, "down", below)):
        @pl.when(present)
        def _():
            if first:
                exchange_coef(way + "_coef").start()
            exchange(way + "_main").start()
            exchange(way + "_west").start()
            exchange(way + "_east").start()

        @pl.when(jnp.logical_not(present))
        def _():
            main[at] = jnp.zeros((DEEP,) + main.shape[1:], jnp.float32)
            if first:
                coef[pl.ds(0, 2), at] = jnp.zeros((2, DEEP, cols), jnp.float32)

    @pl.loop(DEEP, rows - DEEP)
    def _(j):
        turn_in(j)

    for kind in ("west", "east"):
        exchange(kind).start()

    if first:
        for n in range(2):
            for k in range(1, n_lat):
                near(n, k).wait_recv()
            near_own(n).wait()

        @pl.loop(1, n_lon)
        def _(k):
            far(k).start()

        far_own().start()

        for present, way in ((has_up, "down_coef"), (has_down, "up_coef")):
            @pl.when(present)
            def _():
                exchange_coef(way).wait_recv()

        coef[2] = jnp.zeros((ext, cols), jnp.float32)
        for start in (1, 9, ext - 9):
            at = pl.ds(start, 8)
            coef[2, at] = 1.0 - 2.0 * coef[0, at] - coef[1, at] - coef[1, pl.ds(start - 1, 8)]
        coef_out[...] = coef[...]

    for kind in ("west", "east"):
        exchange(kind).wait_recv()
    for present, way in ((has_up, "down"), (has_down, "up")):
        @pl.when(present)
        def _():
            for kind in ("_main", "_west", "_east"):
                exchange(way + kind).wait_recv()

    def swept(source, p, starts):
        rate = lambda k, q: jnp.broadcast_to(coef[k, pl.ds(q, 1), :], (8, cols))
        c, z, n, s = rate(2, p), rate(0, p), rate(1, p), rate(1, p - 1)
        out = []
        for start in starts:
            at = pl.ds(start, 8)
            value = c * source[p, at, :] + z * (source[p, pl.ds(start - 1, 8), :] + source[p, pl.ds(start + 1, 8), :])
            out.append(value + n * source[p + 1, at, :] + s * source[p - 1, at, :])
        return out

    def sweep(source, target, t):
        starts = range(EDGE - DEEP + t, EDGE + cols + DEEP - t, 8)

        @pl.loop(t, ext - t)
        def _(p):
            for start, value in zip(starts, swept(source, p, starts)):
                target[p, pl.ds(start, 8), :] = value

    sweep(main, main2, 1)

    for kind in ("west", "east"):
        exchange(kind).wait_send()
    for present, way in ((has_up, "up"), (has_down, "down")):
        @pl.when(present)
        def _():
            for kind in ("_main", "_west", "_east"):
                exchange(way + kind).wait_send()

    sweep(main2, main, 2)
    sweep(main, main2, 3)
    if not first:
        addend.wait()

    @pl.loop(0, rows // 2)
    def _(i):
        for k in range(2):
            j = i * 2 + k
            turn_out(j, jnp.concatenate(swept(main2, j + DEEP, range(EDGE, EDGE + cols, 8)), axis=0))

    if first:
        for present, way in ((has_up, "up_coef"), (has_down, "down_coef")):
            @pl.when(present)
            def _():
                exchange_coef(way).wait_send()

        for n in range(2):
            for k in range(1, n_lat):
                near(n, k).wait_send()

        @pl.loop(1, n_lon)
        def _(k):
            far(k).wait_recv()
            far(k).wait_send()

        far_own().wait()


def root(field, operands, rows, first):
    cols = field.shape[1]
    ext = rows + 2 * DEEP
    vmem = pl.BlockSpec(memory_space=pltpu.VMEM)
    f32 = lambda *shape: jax.ShapeDtypeStruct(shape, jnp.float32)
    scratch = [pltpu.VMEM((ext, cols + 2 * EDGE, cols), jnp.float32)] * 2
    scratch += [pltpu.SemaphoreType.DMA((len(KINDS),))] * 2
    outs = [f32(*field.shape)]
    far_memory = pl.BlockSpec(memory_space=pltpu.HBM)
    in_specs, out_specs = [vmem] * (1 + len(operands)), [vmem]
    if first:
        in_specs = [far_memory] * 5
        out_specs += [vmem, far_memory]
        n_lon, n_lat = lax.axis_size("lon"), lax.axis_size("lat")
        outs += [f32(3, ext, cols)] + [f32(n_lon, n_lat, 2, cols)]
        scratch = (
            [pltpu.VMEM(field.shape, jnp.float32)]
            + [pltpu.VMEM(operands[0].shape, jnp.float32)] * 2
            + [pltpu.SemaphoreType.DMA((3,))]
            + [pltpu.VMEM((3, ext, cols), jnp.float32)]
            + [pltpu.VMEM((n_lat, n_lon, 2, cols), jnp.float32)]
            + [pltpu.SemaphoreType.DMA((2, 2, n_lat)), pltpu.SemaphoreType.DMA((2, n_lon)), pltpu.SemaphoreType.DMA((3,))]
            + scratch
        )
    else:
        in_specs[2] = far_memory
        scratch = [pltpu.VMEM(field.shape, jnp.float32), pltpu.SemaphoreType.DMA] + scratch
    return pl.pallas_call(
        functools.partial(root_kernel, first, rows),
        out_shape=outs,
        in_specs=in_specs,
        out_specs=out_specs,
        scratch_shapes=scratch,
        compiler_params=pltpu.CompilerParams(
            collective_id=0 if first else 1, has_side_effects=True, vmem_limit_bytes=(60 if first else 16) * 2**20),
        name="root_first" if first else "root_second",
    )(field, *operands)


PAD = 8
NACC = 16
LANES = lax.GatherDimensionNumbers(
    offset_dims=(), collapsed_slice_dims=(1,), start_index_map=(1,),
    operand_batching_dims=(0,), start_indices_batching_dims=(0,))


def pick_lanes(value, index):
    return lax.gather(value, index[:, :, None], LANES, slice_sizes=(1, 1), mode="promise_in_bounds")


def obs_kernel(cnt_ref, tab_hbm, base_hbm, field_hbm, w_hbm, held_hbm, inc_hbm, out_ref,
               base_ref, field_ref, in_sems,
               tab, stack, dense, plan, cidx, ridx, ridx_s, sem, windows, places, sources, *accs):
    rows = tab_hbm.shape[0]
    cells = 16 * 128
    lane = lax.broadcasted_iota(jnp.int32, (8, 128), 1)
    sub = lax.broadcasted_iota(jnp.int32, (8, 128), 0)
    zero = jnp.zeros((8, 128), jnp.float32)
    body = pl.ds(PAD, rows)
    loads = [
        pltpu.make_async_copy(source, target, in_sems.at[k])
        for k, (source, target) in enumerate((
            (base_hbm, base_ref), (field_hbm, field_ref), (held_hbm, stack.at[:, pl.ds(4, 2)]),
            *((w_hbm.at[k], stack.at[:, pl.ds(k, 1)]) for k in range(4)), (tab_hbm, tab.at[body]),
        ))
    ]
    keep = pltpu.make_async_copy(tab.at[body], inc_hbm, in_sems.at[8])
    for load in loads:
        load.start()
    tab[pl.ds(0, 8), :] = zero
    tab[pl.ds(rows + PAD, 8), :] = zero
    for load in loads[:2]:
        load.wait()

    @pl.loop(0, 4)
    def _(b):
        for k in range(4):
            at = pl.multiple_of(b * 32 + 8 * k, 8)
            index = field_ref[pl.ds(at, 8), :] * cells + base_ref[pl.ds(at, 8), :]
            stack[pl.ds(at, 8), 6, :] = index.astype(jnp.float32)

    for load in loads[2:-1]:
        load.wait()

    def compact(o, carry):
        start, kept = carry
        group = stack[o]
        shift = lax.bitwise_and(start, 127)
        row = lax.shift_right_logical(start, 7)
        rolled = pltpu.roll(group, shift, 1)
        merged = jnp.where(lane >= shift, rolled, kept)
        at = pl.multiple_of(row * 8, 8)
        dense[pl.ds(at, 8), :] = merged
        dense[pl.ds(at + 8, 8), :] = rolled
        after = start + cnt_ref[0, o]
        moved = lax.shift_right_logical(after, 7) > row
        return after, jnp.where(moved, rolled, merged)

    total, _ = lax.fori_loop(0, 128, compact, (jnp.int32(0), zero), unroll=32)
    chunks = lax.shift_right_logical(total + 127, 7)

    even = lax.bitwise_and(lane, 1) == 0

    def paired(low, high, add=0):
        after = pltpu.roll(high, 1, 1) + add
        return jnp.where(even, low, after), jnp.where(even, after, low)

    def plan_chunks(at):
        at = pl.multiple_of(at, 8)
        part = pl.ds(at, 8)
        arrays = [dense[pl.ds(at * 8 + k, 8, stride=8), :] for k in range(7)]
        live = (at + sub) * 128 + lane < total
        index = jnp.where(live, arrays[6].astype(jnp.int32), 0)
        ridx[part, :] = lax.shift_right_logical(index, 7) + PAD
        cols = lax.bitwise_and(index, 127)
        cidx[0, part, :], cidx[1, part, :] = paired(cols, cols, 1)
        cidx[2, part, :] = lane - cols
        for a in range(2):
            pair = [jnp.where(live, arrays[2 * a + b], 0.0) for b in range(2)]
            first_row, second_row = paired(*pair)
            plan[a, part, :], plan[2 + a, part, :] = first_row, second_row
        precision = jnp.where(live, arrays[5], 0.0)
        value = jnp.where(live, arrays[4], 0.0)
        plan[4, part, :], plan[5, part, :] = value, precision
        plan[6, part, :], plan[7, part, :] = pltpu.roll(value, 1, 1), pltpu.roll(precision, 1, 1)

    @pl.loop(0, 4)
    def _(b):
        for k in range(4):
            plan_chunks(b * 32 + 8 * k)

    copy = pltpu.make_async_copy(ridx, ridx_s, sem)
    copy.start()

    @pl.loop(0, (rows + 2 * PAD) // 16)
    def _(i):
        for acc in accs:
            for k in range(2):
                acc[pl.ds(pl.multiple_of(i * 16 + 8 * k, 8), 8), :] = zero

    copy.wait()
    loads[-1].wait()
    keep.start()

    quad = lax.shift_right_logical(sub, 1)
    first = lax.bitwise_and(sub, 1) == 0
    keys = (
        lax.shift_right_logical(lane, 1) - 16 * quad,
        lax.shift_right_logical(lax.bitwise_and(lane - 1, 127), 1) - 16 * quad,
    )

    def spread(row):
        return jnp.broadcast_to(row, (8, 128))

    def weights(d):
        line = pl.ds(d, 1)
        return [jnp.where(first, spread(plan[2 * par, line, :]), spread(plan[2 * par + 1, line, :])) for par in range(2)]

    def load_windows(d):
        row_at = ridx_s.at[d]
        for par in range(2):
            for g in range(16):
                merged = None
                for q in range(4):
                    r = row_at[2 * (g + 16 * q) + par]
                    value = tab[pl.ds(r - 2 * q, 8), :]
                    merged = value if q == 0 else jnp.where(sub >= 2 * q, value, merged)
                windows[16 * par + g] = merged

    def gather(d):
        sums = []
        for par in range(2):
            start = spread(cidx[par, pl.ds(d, 1), :])
            found = zero
            for g in range(16):
                found = jnp.where(keys[par] == g, pick_lanes(windows[16 * par + g], start), found)
            sums.append(found)
        return sums

    def compare(d, found):
        line = pl.ds(d, 1)
        weight = weights(d)
        sums = [spread(jnp.sum(found[par] * weight[par], axis=0, keepdims=True)) for par in range(2)]
        here = jnp.where(even, sums[0], sums[1])
        there = jnp.where(even, sums[1], sums[0])
        value, precision, value_w, precision_w = [spread(plan[k, line, :]) for k in range(4, 8)]
        misfit = precision * (here + pltpu.roll(there, 127, 1) - value)
        moved = precision_w * (pltpu.roll(here, 1, 1) + there - value_w)
        return (
            weight[0] * jnp.where(even, misfit, moved),
            weight[1] * jnp.where(even, moved, misfit),
        )

    lane_par = lax.bitwise_and(lane, 1)
    ones = jnp.ones((128, 128), jnp.bfloat16)

    def turn_lanes(d):
        turn = spread(cidx[2, pl.ds(d, 1), :]).astype(jnp.float32)
        picked = [
            jnp.where(jnp.logical_and(keys[par] == g, lane_par == par), turn, 0.0)
            for par in range(2) for g in range(16)
        ]
        picked = jnp.concatenate(picked, axis=0).astype(jnp.bfloat16)
        turns = jnp.dot(picked, ones, preferred_element_type=jnp.float32).astype(jnp.int32)
        for k in range(32):
            sources[k] = lax.bitwise_and(lane + turns[8 * k:8 * k + 8], 127)

    def place(amounts):
        for par in range(2):
            for g in range(16):
                masked = jnp.where(keys[par] == g, amounts[par], 0.0)
                places[16 * par + g] = pick_lanes(masked, sources[16 * par + g])

    def add_rows(d):
        row_at = ridx_s.at[d]
        for par in range(2):
            for g in range(16):
                placed = places[16 * par + g]
                for q in range(4):
                    r = row_at[2 * (g + 16 * q) + par]
                    acc = accs[(g % (len(accs) // 4)) * 4 + q]
                    at = pl.ds(r - 2 * q, 8)
                    acc[at, :] = acc[at, :] + jnp.where(quad == q, placed, 0.0)

    for k in range(32):
        windows[k] = zero
        places[k] = zero
        sources[k] = lane

    def step(d, carry):
        found_e, found_o, amounts_e, amounts_o = carry
        last = jnp.maximum(chunks - 1, 0)
        add_rows(jnp.clip(d - 4, 0, last))
        place((amounts_e, amounts_o))
        turn_lanes(jnp.clip(d - 2, 0, last))
        amounts = compare(jnp.clip(d - 2, 0, last), (found_e, found_o))
        found = gather(jnp.clip(d - 1, 0, last))
        load_windows(jnp.minimum(d, last))
        ready = d > 1
        return (*found, jnp.where(ready, amounts[0], 0.0), jnp.where(ready, amounts[1], 0.0))

    lax.fori_loop(0, chunks + 4, step, (zero,) * 4)

    @pl.loop(0, rows // 80)
    def _(i):
        for k in range(10):
            at = pl.multiple_of(i * 80 + 8 * k, 8)
            parts = [acc[pl.ds(at + PAD, 8), :] for acc in accs]
            while len(parts) > 1:
                parts = [a + b for a, b in zip(parts[::2], parts[1::2])]
            out_ref[pl.ds(at, 8), :] = parts[0]

    keep.wait()


def observe(table, count, base, field, weight, held):
    rows, cols = table.shape
    vmem = pl.BlockSpec(memory_space=pltpu.VMEM)
    anywhere = pl.BlockSpec(memory_space=pl.ANY)
    far_memory = pl.BlockSpec(memory_space=pltpu.HBM)
    smem = pl.BlockSpec(memory_space=pltpu.SMEM)
    return pl.pallas_call(
        obs_kernel,
        out_shape=[jax.ShapeDtypeStruct((rows, cols), jnp.float32)] * 2,
        in_specs=[smem, anywhere] + [far_memory] * 4,
        out_specs=[far_memory, vmem],
        scratch_shapes=[
            pltpu.VMEM((128, 128), jnp.int32),
            pltpu.VMEM((128, 128), jnp.int32),
            pltpu.SemaphoreType.DMA((9,)),
            pltpu.VMEM((rows + 2 * PAD, cols), jnp.float32),
            pltpu.VMEM((128, 8, 128), jnp.float32),
            pltpu.VMEM((129 * 8, 128), jnp.float32),
            pltpu.VMEM((8, 128, 128), jnp.float32),
            pltpu.VMEM((3, 128, 128), jnp.int32),
            pltpu.VMEM((128, 128), jnp.int32),
            pltpu.SMEM((128, 128), jnp.int32),
            pltpu.SemaphoreType.DMA,
            pltpu.VMEM((32, 8, 128), jnp.float32),
            pltpu.VMEM((32, 8, 128), jnp.float32),
            pltpu.VMEM((32, 8, 128), jnp.int32),
        ] + [pltpu.VMEM((rows + 2 * PAD, cols), jnp.float32)] * NACC,
        compiler_params=pltpu.CompilerParams(vmem_limit_bytes=30 * 2**20),
        name="observe",
    )(count, table, base, field, weight, held)


def per_device(
    control,
    lon_coef,
    lat_coef,
    obs_base,
    obs_field,
    obs_weight,
    obs_count,
    obs_value,
    obs_precision,
):
    fields, band_rows, block_cols = control.shape
    owners, slots = obs_base.shape[1:]
    by_device = (lax.axis_size("lon"), lax.axis_size("lat"), 1, slots)
    lines = control.reshape(fields * band_rows, block_cols)
    increment, coefs, held = root(
        lines,
        (lon_coef.T, lat_coef.T, obs_value.reshape(by_device), obs_precision.reshape(by_device)),
        band_rows,
        True,
    )
    increment, forcing = observe(
        increment,
        obs_count,
        obs_base[0],
        obs_field[0],
        obs_weight.reshape(obs_weight.shape[0], owners, 1, slots),
        held.reshape(owners, 2, slots),
    )
    (gradient,) = root(forcing, (coefs, lines), band_rows, False)
    return (increment.reshape(control.shape), gradient.reshape(control.shape))


def solution(mesh):
    in_specs = (
        P(None, "lat", "lon"),
        P(None, "lat"),
        P(None, "lat"),
        P(("lon", "lat"), None, None),
        P(("lon", "lat"), None, None),
        P(None, ("lon", "lat"), None, None),
        P(("lon", "lat"), None),
        P(("lon", "lat"), None, None),
        P(("lon", "lat"), None, None),
    )
    out_specs = (P(None, "lat", "lon"), P(None, "lat", "lon"))
    return jax.shard_map(
        per_device, mesh=mesh, in_specs=in_specs, out_specs=out_specs, check_vma=False
    )
```

```python
import functools

import jax
import jax.numpy as jnp
from jax import lax
from jax.experimental import pallas as pl
from jax.experimental.pallas import tpu as pltpu
from jax.sharding import PartitionSpec as P

MESH = pl.DeviceIdType.MESH
DEEP = 4
EDGE = 8
KINDS = (
    "up_main", "up_west", "up_east", "down_main", "down_west", "down_east", "west", "east", "up_coef", "down_coef",
)


def root_kernel(first, rows, *refs):
    if first:
        (x_hbm, zonal_hbm, merid_hbm, value_ref, precision_ref, out_ref, coef_out, held_out, *scratch) = refs
        (x_ref, zonal_ref, merid_ref, in_sems, coef, held_mid, near_sems, far_sems, own_sems, *scratch) = scratch
        loads = [
            pltpu.make_async_copy(source, target, in_sems.at[k])
            for k, (source, target) in enumerate(((zonal_hbm, zonal_ref), (merid_hbm, merid_ref), (x_hbm, x_ref)))
        ]
        for load in loads:
            load.start()
    else:
        (x_ref, coef, add_hbm, out_ref, add_ref, add_sem, *scratch) = refs
        addend = pltpu.make_async_copy(add_hbm, add_ref, add_sem)
        addend.start()
    (main, main2, send_sems, recv_sems) = scratch
    cols = x_ref.shape[1]
    fields = x_ref.shape[0] // rows
    ext = rows + 2 * DEEP
    n_lon, n_lat = lax.axis_size("lon"), lax.axis_size("lat")
    lon, lat = lax.axis_index("lon"), lax.axis_index("lat")
    west, east = lax.rem(lon + n_lon - 1, n_lon), lax.rem(lon + 1, n_lon)
    has_up, has_down = lat > 0, lat < n_lat - 1
    barrier = pltpu.get_barrier_semaphore()

    def greet(there_lon, there_lat):
        pl.semaphore_signal(barrier, inc=1, device_id={"lon": there_lon, "lat": there_lat}, device_id_type=MESH)

    sides = has_up.astype(jnp.int32) + has_down.astype(jnp.int32)
    for present, there_lat in ((has_up, lat - 1), (has_down, lat + 1)):
        @pl.when(present)
        def _():
            for there_lon in (west, east) if first else (lon, west, east):
                greet(there_lon, there_lat)

    if first:
        for k in range(1, n_lat):
            greet(lon, lax.rem(lat + k, n_lat))

        @pl.loop(1, n_lon)
        def _(k):
            greet(lax.rem(lon + k, n_lon), lat)

        greetings = 2 * sides + (n_lat - 1) + (n_lon - 1)
    else:
        greet(west, lat)
        greet(east, lat)
        greetings = 3 * sides + 2

    def remote(source, target, send, recv, there_lon, there_lat):
        return pltpu.make_async_remote_copy(
            src_ref=source, dst_ref=target, send_sem=send, recv_sem=recv,
            device_id={"lon": there_lon, "lat": there_lat}, device_id_type=MESH,
        )

    above, below = pl.ds(0, DEEP), pl.ds(rows + DEEP, DEEP)
    top, bottom, band = pl.ds(DEEP, DEEP), pl.ds(rows, DEEP), pl.ds(DEEP, rows)
    block = pl.ds(EDGE, cols)
    west_edge, east_edge = pl.ds(EDGE, DEEP), pl.ds(EDGE + cols - DEEP, DEEP)
    west_halo, east_halo = pl.ds(EDGE - DEEP, DEEP), pl.ds(EDGE + cols, DEEP)

    def exchange(kind):
        source_rows, target_rows, source_cols, target_cols, there_lon, there_lat = {
            "up_main": (top, below, block, block, lon, lat - 1),
            "up_west": (top, below, west_edge, east_halo, west, lat - 1),
            "up_east": (top, below, east_edge, west_halo, east, lat - 1),
            "down_main": (bottom, above, block, block, lon, lat + 1),
            "down_west": (bottom, above, west_edge, east_halo, west, lat + 1),
            "down_east": (bottom, above, east_edge, west_halo, east, lat + 1),
            "west": (band, band, west_edge, east_halo, west, lat),
            "east": (band, band, east_edge, west_halo, east, lat),
        }[kind]
        slot = KINDS.index(kind)
        return remote(
            main.at[source_rows, source_cols], main.at[target_rows, target_cols],
            send_sems.at[slot], recv_sems.at[slot], there_lon, there_lat,
        )

    def exchange_coef(kind):
        pair, slot = pl.ds(0, 2), KINDS.index(kind)
        source, target, there_lat = (top, below, lat - 1) if kind == "up_coef" else (bottom, above, lat + 1)
        return remote(coef.at[pair, source], coef.at[pair, target], send_sems.at[slot], recv_sems.at[slot], lon, there_lat)

    whole = fields // 8
    rest = fields - 8 * whole

    def turn_in(j):
        parts = [x_ref[pl.ds(j + rows * 8 * k, 8, stride=rows), :] for k in range(whole)]
        if rest:
            tail = x_ref[pl.ds(j + rows * 8 * whole, rest, stride=rows), :]
            parts.append(jnp.concatenate([tail, jnp.zeros((8 - rest, cols), jnp.float32)], axis=0))
        parts.append(jnp.zeros((cols - 8 * len(parts), cols), jnp.float32))
        main[j + DEEP, block] = jnp.concatenate(parts, axis=0).T

    def turn_out(j, plane):
        turned = plane.T
        for k in range(whole + (rest > 0)):
            size = 8 if k < whole else rest
            at = pl.ds(j + rows * 8 * k, size, stride=rows)
            value = turned[8 * k:8 * k + size]
            if not first:
                value = value + add_ref[at, :]
            out_ref[at, :] = value

    if first:
        for load in loads:
            load.wait()
        row = lax.broadcasted_iota(jnp.int32, (rows, fields), 0)
        closed = jnp.logical_and(row == rows - 1, lat == n_lat - 1)
        blank = jnp.zeros((rows, cols), jnp.float32)
        for k, rates in enumerate((zonal_ref[...], jnp.where(closed, 0.0, merid_ref[...]))):
            coef[k, band] = blank
            coef[k, band, pl.ds(0, fields)] = rates

    for start in (0, rows - DEEP):
        @pl.loop(start, start + DEEP)
        def _(j):
            turn_in(j)

    if first:
        sent = (value_ref, precision_ref)

        def near(n, k):
            there = lax.rem(lat + k, n_lat)
            return remote(
                sent[n].at[:, there], held_mid.at[lat, :, pl.ds(n, 1)],
                near_sems.at[0, n, k], near_sems.at[1, n, k], lon, there,
            )

        def near_own(n):
            return pltpu.make_async_copy(sent[n].at[:, lat], held_mid.at[lat, :, pl.ds(n, 1)], own_sems.at[n])

        def far(k):
            there = lax.rem(lon + k, n_lon)
            return remote(held_mid.at[:, there], held_out.at[lon], far_sems.at[0, k], far_sems.at[1, k], there, lat)

        def far_own():
            return pltpu.make_async_copy(held_mid.at[:, lon], held_out.at[lon], own_sems.at[2])

    pl.semaphore_wait(barrier, greetings)

    if first:
        for n in range(2):
            for k in range(1, n_lat):
                near(n, k).start()
            near_own(n).start()

    for present, way, at in ((has_up, "up", above), (has_down, "down", below)):
        @pl.when(present)
        def _():
            if first:
                exchange_coef(way + "_coef").start()
            exchange(way + "_main").start()
            exchange(way + "_west").start()
            exchange(way + "_east").start()

        @pl.when(jnp.logical_not(present))
        def _():
            main[at] = jnp.zeros((DEEP,) + main.shape[1:], jnp.float32)
            if first:
                coef[pl.ds(0, 2), at] = jnp.zeros((2, DEEP, cols), jnp.float32)

    @pl.loop(DEEP, rows - DEEP)
    def _(j):
        turn_in(j)

    for kind in ("west", "east"):
        exchange(kind).start()

    if first:
        for n in range(2):
            for k in range(1, n_lat):
                near(n, k).wait_recv()
            near_own(n).wait()

        @pl.loop(1, n_lon)
        def _(k):
            far(k).start()

        far_own().start()

        for present, way in ((has_up, "down_coef"), (has_down, "up_coef")):
            @pl.when(present)
            def _():
                exchange_coef(way).wait_recv()

        coef[2] = jnp.zeros((ext, cols), jnp.float32)
        for start in (1, 9, ext - 9):
            at = pl.ds(start, 8)
            coef[2, at] = 1.0 - 2.0 * coef[0, at] - coef[1, at] - coef[1, pl.ds(start - 1, 8)]
        coef_out[...] = coef[...]

    for kind in ("west", "east"):
        exchange(kind).wait_recv()
    for present, way in ((has_up, "down"), (has_down, "up")):
        @pl.when(present)
        def _():
            for kind in ("_main", "_west", "_east"):
                exchange(way + kind).wait_recv()

    def swept(source, p, starts):
        rate = lambda k, q: jnp.broadcast_to(coef[k, pl.ds(q, 1), :], (8, cols))
        c, z, n, s = rate(2, p), rate(0, p), rate(1, p), rate(1, p - 1)
        out = []
        for start in starts:
            at = pl.ds(start, 8)
            value = c * source[p, at, :] + z * (source[p, pl.ds(start - 1, 8), :] + source[p, pl.ds(start + 1, 8), :])
            out.append(value + n * source[p + 1, at, :] + s * source[p - 1, at, :])
        return out

    def sweep(source, target, t):
        starts = range(EDGE - DEEP + t, EDGE + cols + DEEP - t, 8)

        @pl.loop(t, ext - t)
        def _(p):
            for start, value in zip(starts, swept(source, p, starts)):
                target[p, pl.ds(start, 8), :] = value

    sweep(main, main2, 1)

    for kind in ("west", "east"):
        exchange(kind).wait_send()
    for present, way in ((has_up, "up"), (has_down, "down")):
        @pl.when(present)
        def _():
            for kind in ("_main", "_west", "_east"):
                exchange(way + kind).wait_send()

    sweep(main2, main, 2)
    sweep(main, main2, 3)
    if not first:
        addend.wait()

    @pl.loop(0, rows // 2)
    def _(i):
        for k in range(2):
            j = i * 2 + k
            turn_out(j, jnp.concatenate(swept(main2, j + DEEP, range(EDGE, EDGE + cols, 8)), axis=0))

    if first:
        for present, way in ((has_up, "up_coef"), (has_down, "down_coef")):
            @pl.when(present)
            def _():
                exchange_coef(way).wait_send()

        for n in range(2):
            for k in range(1, n_lat):
                near(n, k).wait_send()

        @pl.loop(1, n_lon)
        def _(k):
            far(k).wait_recv()
            far(k).wait_send()

        far_own().wait()


def root(field, operands, rows, first):
    cols = field.shape[1]
    ext = rows + 2 * DEEP
    vmem = pl.BlockSpec(memory_space=pltpu.VMEM)
    f32 = lambda *shape: jax.ShapeDtypeStruct(shape, jnp.float32)
    scratch = [pltpu.VMEM((ext, cols + 2 * EDGE, cols), jnp.float32)] * 2
    scratch += [pltpu.SemaphoreType.DMA((len(KINDS),))] * 2
    outs = [f32(*field.shape)]
    far_memory = pl.BlockSpec(memory_space=pltpu.HBM)
    in_specs, out_specs = [vmem] * (1 + len(operands)), [vmem]
    if first:
        in_specs = [far_memory] * 5
        out_specs += [vmem, far_memory]
        n_lon, n_lat = lax.axis_size("lon"), lax.axis_size("lat")
        outs += [f32(3, ext, cols)] + [f32(n_lon, n_lat, 2, cols)]
        scratch = (
            [pltpu.VMEM(field.shape, jnp.float32)]
            + [pltpu.VMEM(operands[0].shape, jnp.float32)] * 2
            + [pltpu.SemaphoreType.DMA((3,))]
            + [pltpu.VMEM((3, ext, cols), jnp.float32)]
            + [pltpu.VMEM((n_lat, n_lon, 2, cols), jnp.float32)]
            + [pltpu.SemaphoreType.DMA((2, 2, n_lat)), pltpu.SemaphoreType.DMA((2, n_lon)), pltpu.SemaphoreType.DMA((3,))]
            + scratch
        )
    else:
        in_specs[2] = far_memory
        scratch = [pltpu.VMEM(field.shape, jnp.float32), pltpu.SemaphoreType.DMA] + scratch
    return pl.pallas_call(
        functools.partial(root_kernel, first, rows),
        out_shape=outs,
        in_specs=in_specs,
        out_specs=out_specs,
        scratch_shapes=scratch,
        compiler_params=pltpu.CompilerParams(
            collective_id=0 if first else 1, has_side_effects=True, vmem_limit_bytes=(60 if first else 16) * 2**20),
        name="root_first" if first else "root_second",
    )(field, *operands)


PAD = 8
NACC = 16
LANES = lax.GatherDimensionNumbers(
    offset_dims=(), collapsed_slice_dims=(1,), start_index_map=(1,),
    operand_batching_dims=(0,), start_indices_batching_dims=(0,))


def pick_lanes(value, index):
    return lax.gather(value, index[:, :, None], LANES, slice_sizes=(1, 1), mode="promise_in_bounds")


def obs_kernel(cnt_ref, tab_hbm, base_hbm, field_hbm, w_hbm, held_hbm, inc_hbm, out_ref,
               base_ref, field_ref, in_sems,
               tab, stack, dense, plan, cidx, ridx, ridx_s, sem, windows, places, sources, *accs):
    rows = tab_hbm.shape[0]
    cells = 16 * 128
    lane = lax.broadcasted_iota(jnp.int32, (8, 128), 1)
    sub = lax.broadcasted_iota(jnp.int32, (8, 128), 0)
    zero = jnp.zeros((8, 128), jnp.float32)
    body = pl.ds(PAD, rows)
    loads = [
        pltpu.make_async_copy(source, target, in_sems.at[k])
        for k, (source, target) in enumerate((
            (base_hbm, base_ref), (field_hbm, field_ref), (held_hbm, stack.at[:, pl.ds(4, 2)]),
            *((w_hbm.at[k], stack.at[:, pl.ds(k, 1)]) for k in range(4)), (tab_hbm, tab.at[body]),
        ))
    ]
    keep = pltpu.make_async_copy(tab.at[body], inc_hbm, in_sems.at[8])
    for load in loads:
        load.start()
    tab[pl.ds(0, 8), :] = zero
    tab[pl.ds(rows + PAD, 8), :] = zero
    for load in loads[:2]:
        load.wait()

    @pl.loop(0, 4)
    def _(b):
        for k in range(4):
            at = pl.multiple_of(b * 32 + 8 * k, 8)
            index = field_ref[pl.ds(at, 8), :] * cells + base_ref[pl.ds(at, 8), :]
            stack[pl.ds(at, 8), 6, :] = index.astype(jnp.float32)

    for load in loads[2:-1]:
        load.wait()

    def compact(o, carry):
        start, kept = carry
        group = stack[o]
        shift = lax.bitwise_and(start, 127)
        row = lax.shift_right_logical(start, 7)
        rolled = pltpu.roll(group, shift, 1)
        merged = jnp.where(lane >= shift, rolled, kept)
        at = pl.multiple_of(row * 8, 8)
        dense[pl.ds(at, 8), :] = merged
        dense[pl.ds(at + 8, 8), :] = rolled
        after = start + cnt_ref[0, o]
        moved = lax.shift_right_logical(after, 7) > row
        return after, jnp.where(moved, rolled, merged)

    total, _ = lax.fori_loop(0, 128, compact, (jnp.int32(0), zero), unroll=32)
    chunks = lax.shift_right_logical(total + 127, 7)

    even = lax.bitwise_and(lane, 1) == 0

    def paired(low, high, add=0):
        after = pltpu.roll(high, 1, 1) + add
        return jnp.where(even, low, after), jnp.where(even, after, low)

    def plan_chunks(at):
        at = pl.multiple_of(at, 8)
        part = pl.ds(at, 8)
        arrays = [dense[pl.ds(at * 8 + k, 8, stride=8), :] for k in range(7)]
        live = (at + sub) * 128 + lane < total
        index = jnp.where(live, arrays[6].astype(jnp.int32), 0)
        ridx[part, :] = lax.shift_right_logical(index, 7) + PAD
        cols = lax.bitwise_and(index, 127)
        cidx[0, part, :], cidx[1, part, :] = paired(cols, cols, 1)
        cidx[2, part, :] = lane - cols
        for a in range(2):
            pair = [jnp.where(live, arrays[2 * a + b], 0.0) for b in range(2)]
            first_row, second_row = paired(*pair)
            plan[a, part, :], plan[2 + a, part, :] = first_row, second_row
        precision = jnp.where(live, arrays[5], 0.0)
        value = jnp.where(live, arrays[4], 0.0)
        plan[4, part, :], plan[5, part, :] = value, precision
        plan[6, part, :], plan[7, part, :] = pltpu.roll(value, 1, 1), pltpu.roll(precision, 1, 1)

    @pl.loop(0, 4)
    def _(b):
        for k in range(4):
            plan_chunks(b * 32 + 8 * k)

    copy = pltpu.make_async_copy(ridx, ridx_s, sem)
    copy.start()

    @pl.loop(0, (rows + 2 * PAD) // 16)
    def _(i):
        for acc in accs:
            for k in range(2):
                acc[pl.ds(pl.multiple_of(i * 16 + 8 * k, 8), 8), :] = zero

    copy.wait()
    loads[-1].wait()
    keep.start()

    quad = lax.shift_right_logical(sub, 1)
    first = lax.bitwise_and(sub, 1) == 0
    keys = (
        lax.shift_right_logical(lane, 1) - 16 * quad,
        lax.shift_right_logical(lax.bitwise_and(lane - 1, 127), 1) - 16 * quad,
    )

    def spread(row):
        return jnp.broadcast_to(row, (8, 128))

    def weights(d):
        line = pl.ds(d, 1)
        return [jnp.where(first, spread(plan[2 * par, line, :]), spread(plan[2 * par + 1, line, :])) for par in range(2)]

    def load_windows(d):
        row_at = ridx_s.at[d]
        for par in range(2):
            for g in range(16):
                merged = None
                for q in range(4):
                    r = row_at[2 * (g + 16 * q) + par]
                    value = tab[pl.ds(r - 2 * q, 8), :]
                    merged = value if q == 0 else jnp.where(sub >= 2 * q, value, merged)
                windows[16 * par + g] = merged

    def gather(d):
        sums = []
        for par in range(2):
            start = spread(cidx[par, pl.ds(d, 1), :])
            found = zero
            for g in range(16):
                found = jnp.where(keys[par] == g, pick_lanes(windows[16 * par + g], start), found)
            sums.append(found)
        return sums

    def compare(d, found):
        line = pl.ds(d, 1)
        weight = weights(d)
        sums = [spread(jnp.sum(found[par] * weight[par], axis=0, keepdims=True)) for par in range(2)]
        here = jnp.where(even, sums[0], sums[1])
        there = jnp.where(even, sums[1], sums[0])
        value, precision, value_w, precision_w = [spread(plan[k, line, :]) for k in range(4, 8)]
        misfit = precision * (here + pltpu.roll(there, 127, 1) - value)
        moved = precision_w * (pltpu.roll(here, 1, 1) + there - value_w)
        return (
            weight[0] * jnp.where(even, misfit, moved),
            weight[1] * jnp.where(even, moved, misfit),
        )

    lane_par = lax.bitwise_and(lane, 1)
    ones = jnp.ones((128, 128), jnp.bfloat16)

    def turn_lanes(d):
        turn = spread(cidx[2, pl.ds(d, 1), :]).astype(jnp.float32)
        picked = [
            jnp.where(jnp.logical_and(keys[par] == g, lane_par == par), turn, 0.0)
            for par in range(2) for g in range(16)
        ]
        picked = jnp.concatenate(picked, axis=0).astype(jnp.bfloat16)
        turns = jnp.dot(picked, ones, preferred_element_type=jnp.float32).astype(jnp.int32)
        for k in range(32):
            sources[k] = lax.bitwise_and(lane + turns[8 * k:8 * k + 8], 127)

    def place(amounts):
        for par in range(2):
            for g in range(16):
                masked = jnp.where(keys[par] == g, amounts[par], 0.0)
                places[16 * par + g] = pick_lanes(masked, sources[16 * par + g])

    def add_rows(d):
        row_at = ridx_s.at[d]
        for par in range(2):
            for g in range(16):
                placed = places[16 * par + g]
                for q in range(4):
                    r = row_at[2 * (g + 16 * q) + par]
                    acc = accs[(g % (len(accs) // 4)) * 4 + q]
                    at = pl.ds(r - 2 * q, 8)
                    acc[at, :] = acc[at, :] + jnp.where(quad == q, placed, 0.0)

    for k in range(32):
        windows[k] = zero
        places[k] = zero
        sources[k] = lane

    def step(d, carry):
        found_e, found_o, amounts_e, amounts_o = carry
        last = jnp.maximum(chunks - 1, 0)
        add_rows(jnp.clip(d - 4, 0, last))
        place((amounts_e, amounts_o))
        turn_lanes(jnp.clip(d - 2, 0, last))
        amounts = compare(jnp.clip(d - 2, 0, last), (found_e, found_o))
        found = gather(jnp.clip(d - 1, 0, last))
        load_windows(jnp.minimum(d, last))
        ready = d > 1
        return (*found, jnp.where(ready, amounts[0], 0.0), jnp.where(ready, amounts[1], 0.0))

    def first_step(d, carry):
        last = jnp.maximum(chunks - 1, 0)
        turn_lanes(jnp.clip(d - 2, 0, last))
        amounts = compare(jnp.clip(d - 2, 0, last), carry[:2])
        found = gather(jnp.clip(d - 1, 0, last))
        load_windows(jnp.minimum(d, last))
        return (*found, jnp.where(d > 1, amounts[0], 0.0), jnp.where(d > 1, amounts[1], 0.0))

    def last_step(d, carry):
        add_rows(jnp.clip(d - 4, 0, jnp.maximum(chunks - 1, 0)))
        place(carry[2:])
        return carry

    carry = lax.fori_loop(0, 3, first_step, (zero,) * 4)
    carry = lax.fori_loop(3, chunks + 2, step, carry)
    lax.fori_loop(chunks + 2, chunks + 4, last_step, carry)

    @pl.loop(0, rows // 80)
    def _(i):
        for k in range(10):
            at = pl.multiple_of(i * 80 + 8 * k, 8)
            parts = [acc[pl.ds(at + PAD, 8), :] for acc in accs]
            while len(parts) > 1:
                parts = [a + b for a, b in zip(parts[::2], parts[1::2])]
            out_ref[pl.ds(at, 8), :] = parts[0]

    keep.wait()


def observe(table, count, base, field, weight, held):
    rows, cols = table.shape
    vmem = pl.BlockSpec(memory_space=pltpu.VMEM)
    anywhere = pl.BlockSpec(memory_space=pl.ANY)
    far_memory = pl.BlockSpec(memory_space=pltpu.HBM)
    smem = pl.BlockSpec(memory_space=pltpu.SMEM)
    return pl.pallas_call(
        obs_kernel,
        out_shape=[jax.ShapeDtypeStruct((rows, cols), jnp.float32)] * 2,
        in_specs=[smem, anywhere] + [far_memory] * 4,
        out_specs=[far_memory, vmem],
        scratch_shapes=[
            pltpu.VMEM((128, 128), jnp.int32),
            pltpu.VMEM((128, 128), jnp.int32),
            pltpu.SemaphoreType.DMA((9,)),
            pltpu.VMEM((rows + 2 * PAD, cols), jnp.float32),
            pltpu.VMEM((128, 8, 128), jnp.float32),
            pltpu.VMEM((129 * 8, 128), jnp.float32),
            pltpu.VMEM((8, 128, 128), jnp.float32),
            pltpu.VMEM((3, 128, 128), jnp.int32),
            pltpu.VMEM((128, 128), jnp.int32),
            pltpu.SMEM((128, 128), jnp.int32),
            pltpu.SemaphoreType.DMA,
            pltpu.VMEM((32, 8, 128), jnp.float32),
            pltpu.VMEM((32, 8, 128), jnp.float32),
            pltpu.VMEM((32, 8, 128), jnp.int32),
        ] + [pltpu.VMEM((rows + 2 * PAD, cols), jnp.float32)] * NACC,
        compiler_params=pltpu.CompilerParams(vmem_limit_bytes=30 * 2**20),
        name="observe",
    )(count, table, base, field, weight, held)


def per_device(
    control,
    lon_coef,
    lat_coef,
    obs_base,
    obs_field,
    obs_weight,
    obs_count,
    obs_value,
    obs_precision,
):
    fields, band_rows, block_cols = control.shape
    owners, slots = obs_base.shape[1:]
    by_device = (lax.axis_size("lon"), lax.axis_size("lat"), 1, slots)
    lines = control.reshape(fields * band_rows, block_cols)
    increment, coefs, held = root(
        lines,
        (lon_coef.T, lat_coef.T, obs_value.reshape(by_device), obs_precision.reshape(by_device)),
        band_rows,
        True,
    )
    increment, forcing = observe(
        increment,
        obs_count,
        obs_base[0],
        obs_field[0],
        obs_weight.reshape(obs_weight.shape[0], owners, 1, slots),
        held.reshape(owners, 2, slots),
    )
    (gradient,) = root(forcing, (coefs, lines), band_rows, False)
    return (increment.reshape(control.shape), gradient.reshape(control.shape))


def solution(mesh):
    in_specs = (
        P(None, "lat", "lon"),
        P(None, "lat"),
        P(None, "lat"),
        P(("lon", "lat"), None, None),
        P(("lon", "lat"), None, None),
        P(None, ("lon", "lat"), None, None),
        P(("lon", "lat"), None),
        P(("lon", "lat"), None, None),
        P(("lon", "lat"), None, None),
    )
    out_specs = (P(None, "lat", "lon"), P(None, "lat", "lon"))
    return jax.shard_map(
        per_device, mesh=mesh, in_specs=in_specs, out_specs=out_specs, check_vma=False
    )
```

```python
import functools

import jax
import jax.numpy as jnp
from jax import lax
from jax.experimental import pallas as pl
from jax.experimental.pallas import tpu as pltpu
from jax.sharding import PartitionSpec as P

MESH = pl.DeviceIdType.MESH
DEEP = 4
EDGE = 8
KINDS = (
    "up_main", "up_west", "up_east", "down_main", "down_west", "down_east", "west", "east", "up_coef", "down_coef",
)


def root_kernel(first, rows, *refs):
    if first:
        (x_hbm, zonal_hbm, merid_hbm, value_ref, precision_ref, out_ref, coef_out, held_out, *scratch) = refs
        (x_ref, zonal_ref, merid_ref, in_sems, coef, held_mid, near_sems, far_sems, own_sems, *scratch) = scratch
        loads = [
            pltpu.make_async_copy(source, target, in_sems.at[k])
            for k, (source, target) in enumerate(((zonal_hbm, zonal_ref), (merid_hbm, merid_ref), (x_hbm, x_ref)))
        ]
        for load in loads:
            load.start()
    else:
        (x_ref, coef, add_hbm, out_ref, add_ref, add_sem, *scratch) = refs
        addend = pltpu.make_async_copy(add_hbm, add_ref, add_sem)
        addend.start()
    (main, main2, send_sems, recv_sems) = scratch
    cols = x_ref.shape[1]
    fields = x_ref.shape[0] // rows
    ext = rows + 2 * DEEP
    n_lon, n_lat = lax.axis_size("lon"), lax.axis_size("lat")
    lon, lat = lax.axis_index("lon"), lax.axis_index("lat")
    west, east = lax.rem(lon + n_lon - 1, n_lon), lax.rem(lon + 1, n_lon)
    has_up, has_down = lat > 0, lat < n_lat - 1
    barrier = pltpu.get_barrier_semaphore()

    def greet(there_lon, there_lat):
        pl.semaphore_signal(barrier, inc=1, device_id={"lon": there_lon, "lat": there_lat}, device_id_type=MESH)

    sides = has_up.astype(jnp.int32) + has_down.astype(jnp.int32)
    for present, there_lat in ((has_up, lat - 1), (has_down, lat + 1)):
        @pl.when(present)
        def _():
            for there_lon in (west, east) if first else (lon, west, east):
                greet(there_lon, there_lat)

    if first:
        for k in range(1, n_lat):
            greet(lon, lax.rem(lat + k, n_lat))

        @pl.loop(1, n_lon)
        def _(k):
            greet(lax.rem(lon + k, n_lon), lat)

        greetings = 2 * sides + (n_lat - 1) + (n_lon - 1)
    else:
        greet(west, lat)
        greet(east, lat)
        greetings = 3 * sides + 2

    def remote(source, target, send, recv, there_lon, there_lat):
        return pltpu.make_async_remote_copy(
            src_ref=source, dst_ref=target, send_sem=send, recv_sem=recv,
            device_id={"lon": there_lon, "lat": there_lat}, device_id_type=MESH,
        )

    above, below = pl.ds(0, DEEP), pl.ds(rows + DEEP, DEEP)
    top, bottom, band = pl.ds(DEEP, DEEP), pl.ds(rows, DEEP), pl.ds(DEEP, rows)
    block = pl.ds(EDGE, cols)
    west_edge, east_edge = pl.ds(EDGE, DEEP), pl.ds(EDGE + cols - DEEP, DEEP)
    west_halo, east_halo = pl.ds(EDGE - DEEP, DEEP), pl.ds(EDGE + cols, DEEP)

    def exchange(kind):
        source_rows, target_rows, source_cols, target_cols, there_lon, there_lat = {
            "up_main": (top, below, block, block, lon, lat - 1),
            "up_west": (top, below, west_edge, east_halo, west, lat - 1),
            "up_east": (top, below, east_edge, west_halo, east, lat - 1),
            "down_main": (bottom, above, block, block, lon, lat + 1),
            "down_west": (bottom, above, west_edge, east_halo, west, lat + 1),
            "down_east": (bottom, above, east_edge, west_halo, east, lat + 1),
            "west": (band, band, west_edge, east_halo, west, lat),
            "east": (band, band, east_edge, west_halo, east, lat),
        }[kind]
        slot = KINDS.index(kind)
        return remote(
            main.at[source_rows, source_cols], main.at[target_rows, target_cols],
            send_sems.at[slot], recv_sems.at[slot], there_lon, there_lat,
        )

    def exchange_coef(kind):
        pair, slot = pl.ds(0, 2), KINDS.index(kind)
        source, target, there_lat = (top, below, lat - 1) if kind == "up_coef" else (bottom, above, lat + 1)
        return remote(coef.at[pair, source], coef.at[pair, target], send_sems.at[slot], recv_sems.at[slot], lon, there_lat)

    whole = fields // 8
    rest = fields - 8 * whole

    def turn_in(j):
        parts = [x_ref[pl.ds(j + rows * 8 * k, 8, stride=rows), :] for k in range(whole)]
        if rest:
            tail = x_ref[pl.ds(j + rows * 8 * whole, rest, stride=rows), :]
            parts.append(jnp.concatenate([tail, jnp.zeros((8 - rest, cols), jnp.float32)], axis=0))
        parts.append(jnp.zeros((cols - 8 * len(parts), cols), jnp.float32))
        main[j + DEEP, block] = jnp.concatenate(parts, axis=0).T

    def turn_out(j, plane):
        turned = plane.T
        for k in range(whole + (rest > 0)):
            size = 8 if k < whole else rest
            at = pl.ds(j + rows * 8 * k, size, stride=rows)
            value = turned[8 * k:8 * k + size]
            if not first:
                value = value + add_ref[at, :]
            out_ref[at, :] = value

    if first:
        for load in loads:
            load.wait()
        row = lax.broadcasted_iota(jnp.int32, (rows, fields), 0)
        closed = jnp.logical_and(row == rows - 1, lat == n_lat - 1)
        blank = jnp.zeros((rows, cols), jnp.float32)
        for k, rates in enumerate((zonal_ref[...], jnp.where(closed, 0.0, merid_ref[...]))):
            coef[k, band] = blank
            coef[k, band, pl.ds(0, fields)] = rates

    for start in (0, rows - DEEP):
        @pl.loop(start // 2, (start + DEEP) // 2)
        def _(i):
            turn_in(2 * i)
            turn_in(2 * i + 1)

    if first:
        sent = (value_ref, precision_ref)

        def near(n, k):
            there = lax.rem(lat + k, n_lat)
            return remote(
                sent[n].at[:, there], held_mid.at[lat, :, pl.ds(n, 1)],
                near_sems.at[0, n, k], near_sems.at[1, n, k], lon, there,
            )

        def near_own(n):
            return pltpu.make_async_copy(sent[n].at[:, lat], held_mid.at[lat, :, pl.ds(n, 1)], own_sems.at[n])

        def far(k):
            there = lax.rem(lon + k, n_lon)
            return remote(held_mid.at[:, there], held_out.at[lon], far_sems.at[0, k], far_sems.at[1, k], there, lat)

        def far_own():
            return pltpu.make_async_copy(held_mid.at[:, lon], held_out.at[lon], own_sems.at[2])

    pl.semaphore_wait(barrier, greetings)

    if first:
        for n in range(2):
            for k in range(1, n_lat):
                near(n, k).start()
            near_own(n).start()

    for present, way, at in ((has_up, "up", above), (has_down, "down", below)):
        @pl.when(present)
        def _():
            if first:
                exchange_coef(way + "_coef").start()
            exchange(way + "_main").start()
            exchange(way + "_west").start()
            exchange(way + "_east").start()

        @pl.when(jnp.logical_not(present))
        def _():
            main[at] = jnp.zeros((DEEP,) + main.shape[1:], jnp.float32)
            if first:
                coef[pl.ds(0, 2), at] = jnp.zeros((2, DEEP, cols), jnp.float32)

    @pl.loop(DEEP // 2, (rows - DEEP) // 2)
    def _(i):
        turn_in(2 * i)
        turn_in(2 * i + 1)

    for kind in ("west", "east"):
        exchange(kind).start()

    if first:
        for n in range(2):
            for k in range(1, n_lat):
                near(n, k).wait_recv()
            near_own(n).wait()

        @pl.loop(1, n_lon)
        def _(k):
            far(k).start()

        far_own().start()

        for present, way in ((has_up, "down_coef"), (has_down, "up_coef")):
            @pl.when(present)
            def _():
                exchange_coef(way).wait_recv()

        coef[2] = jnp.zeros((ext, cols), jnp.float32)
        for start in (1, 9, ext - 9):
            at = pl.ds(start, 8)
            coef[2, at] = 1.0 - 2.0 * coef[0, at] - coef[1, at] - coef[1, pl.ds(start - 1, 8)]
        coef_out[...] = coef[...]

    for kind in ("west", "east"):
        exchange(kind).wait_recv()
    for present, way in ((has_up, "down"), (has_down, "up")):
        @pl.when(present)
        def _():
            for kind in ("_main", "_west", "_east"):
                exchange(way + kind).wait_recv()

    def swept(source, p, starts):
        rate = lambda k, q: jnp.broadcast_to(coef[k, pl.ds(q, 1), :], (8, cols))
        c, z, n, s = rate(2, p), rate(0, p), rate(1, p), rate(1, p - 1)
        out = []
        for start in starts:
            at = pl.ds(start, 8)
            value = c * source[p, at, :] + z * (source[p, pl.ds(start - 1, 8), :] + source[p, pl.ds(start + 1, 8), :])
            out.append(value + n * source[p + 1, at, :] + s * source[p - 1, at, :])
        return out

    def sweep(source, target, t):
        starts = range(EDGE - DEEP + t, EDGE + cols + DEEP - t, 8)

        @pl.loop(t, ext - t)
        def _(p):
            for start, value in zip(starts, swept(source, p, starts)):
                target[p, pl.ds(start, 8), :] = value

    sweep(main, main2, 1)

    for kind in ("west", "east"):
        exchange(kind).wait_send()
    for present, way in ((has_up, "up"), (has_down, "down")):
        @pl.when(present)
        def _():
            for kind in ("_main", "_west", "_east"):
                exchange(way + kind).wait_send()

    sweep(main2, main, 2)
    sweep(main, main2, 3)
    if not first:
        addend.wait()

    @pl.loop(0, rows // 2)
    def _(i):
        for k in range(2):
            j = i * 2 + k
            turn_out(j, jnp.concatenate(swept(main2, j + DEEP, range(EDGE, EDGE + cols, 8)), axis=0))

    if first:
        for present, way in ((has_up, "up_coef"), (has_down, "down_coef")):
            @pl.when(present)
            def _():
                exchange_coef(way).wait_send()

        for n in range(2):
            for k in range(1, n_lat):
                near(n, k).wait_send()

        @pl.loop(1, n_lon)
        def _(k):
            far(k).wait_recv()
            far(k).wait_send()

        far_own().wait()


def root(field, operands, rows, first):
    cols = field.shape[1]
    ext = rows + 2 * DEEP
    vmem = pl.BlockSpec(memory_space=pltpu.VMEM)
    f32 = lambda *shape: jax.ShapeDtypeStruct(shape, jnp.float32)
    scratch = [pltpu.VMEM((ext, cols + 2 * EDGE, cols), jnp.float32)] * 2
    scratch += [pltpu.SemaphoreType.DMA((len(KINDS),))] * 2
    outs = [f32(*field.shape)]
    far_memory = pl.BlockSpec(memory_space=pltpu.HBM)
    in_specs, out_specs = [vmem] * (1 + len(operands)), [vmem]
    if first:
        in_specs = [far_memory] * 5
        out_specs += [vmem, far_memory]
        n_lon, n_lat = lax.axis_size("lon"), lax.axis_size("lat")
        outs += [f32(3, ext, cols)] + [f32(n_lon, n_lat, 2, cols)]
        scratch = (
            [pltpu.VMEM(field.shape, jnp.float32)]
            + [pltpu.VMEM(operands[0].shape, jnp.float32)] * 2
            + [pltpu.SemaphoreType.DMA((3,))]
            + [pltpu.VMEM((3, ext, cols), jnp.float32)]
            + [pltpu.VMEM((n_lat, n_lon, 2, cols), jnp.float32)]
            + [pltpu.SemaphoreType.DMA((2, 2, n_lat)), pltpu.SemaphoreType.DMA((2, n_lon)), pltpu.SemaphoreType.DMA((3,))]
            + scratch
        )
    else:
        in_specs[2] = far_memory
        scratch = [pltpu.VMEM(field.shape, jnp.float32), pltpu.SemaphoreType.DMA] + scratch
    return pl.pallas_call(
        functools.partial(root_kernel, first, rows),
        out_shape=outs,
        in_specs=in_specs,
        out_specs=out_specs,
        scratch_shapes=scratch,
        compiler_params=pltpu.CompilerParams(
            collective_id=0 if first else 1, has_side_effects=True, vmem_limit_bytes=(60 if first else 16) * 2**20),
        name="root_first" if first else "root_second",
    )(field, *operands)


PAD = 8
NACC = 16
LANES = lax.GatherDimensionNumbers(
    offset_dims=(), collapsed_slice_dims=(1,), start_index_map=(1,),
    operand_batching_dims=(0,), start_indices_batching_dims=(0,))


def pick_lanes(value, index):
    return lax.gather(value, index[:, :, None], LANES, slice_sizes=(1, 1), mode="promise_in_bounds")


def obs_kernel(cnt_ref, tab_hbm, base_hbm, field_hbm, w_hbm, held_hbm, inc_hbm, out_ref,
               base_ref, field_ref, in_sems,
               tab, stack, dense, plan, cidx, ridx, ridx_s, sem, windows, places, sources, *accs):
    rows = tab_hbm.shape[0]
    cells = 16 * 128
    lane = lax.broadcasted_iota(jnp.int32, (8, 128), 1)
    sub = lax.broadcasted_iota(jnp.int32, (8, 128), 0)
    zero = jnp.zeros((8, 128), jnp.float32)
    body = pl.ds(PAD, rows)
    loads = [
        pltpu.make_async_copy(source, target, in_sems.at[k])
        for k, (source, target) in enumerate((
            (base_hbm, base_ref), (field_hbm, field_ref), (held_hbm, stack.at[:, pl.ds(4, 2)]),
            *((w_hbm.at[k], stack.at[:, pl.ds(k, 1)]) for k in range(4)), (tab_hbm, tab.at[body]),
        ))
    ]
    keep = pltpu.make_async_copy(tab.at[body], inc_hbm, in_sems.at[8])
    for load in loads:
        load.start()
    tab[pl.ds(0, 8), :] = zero
    tab[pl.ds(rows + PAD, 8), :] = zero
    for load in loads[:2]:
        load.wait()

    @pl.loop(0, 4)
    def _(b):
        for k in range(4):
            at = pl.multiple_of(b * 32 + 8 * k, 8)
            index = field_ref[pl.ds(at, 8), :] * cells + base_ref[pl.ds(at, 8), :]
            stack[pl.ds(at, 8), 6, :] = index.astype(jnp.float32)

    for load in loads[2:-1]:
        load.wait()

    def compact(o, carry):
        start, kept = carry
        group = stack[o]
        shift = lax.bitwise_and(start, 127)
        row = lax.shift_right_logical(start, 7)
        rolled = pltpu.roll(group, shift, 1)
        merged = jnp.where(lane >= shift, rolled, kept)
        at = pl.multiple_of(row * 8, 8)
        dense[pl.ds(at, 8), :] = merged
        dense[pl.ds(at + 8, 8), :] = rolled
        after = start + cnt_ref[0, o]
        moved = lax.shift_right_logical(after, 7) > row
        return after, jnp.where(moved, rolled, merged)

    total, _ = lax.fori_loop(0, 128, compact, (jnp.int32(0), zero), unroll=32)
    chunks = lax.shift_right_logical(total + 127, 7)

    even = lax.bitwise_and(lane, 1) == 0

    def paired(low, high, add=0):
        after = pltpu.roll(high, 1, 1) + add
        return jnp.where(even, low, after), jnp.where(even, after, low)

    def plan_chunks(at):
        at = pl.multiple_of(at, 8)
        part = pl.ds(at, 8)
        arrays = [dense[pl.ds(at * 8 + k, 8, stride=8), :] for k in range(7)]
        live = (at + sub) * 128 + lane < total
        index = jnp.where(live, arrays[6].astype(jnp.int32), 0)
        ridx[part, :] = lax.shift_right_logical(index, 7) + PAD
        cols = lax.bitwise_and(index, 127)
        cidx[0, part, :], cidx[1, part, :] = paired(cols, cols, 1)
        cidx[2, part, :] = lane - cols
        for a in range(2):
            pair = [jnp.where(live, arrays[2 * a + b], 0.0) for b in range(2)]
            first_row, second_row = paired(*pair)
            plan[a, part, :], plan[2 + a, part, :] = first_row, second_row
        precision = jnp.where(live, arrays[5], 0.0)
        value = jnp.where(live, arrays[4], 0.0)
        plan[4, part, :], plan[5, part, :] = value, precision
        plan[6, part, :], plan[7, part, :] = pltpu.roll(value, 1, 1), pltpu.roll(precision, 1, 1)

    @pl.loop(0, 4)
    def _(b):
        for k in range(4):
            plan_chunks(b * 32 + 8 * k)

    copy = pltpu.make_async_copy(ridx, ridx_s, sem)
    copy.start()

    @pl.loop(0, (rows + 2 * PAD) // 16)
    def _(i):
        for acc in accs:
            for k in range(2):
                acc[pl.ds(pl.multiple_of(i * 16 + 8 * k, 8), 8), :] = zero

    copy.wait()
    loads[-1].wait()
    keep.start()

    quad = lax.shift_right_logical(sub, 1)
    first = lax.bitwise_and(sub, 1) == 0
    keys = (
        lax.shift_right_logical(lane, 1) - 16 * quad,
        lax.shift_right_logical(lax.bitwise_and(lane - 1, 127), 1) - 16 * quad,
    )

    def spread(row):
        return jnp.broadcast_to(row, (8, 128))

    def weights(d):
        line = pl.ds(d, 1)
        return [jnp.where(first, spread(plan[2 * par, line, :]), spread(plan[2 * par + 1, line, :])) for par in range(2)]

    def load_windows(d):
        row_at = ridx_s.at[d]
        for par in range(2):
            for g in range(16):
                merged = None
                for q in range(4):
                    r = row_at[2 * (g + 16 * q) + par]
                    value = tab[pl.ds(r - 2 * q, 8), :]
                    merged = value if q == 0 else jnp.where(sub >= 2 * q, value, merged)
                windows[16 * par + g] = merged

    def gather(d):
        sums = []
        for par in range(2):
            start = spread(cidx[par, pl.ds(d, 1), :])
            found = zero
            for g in range(16):
                found = jnp.where(keys[par] == g, pick_lanes(windows[16 * par + g], start), found)
            sums.append(found)
        return sums

    def compare(d, found):
        line = pl.ds(d, 1)
        weight = weights(d)
        sums = [spread(jnp.sum(found[par] * weight[par], axis=0, keepdims=True)) for par in range(2)]
        here = jnp.where(even, sums[0], sums[1])
        there = jnp.where(even, sums[1], sums[0])
        value, precision, value_w, precision_w = [spread(plan[k, line, :]) for k in range(4, 8)]
        misfit = precision * (here + pltpu.roll(there, 127, 1) - value)
        moved = precision_w * (pltpu.roll(here, 1, 1) + there - value_w)
        return (
            weight[0] * jnp.where(even, misfit, moved),
            weight[1] * jnp.where(even, moved, misfit),
        )

    lane_par = lax.bitwise_and(lane, 1)
    ones = jnp.ones((128, 128), jnp.bfloat16)

    def turn_lanes(d):
        turn = spread(cidx[2, pl.ds(d, 1), :]).astype(jnp.float32)
        picked = [
            jnp.where(jnp.logical_and(keys[par] == g, lane_par == par), turn, 0.0)
            for par in range(2) for g in range(16)
        ]
        picked = jnp.concatenate(picked, axis=0).astype(jnp.bfloat16)
        turns = jnp.dot(picked, ones, preferred_element_type=jnp.float32).astype(jnp.int32)
        for k in range(32):
            sources[k] = lax.bitwise_and(lane + turns[8 * k:8 * k + 8], 127)

    def place(amounts):
        for par in range(2):
            for g in range(16):
                masked = jnp.where(keys[par] == g, amounts[par], 0.0)
                places[16 * par + g] = pick_lanes(masked, sources[16 * par + g])

    def add_rows(d):
        row_at = ridx_s.at[d]
        for par in range(2):
            for g in range(16):
                placed = places[16 * par + g]
                for q in range(4):
                    r = row_at[2 * (g + 16 * q) + par]
                    acc = accs[(g % (len(accs) // 4)) * 4 + q]
                    at = pl.ds(r - 2 * q, 8)
                    acc[at, :] = acc[at, :] + jnp.where(quad == q, placed, 0.0)

    for k in range(32):
        windows[k] = zero
        places[k] = zero
        sources[k] = lane

    def step(d, carry):
        found_e, found_o, amounts_e, amounts_o = carry
        last = jnp.maximum(chunks - 1, 0)
        add_rows(jnp.clip(d - 4, 0, last))
        place((amounts_e, amounts_o))
        turn_lanes(jnp.clip(d - 2, 0, last))
        amounts = compare(jnp.clip(d - 2, 0, last), (found_e, found_o))
        found = gather(jnp.clip(d - 1, 0, last))
        load_windows(jnp.minimum(d, last))
        ready = d > 1
        return (*found, jnp.where(ready, amounts[0], 0.0), jnp.where(ready, amounts[1], 0.0))

    def first_step(d, carry):
        last = jnp.maximum(chunks - 1, 0)
        turn_lanes(jnp.clip(d - 2, 0, last))
        amounts = compare(jnp.clip(d - 2, 0, last), carry[:2])
        found = gather(jnp.clip(d - 1, 0, last))
        load_windows(jnp.minimum(d, last))
        return (*found, jnp.where(d > 1, amounts[0], 0.0), jnp.where(d > 1, amounts[1], 0.0))

    def last_step(d, carry):
        add_rows(jnp.clip(d - 4, 0, jnp.maximum(chunks - 1, 0)))
        place(carry[2:])
        return carry

    carry = lax.fori_loop(0, 3, first_step, (zero,) * 4)
    carry = lax.fori_loop(3, chunks + 2, step, carry)
    lax.fori_loop(chunks + 2, chunks + 4, last_step, carry)

    @pl.loop(0, rows // 80)
    def _(i):
        for k in range(10):
            at = pl.multiple_of(i * 80 + 8 * k, 8)
            parts = [acc[pl.ds(at + PAD, 8), :] for acc in accs]
            while len(parts) > 1:
                parts = [a + b for a, b in zip(parts[::2], parts[1::2])]
            out_ref[pl.ds(at, 8), :] = parts[0]

    keep.wait()


def observe(table, count, base, field, weight, held):
    rows, cols = table.shape
    vmem = pl.BlockSpec(memory_space=pltpu.VMEM)
    anywhere = pl.BlockSpec(memory_space=pl.ANY)
    far_memory = pl.BlockSpec(memory_space=pltpu.HBM)
    smem = pl.BlockSpec(memory_space=pltpu.SMEM)
    return pl.pallas_call(
        obs_kernel,
        out_shape=[jax.ShapeDtypeStruct((rows, cols), jnp.float32)] * 2,
        in_specs=[smem, anywhere] + [far_memory] * 4,
        out_specs=[far_memory, vmem],
        scratch_shapes=[
            pltpu.VMEM((128, 128), jnp.int32),
            pltpu.VMEM((128, 128), jnp.int32),
            pltpu.SemaphoreType.DMA((9,)),
            pltpu.VMEM((rows + 2 * PAD, cols), jnp.float32),
            pltpu.VMEM((128, 8, 128), jnp.float32),
            pltpu.VMEM((129 * 8, 128), jnp.float32),
            pltpu.VMEM((8, 128, 128), jnp.float32),
            pltpu.VMEM((3, 128, 128), jnp.int32),
            pltpu.VMEM((128, 128), jnp.int32),
            pltpu.SMEM((128, 128), jnp.int32),
            pltpu.SemaphoreType.DMA,
            pltpu.VMEM((32, 8, 128), jnp.float32),
            pltpu.VMEM((32, 8, 128), jnp.float32),
            pltpu.VMEM((32, 8, 128), jnp.int32),
        ] + [pltpu.VMEM((rows + 2 * PAD, cols), jnp.float32)] * NACC,
        compiler_params=pltpu.CompilerParams(vmem_limit_bytes=30 * 2**20),
        name="observe",
    )(count, table, base, field, weight, held)


def per_device(
    control,
    lon_coef,
    lat_coef,
    obs_base,
    obs_field,
    obs_weight,
    obs_count,
    obs_value,
    obs_precision,
):
    fields, band_rows, block_cols = control.shape
    owners, slots = obs_base.shape[1:]
    by_device = (lax.axis_size("lon"), lax.axis_size("lat"), 1, slots)
    lines = control.reshape(fields * band_rows, block_cols)
    increment, coefs, held = root(
        lines,
        (lon_coef.T, lat_coef.T, obs_value.reshape(by_device), obs_precision.reshape(by_device)),
        band_rows,
        True,
    )
    increment, forcing = observe(
        increment,
        obs_count,
        obs_base[0],
        obs_field[0],
        obs_weight.reshape(obs_weight.shape[0], owners, 1, slots),
        held.reshape(owners, 2, slots),
    )
    (gradient,) = root(forcing, (coefs, lines), band_rows, False)
    return (increment.reshape(control.shape), gradient.reshape(control.shape))


def solution(mesh):
    in_specs = (
        P(None, "lat", "lon"),
        P(None, "lat"),
        P(None, "lat"),
        P(("lon", "lat"), None, None),
        P(("lon", "lat"), None, None),
        P(None, ("lon", "lat"), None, None),
        P(("lon", "lat"), None),
        P(("lon", "lat"), None, None),
        P(("lon", "lat"), None, None),
    )
    out_specs = (P(None, "lat", "lon"), P(None, "lat", "lon"))
    return jax.shard_map(
        per_device, mesh=mesh, in_specs=in_specs, out_specs=out_specs, check_vma=False
    )
```
